256 devices in a mesh: tm: 16 (over z_hi, x, core), sx: 4 (over z_lo), sy: 4 (over y).
Axes of the slice: x: 4, y: 4, z: 8 (z_hi: 2, z_lo: 4; z = z_hi * 4 + z_lo), core: 2. Of those that a mesh axis runs over, the one named last changes fastest.
Arguments:
- heat_source: float32 [64, 64, 64, 128], P('tm', 'sx', 'sy'), may hold values from -8 to 8
- conductivity: float32 [64, 64, 128], P('sx', 'sy'), may hold values from 0.001 to 0.5
- initial_iterate: float32 [64, 64, 64, 128], P('tm', 'sx', 'sy'), may hold values from -6 to 6
Outputs:
- solution: float32 [64, 64, 64, 128], P('tm', 'sx', 'sy')
- residual: float32 [64, 64, 64, 128], P('tm', 'sx', 'sy')
The draws below stay inside these ranges and needn't reach their ends.
All inputs are finite; a program needn't handle non-finite values.
Results may differ from the reference program's by a relative error of at most 0.000074.
Values sent between devices are 32-bit elements; how exact they have to be, the bound alone decides.
No kernel may reach another device: no remote copies, remote signals or barrier semaphores. Data moves between devices by JAX's collectives and lax.ppermute only.
A program may use at most 64 MiB of HBM per device.

```python
import jax
import jax.numpy as jnp
from jax import lax

STEPS = 4
NT = 64
NX = 64
NY = 64
NZ = 128


def draw_heat_source(key, part):
    rough = jax.random.normal(key, (NT, NX, NY, NZ), jnp.float32)
    return jnp.clip(rough, -8.0, 8.0)


def draw_conductivity(key, part):
    region_key = jax.random.fold_in(key, 13)
    high_key = jax.random.fold_in(key, 11)
    low_key = jax.random.fold_in(key, 12)
    regions_x = (NX + 2) // 4 + 1
    regions_y = (NY + 2) // 4 + 1
    flags = jax.random.randint(region_key, (regions_x, regions_y), 0, 2)
    index_x = ((jnp.arange(NX) + 2) // 4).astype(jnp.int32)
    index_y = ((jnp.arange(NY) + 2) // 4).astype(jnp.int32)
    low_cells = jnp.take(jnp.take(flags, index_x, axis=0), index_y, axis=1)
    high = jnp.exp(jax.random.uniform(high_key, (NX, NY, NZ), jnp.float32, jnp.log(0.02), jnp.log(0.5)))
    low = jnp.exp(jax.random.uniform(low_key, (NX, NY, NZ), jnp.float32, jnp.log(0.001), jnp.log(0.004)))
    return jnp.clip(jnp.where(low_cells[:, :, None] == 1, low, high), 0.001, 0.5)


def block_levels(key, dims, cuts, low, top_value):
    loudness, own = 1.0, jax.random.fold_in(key, 6)
    for axis_at, blocks in cuts:
        draws = jnp.exp(jax.random.uniform(jax.random.fold_in(own, axis_at), (blocks,), jnp.float32, low / len(cuts), top_value / len(cuts)))
        loudness = loudness * jnp.repeat(draws, dims[axis_at] // blocks).reshape([-1 if axis == axis_at else 1 for axis in range(len(dims))])
    return loudness


def gaussian(rng, extent, width, reach, cuts=(), dtype=jnp.bfloat16):
    values = jax.random.normal(rng, extent, jnp.float32) * width
    if len(cuts) > 0:
        values = block_levels(rng, extent, cuts, -0.22, 0.18) * values
    return jnp.clip(values, min=-reach, max=reach).astype(dtype)


def setup_inputs(seed: int = 0) -> dict:
    key_list = jax.random.split(jax.random.key(seed), 4)
    return {
        "heat_source": draw_heat_source(jax.random.fold_in(key_list[3], 71), 0),
        "conductivity": draw_conductivity(jax.random.fold_in(key_list[3], 71), 0),
        "initial_iterate": gaussian(key_list[2], (NT, NX, NY, NZ), 1.0, 6.0, ((0, 16), (1, 4), (2, 4)), jnp.float32),
    }


relax_weight = 0.8
fine_step = 1.0


def face_terms(conductivity):
    padded = jnp.pad(conductivity, 1)
    center = conductivity
    couple = (0.5 * (center + padded[2:, 1:-1, 1:-1]), 0.5 * (center + padded[:-2, 1:-1, 1:-1]),
              0.5 * (center + padded[1:-1, 2:, 1:-1]), 0.5 * (center + padded[1:-1, :-2, 1:-1]),
              0.5 * (center + padded[1:-1, 1:-1, 2:]), 0.5 * (center + padded[1:-1, 1:-1, :-2]))
    coupling = couple[0] + couple[1] + couple[2] + couple[3] + couple[4] + couple[5]
    return couple, coupling


def combine_neighbours(values, padded, couple, coupling, tau_step):
    beside = couple[0] * padded[:, 2:, 1:-1, 1:-1] + couple[1] * padded[:, :-2, 1:-1, 1:-1]
    beside = beside + couple[2] * padded[:, 1:-1, 2:, 1:-1] + couple[3] * padded[:, 1:-1, :-2, 1:-1]
    beside = beside + couple[4] * padded[:, 1:-1, 1:-1, 2:] + couple[5] * padded[:, 1:-1, 1:-1, :-2]
    return (1.0 + tau_step * coupling) * values - tau_step * beside


def apply_operator(values, couple, coupling, tau_step):
    padded = jnp.pad(values, ((0, 0), (1, 1), (1, 1), (1, 1)))
    return combine_neighbours(values, padded, couple, coupling, tau_step)


def smooth(values, source, couple, coupling, tau_step, block_len):
    diagonal = 1.0 + tau_step * coupling
    factor = relax_weight / diagonal
    applied = apply_operator(values, couple, coupling, tau_step)
    update = values + relax_weight * (source - applied) / diagonal
    earlier = jnp.concatenate([jnp.zeros_like(values[:1]), values[:-1]], axis=0)
    groups = values.shape[0] // block_len
    shaped = update.reshape((groups, block_len) + values.shape[1:])
    running = earlier.reshape((groups, block_len) + values.shape[1:])[:, 0]
    results = []
    for position in range(block_len):
        running = shaped[:, position] + factor * running
        results.append(running)
    return jnp.stack(results, axis=1).reshape(values.shape)


def defect(values, source, couple, coupling, tau_step):
    earlier = jnp.concatenate([jnp.zeros_like(values[:1]), values[:-1]], axis=0)
    return source + earlier - apply_operator(values, couple, coupling, tau_step)


def coarse_sweep(values, source, couple, coupling, tau_step):
    diagonal = 1.0 + tau_step * coupling
    factor = relax_weight / diagonal
    applied = apply_operator(values, couple, coupling, tau_step)
    update = values + relax_weight * (source - applied) / diagonal

    def advance(running, term):
        fresh_value = term + factor * running
        return fresh_value, fresh_value

    _, result = lax.scan(advance, jnp.zeros_like(values[0]), update)
    return result


def reference(heat_source, conductivity, initial_iterate):
    couple, coupling = face_terms(conductivity)
    first = smooth(initial_iterate, heat_source, couple, coupling, fine_step, STEPS)
    defect_fine = defect(first, heat_source, couple, coupling, fine_step)
    source_one = defect_fine[0::2] + defect_fine[1::2]
    error_one = smooth(jnp.zeros_like(source_one), source_one, couple, coupling, 2.0 * fine_step, STEPS // 2)
    defect_one = defect(error_one, source_one, couple, coupling, 2.0 * fine_step)
    source_two = defect_one[0::2] + defect_one[1::2]
    error_two = smooth(jnp.zeros_like(source_two), source_two, couple, coupling, 4.0 * fine_step, 1)
    defect_two = defect(error_two, source_two, couple, coupling, 4.0 * fine_step)
    source_three = defect_two[0::2] + defect_two[1::2]
    error_three = coarse_sweep(jnp.zeros_like(source_three), source_three, couple, coupling, 8.0 * fine_step)
    error_three = coarse_sweep(error_three, source_three, couple, coupling, 8.0 * fine_step)
    error_two = smooth(error_two + jnp.repeat(error_three, 2, axis=0), source_two, couple, coupling, 4.0 * fine_step, 1)
    error_one = smooth(error_one + jnp.repeat(error_two, 2, axis=0), source_one, couple, coupling, 2.0 * fine_step, STEPS // 2)
    solution = smooth(first + jnp.repeat(error_one, 2, axis=0), heat_source, couple, coupling, fine_step, STEPS)
    return solution, defect(solution, heat_source, couple, coupling, fine_step)
```

```python
import jax
import jax.numpy as jnp
from jax import lax
from jax.experimental import pallas as pl
from jax.experimental.pallas import tpu as pltpu
from jax.sharding import PartitionSpec as P

relax = 0.8
keep = 1.0 - relax
STEPS, BX, BY, BZ = 4, 16, 16, 128
COARSE = 8
EX, EY = BX + 4, 24
KX = BX + 6
f32 = jnp.float32
FIELD = (BX, BY, BZ)
EDGE = (BX, BZ)
YROWS = STEPS * BX + 3 * KX
YPACK = YROWS + (-YROWS) % 8


def turn(value, axis, by):
    devices = lax.axis_size(axis)
    return lax.ppermute(value, axis, [(i, (i + by) % devices) for i in range(devices)])


def across_tm(value, where):
    return lax.ppermute(value, "tm", [(i, where(i)) for i in range(16)])


def crossed(value, by_x, by_y):
    pairs = []
    for t in range(16):
        sign = 1 if t % 2 else -1
        for i in range(4):
            for j in range(4):
                to = ((t ^ 1) * 4 + (i + sign * by_x) % 4) * 4 + (j + sign * by_y) % 4
                pairs.append(((t * 4 + i) * 4 + j, to))
    return lax.ppermute(value, ("tm", "sx", "sy"), pairs)


def exchange(edges, last):
    x_low, x_high, y_low, y_high = edges
    earlier = turn(last, "tm", 1)
    return (
        turn(x_high, "sx", 1),
        turn(x_low, "sx", -1),
        turn(y_high, "sy", 1),
        turn(y_low, "sy", -1),
    ), earlier


def call(kernel, outs, *args, scratch=()):
    vmem = pl.BlockSpec(memory_space=pltpu.VMEM)
    return pl.pallas_call(
        kernel,
        out_shape=[jax.ShapeDtypeStruct(s, f32) for s in outs],
        in_specs=[vmem] * len(args),
        out_specs=[vmem] * len(outs),
        scratch_shapes=[pltpu.VMEM(s, f32) for s in scratch],
        compiler_params=pltpu.CompilerParams(vmem_limit_bytes=40 * 2**20),
    )(*args)


def inside(condition):
    return jnp.where(condition, f32(1.0), f32(0.0))


def row_index(rows=BY):
    return lax.broadcasted_iota(jnp.int32, (rows, BZ), 0)


def lane_index(rows=BY):
    return lax.broadcasted_iota(jnp.int32, (rows, BZ), 1)


def y_sides(value, low, high, row):
    below = jnp.where(row == 0, low, pltpu.roll(value, 1, 0))
    above = jnp.where(row == BY - 1, high, pltpu.roll(value, BY - 1, 0))
    return below, above


def beside(value, x_below, x_above, y_below, y_above, g):
    total = g[0] * x_below + g[1] * x_above
    total = total + g[2] * y_below + g[3] * y_above
    return total + g[4] * pltpu.roll(value, 1, 1) + g[5] * pltpu.roll(value, BZ - 1, 1)


def row_coefficients(g_ref, x):
    return [g_ref[i, x] for i in range(6)], g_ref[6, x]


def put_edges(refs, n, x, value):
    x_low, x_high, y_low, y_high = refs
    if x == 0:
        x_low[n] = value
    if x == BX - 1:
        x_high[n] = value
    y_low[n, pl.ds(x, 1), :] = value[0:1]
    y_high[n, pl.ds(x, 1), :] = value[BY - 1 : BY]


def edge_shapes(n):
    return [(n, *EDGE)] * 4


def first_edges_kernel(u, k, x_low, x_high, y_low, y_high, last):
    for n in range(STEPS):
        x_low[n] = u[n, 0]
        x_high[n] = u[n, BX - 1]
    for j in range(3):
        x_low[STEPS + j] = k[j]
        x_high[STEPS + j] = k[BX - 3 + j]
    for n in range(STEPS + 1):
        for x in range(BX):
            row = u[n, x] if n < STEPS else k[x]
            y_low[n, pl.ds(x, 1), :] = row[0:1]
            y_high[n, pl.ds(x, 1), :] = row[BY - 1 : BY]
    last[...] = u[STEPS - 1]


def first_kernel(u, h, k, hxl, hxh, hyl, hyh, prev, g_out, first, x_low, x_high, y_low, y_high, last, kx):
    sx, sy, tm = lax.axis_index("sx"), lax.axis_index("sy"), lax.axis_index("tm")
    has_xl, has_xh = inside(sx > 0), inside(sx < 3)
    has_yl, has_yh = inside(sy > 0), inside(sy < 3)
    has_prev = inside(tm > 0)
    row, lane = row_index(), lane_index()
    for j in range(3):
        kx[j] = hxl[STEPS + j] * has_xl
        kx[3 + BX + j] = hxh[STEPS + j] * has_xh
    for x in range(BX):
        kx[3 + x] = k[x]
    for x in range(BX):
        kc = k[x]
        k_yl = hyl[STEPS, pl.ds(x, 1), :] * has_yl
        k_yh = hyh[STEPS, pl.ds(x, 1), :] * has_yh
        k_below, k_above = y_sides(kc, k_yl, k_yh, row)
        z_below = jnp.where(lane == 0, 0.0, pltpu.roll(kc, 1, 1))
        z_above = jnp.where(lane == BZ - 1, 0.0, pltpu.roll(kc, BZ - 1, 1))
        g = [0.5 * (kc + other) for other in (kx[2 + x], kx[4 + x], k_below, k_above, z_below, z_above)]
        coupling = g[0] + g[1] + g[2] + g[3] + g[4] + g[5]
        if x == 0:
            g[0] = g[0] * has_xl
        if x == BX - 1:
            g[1] = g[1] * has_xh
        g[2] = jnp.where(row == 0, g[2] * has_yl, g[2])
        g[3] = jnp.where(row == BY - 1, g[3] * has_yh, g[3])
        g[4] = jnp.where(lane == 0, 0.0, g[4])
        g[5] = jnp.where(lane == BZ - 1, 0.0, g[5])
        for i in range(6):
            g_out[i, x] = g[i]
        g_out[6, x] = coupling
        factor = relax / (1.0 + coupling)
        running = prev[x] * has_prev
        for n in range(STEPS):
            value = u[n, x]
            below = u[n, x - 1] if x > 0 else hxl[n]
            above = u[n, x + 1] if x < BX - 1 else hxh[n]
            sides = y_sides(value, hyl[n, pl.ds(x, 1), :], hyh[n, pl.ds(x, 1), :], row)
            running = keep * value + factor * (h[n, x] + beside(value, below, above, *sides, g) + running)
            first[n, x] = running
            if x == 0:
                x_low[n] = running
            if x == BX - 1:
                x_high[n] = running
            y_low[pl.ds(n * BX + x, 1), :] = running[0:1]
            y_high[pl.ds(n * BX + x, 1), :] = running[BY - 1 : BY]
        last[x] = running
    for x in range(KX):
        kc = kx[x]
        for j in range(3):
            at = STEPS * BX + j * KX + x
            y_low[pl.ds(at, 1), :] = kc[j : j + 1]
            y_high[pl.ds(at, 1), :] = kc[BY - 3 + j : BY - 2 + j]
    if YPACK > YROWS:
        rest = jnp.zeros((YPACK - YROWS, BZ), f32)
        y_low[pl.ds(YROWS, YPACK - YROWS), :] = rest
        y_high[pl.ds(YROWS, YPACK - YROWS), :] = rest


def coarse_terms_kernel(kx, yl, yh, factor, g_out, ke):
    sx, sy = lax.axis_index("sx"), lax.axis_index("sy")
    has_yl, has_yh = inside(sy > 0), inside(sy < 3)
    row, lane = row_index(EY), lane_index(EY)
    for x in range(KX):
        ke[x, pl.ds(0, BY), :] = kx[x]
        ke[x, pl.ds(BY, 8), :] = jnp.zeros((8, BZ), f32)
        for j in range(3):
            at = STEPS * BX + j * KX + x
            ke[x, pl.ds(BY + j, 1), :] = yh[pl.ds(at, 1), :] * has_yh
            ke[x, pl.ds(EY - 3 + j, 1), :] = yl[pl.ds(at, 1), :] * has_yl
    y_in = jnp.where(row < BY, 1.0, jnp.where(row < BY + 4, has_yh, has_yl))
    for x in range(EX):
        kc = ke[x + 1]
        others = (
            ke[x],
            ke[x + 2],
            pltpu.roll(kc, 1, 0),
            pltpu.roll(kc, EY - 1, 0),
            jnp.where(lane == 0, 0.0, pltpu.roll(kc, 1, 1)),
            jnp.where(lane == BZ - 1, 0.0, pltpu.roll(kc, BZ - 1, 1)),
        )
        g = [0.5 * (kc + other) for other in others]
        coupling = g[0] + g[1] + g[2] + g[3] + g[4] + g[5]
        x_in = inside(sx > 0) if x < 2 else inside(sx < 3) if x >= BX + 2 else f32(1.0)
        factor[x] = (relax / (1.0 + 8.0 * coupling)) * (y_in * x_in)
        if 1 <= x <= EX - 2:
            g[4] = jnp.where(lane == 0, 0.0, g[4])
            g[5] = jnp.where(lane == BZ - 1, 0.0, g[5])
            for i in range(6):
                g_out[i, x - 1] = g[i]


def defect_fine_kernel(first, h, g_ref, hxl, hxh, yl, yh, prev, rhs, e0, e1, x_low, x_high, y_low, y_high):
    has_prev = inside(lax.axis_index("tm") > 0)
    row = row_index()
    for x in range(BX):
        g, coupling = row_coefficients(g_ref, x)
        diagonal = 1.0 + coupling
        factor = relax / (1.0 + 2.0 * coupling)
        earlier = prev[x] * has_prev
        parts = []
        for n in range(STEPS):
            value = first[n, x]
            below = first[n, x - 1] if x > 0 else hxl[n]
            above = first[n, x + 1] if x < BX - 1 else hxh[n]
            at = pl.ds(n * BX + x, 1)
            sides = y_sides(value, yl[at, :], yh[at, :], row)
            parts.append(h[n, x] + earlier - diagonal * value + beside(value, below, above, *sides, g))
            earlier = value
        r0, r1 = parts[0] + parts[1], parts[2] + parts[3]
        rhs[0, x] = r0
        rhs[1, x] = r1
        v0 = factor * r0
        v1 = factor * (r1 + v0)
        e0[x] = v0
        e1[x] = v1
        put_edges((x_low, x_high, y_low, y_high), 0, x, v0)
        put_edges((x_low, x_high, y_low, y_high), 1, x, v1)


def defect_mid_kernel(e0, e1, rhs, g_ref, hxl, hxh, hyl, hyh, prev, rhs2, err2, x_low, x_high, y_low, y_high):
    has_prev = inside(lax.axis_index("tm") > 0)
    row = row_index()
    for x in range(BX):
        g, coupling = row_coefficients(g_ref, x)
        diagonal = 1.0 + 2.0 * coupling
        earlier = prev[x] * has_prev
        total = None
        for n, e in enumerate((e0, e1)):
            value = e[x]
            below = e[x - 1] if x > 0 else hxl[n]
            above = e[x + 1] if x < BX - 1 else hxh[n]
            sides = y_sides(value, hyl[n, pl.ds(x, 1), :], hyh[n, pl.ds(x, 1), :], row)
            part = rhs[n, x] + earlier - diagonal * value + 2.0 * beside(value, below, above, *sides, g)
            total = part if total is None else total + part
            earlier = value
        rhs2[x] = total
        value = relax / (1.0 + 4.0 * coupling) * total
        err2[x] = value
        put_edges((x_low, x_high, y_low, y_high), 0, x, value)


def defect_last_kernel(err2, rhs2, g_ref, hxl, hxh, hyl, hyh, prev, out):
    has_prev = inside(lax.axis_index("tm") > 0)
    row = row_index()
    for x in range(BX):
        g, coupling = row_coefficients(g_ref, x)
        value = err2[x]
        below = err2[x - 1] if x > 0 else hxl[0]
        above = err2[x + 1] if x < BX - 1 else hxh[0]
        sides = y_sides(value, hyl[0, pl.ds(x, 1), :], hyh[0, pl.ds(x, 1), :], row)
        near = 4.0 * beside(value, below, above, *sides, g)
        out[x] = rhs2[x] + prev[x] * has_prev - (1.0 + 4.0 * coupling) * value + near


def order_kernel(*refs):
    parts, (rhs3, x_edge, y_edge, corner_a, corner_b) = refs[:8], refs[8:]
    tm = lax.axis_index("tm")
    core, ring, half = tm % 2, (tm // 2) % 4, tm // 8
    for far in range(2):
        for s in range(4):
            step = (half + far) % 2 * 4 + (ring + 4 - s) % 4
            for x in range(BX):
                rhs3[step, x] = parts[far * 4 + s][x]

    def send(x_from, y_from):
        for m in range(COARSE):
            for j in range(2):
                x_edge[m, j] = rhs3[m, x_from + j]
            for x in range(BX):
                y_edge[pl.ds((m * BX + x) * 2, 2), :] = rhs3[m, x, pl.ds(y_from, 2), :]
            x_end = x_from + (1 if x_from else 0)
            y_end = y_from + (1 if y_from else 0)
            corner_a[pl.ds(m, 1), :] = rhs3[m, x_end, pl.ds(y_end, 1), :]
            corner_b[pl.ds(m, 1), :] = rhs3[m, x_end, pl.ds(BY - 1 - y_end, 1), :]

    pl.when(core == 1)(lambda: send(BX - 2, BY - 2))
    pl.when(core == 0)(lambda: send(0, 0))


XH, YH = COARSE * 2 * BY, COARSE * BX * 2
HALO = XH + YH + 2 * COARSE


def coarse_kernel(rhs3, mine, other, factor, ge_ref, err2, rhs2, g_ref, hxl, hxh, hyl, hyh, prev,
                  fixed2, x_low, x_high, y_low, y_high, r, e, err3):
    tm = lax.axis_index("tm")
    core = tm % 2

    def fill(low, high):
        for m in range(COARSE):
            for j in range(2):
                r[m, j, pl.ds(0, BY), :] = low[pl.ds((m * 2 + j) * BY, BY), :]
                r[m, BX + 2 + j, pl.ds(0, BY), :] = high[pl.ds((m * 2 + j) * BY, BY), :]
            for x in range(EX):
                r[m, x, pl.ds(BY, 8), :] = jnp.zeros((8, BZ), f32)
            for x in range(BX):
                at = XH + (m * BX + x) * 2
                r[m, x + 2, pl.ds(0, BY), :] = rhs3[m, x]
                r[m, x + 2, pl.ds(BY, 2), :] = high[pl.ds(at, 2), :]
                r[m, x + 2, pl.ds(EY - 2, 2), :] = low[pl.ds(at, 2), :]
            a, b = XH + YH + m, XH + YH + COARSE + m
            r[m, 1, pl.ds(EY - 1, 1), :] = low[pl.ds(a, 1), :]
            r[m, 1, pl.ds(BY, 1), :] = low[pl.ds(b, 1), :]
            r[m, BX + 2, pl.ds(BY, 1), :] = high[pl.ds(a, 1), :]
            r[m, BX + 2, pl.ds(EY - 1, 1), :] = high[pl.ds(b, 1), :]

    pl.when(core == 0)(lambda: fill(mine, other))
    pl.when(core == 1)(lambda: fill(other, mine))

    def sweep_one(x, carry):
        w = factor[x]
        running = jnp.zeros((EY, BZ), f32)
        for m in range(COARSE):
            running = w * (r[m, x] + running)
            e[m, x] = running
        return carry

    lax.fori_loop(0, EX, sweep_one, 0)

    def sweep_two(x, carry):
        w = factor[x + 1]
        g = [ge_ref[i, x] for i in range(6)]
        running = jnp.zeros((EY, BZ), f32)
        err3[0, x] = running
        for m in range(COARSE):
            value = e[m, x + 1]
            near = beside(value, e[m, x], e[m, x + 2], pltpu.roll(value, 1, 0), pltpu.roll(value, EY - 1, 0), g)
            running = keep * value + w * (r[m, x + 1] + 8.0 * near + running)
            err3[m + 1, x] = running
        return carry

    lax.fori_loop(0, BX + 2, sweep_two, 0)

    has_prev = inside(tm > 0)
    row = row_index()
    now, before = tm // 2 + 1, (tm + 1) // 2
    for x in range(BX):
        g, coupling = row_coefficients(g_ref, x)
        own = err3[now, x + 1]
        value = err2[x] + own[0:BY]
        below = (err2[x - 1] if x > 0 else hxl[0]) + err3[now, x, pl.ds(0, BY), :]
        above = (err2[x + 1] if x < BX - 1 else hxh[0]) + err3[now, x + 2, pl.ds(0, BY), :]
        low = hyl[0, pl.ds(x, 1), :] + own[EY - 1 : EY]
        high = hyh[0, pl.ds(x, 1), :] + own[BY : BY + 1]
        sides = y_sides(value, low, high, row)
        earlier = prev[x] * has_prev + err3[before, x + 1, pl.ds(0, BY), :]
        near = 4.0 * beside(value, below, above, *sides, g)
        new = keep * value + relax / (1.0 + 4.0 * coupling) * (rhs2[x] + near + earlier)
        fixed2[x] = new
        put_edges((x_low, x_high, y_low, y_high), 0, x, new)


def fixed_mid_kernel(fix, fxl, fxh, fyl, fyh, fprev, e0, e1, exl, exh, eyl, eyh, eprev, rhs, g_ref,
                     out0, out1, x_low, x_high, y_low, y_high):
    has_prev = inside(lax.axis_index("tm") > 0)
    row = row_index()
    for x in range(BX):
        g, coupling = row_coefficients(g_ref, x)
        factor = relax / (1.0 + 2.0 * coupling)
        running = (eprev[x] + fprev[x]) * has_prev
        f_here = fix[x]
        f_below = fix[x - 1] if x > 0 else fxl[0]
        f_above = fix[x + 1] if x < BX - 1 else fxh[0]
        f_low, f_high = fyl[0, pl.ds(x, 1), :], fyh[0, pl.ds(x, 1), :]
        for n, (e, out) in enumerate(((e0, out0), (e1, out1))):
            value = e[x] + f_here
            below = (e[x - 1] if x > 0 else exl[n]) + f_below
            above = (e[x + 1] if x < BX - 1 else exh[n]) + f_above
            sides = y_sides(value, eyl[n, pl.ds(x, 1), :] + f_low, eyh[n, pl.ds(x, 1), :] + f_high, row)
            near = 2.0 * beside(value, below, above, *sides, g)
            running = keep * value + factor * (rhs[n, x] + near + running)
            out[x] = running
            put_edges((x_low, x_high, y_low, y_high), n, x, running)


def solution_kernel(fix0, fix1, fxl, fxh, fyl, fyh, fprev, first, exl, exh, yl, yh, eprev, h, g_ref,
                    out, x_low, x_high, y_low, y_high, last):
    has_prev = inside(lax.axis_index("tm") > 0)
    row = row_index()
    for x in range(BX):
        g, coupling = row_coefficients(g_ref, x)
        factor = relax / (1.0 + coupling)
        running = (eprev[x] + fprev[x]) * has_prev
        for n in range(STEPS):
            fix, c = (fix0, fix1)[n // 2], n // 2
            value = first[n, x] + fix[x]
            below = (first[n, x - 1] + fix[x - 1]) if x > 0 else (exl[n] + fxl[c])
            above = (first[n, x + 1] + fix[x + 1]) if x < BX - 1 else (exh[n] + fxh[c])
            at = pl.ds(n * BX + x, 1)
            low = yl[at, :] + fyl[c, pl.ds(x, 1), :]
            high = yh[at, :] + fyh[c, pl.ds(x, 1), :]
            sides = y_sides(value, low, high, row)
            running = keep * value + factor * (h[n, x] + beside(value, below, above, *sides, g) + running)
            out[n, x] = running
            put_edges((x_low, x_high, y_low, y_high), n, x, running)
        last[x] = running


def residual_kernel(sol, h, g_ref, hxl, hxh, hyl, hyh, prev, out):
    has_prev = inside(lax.axis_index("tm") > 0)
    row = row_index()
    for x in range(BX):
        g, coupling = row_coefficients(g_ref, x)
        diagonal = 1.0 + coupling
        earlier = prev[x] * has_prev
        for n in range(STEPS):
            value = sol[n, x]
            below = sol[n, x - 1] if x > 0 else hxl[n]
            above = sol[n, x + 1] if x < BX - 1 else hxh[n]
            sides = y_sides(value, hyl[n, pl.ds(x, 1), :], hyh[n, pl.ds(x, 1), :], row)
            out[n, x] = h[n, x] + earlier - diagonal * value + beside(value, below, above, *sides, g)
            earlier = value


def gather_steps(own):
    def along(value, s):
        return across_tm(value, lambda i: (i & 9) | ((i + 2 * s) & 6))

    far = across_tm(own, lambda i: i ^ 8)
    near = [own] + [along(own, s) for s in (1, 2, 3)]
    return near + [far] + [along(far, s) for s in (1, 2, 3)]


def per_device(h, k, u):
    fine, two = (STEPS, *FIELD), (2, *FIELD)
    ypack = (YPACK, BZ)
    *edges, last = call(first_edges_kernel, [(STEPS + 3, *EDGE)] * 2 + [(STEPS + 1, *EDGE)] * 2 + [FIELD], u, k)
    halo, prev = exchange(edges, last)
    g, first, *edges, last, kx = call(
        first_kernel,
        [(7, *FIELD), fine, (STEPS, *EDGE), (STEPS, *EDGE), ypack, ypack, FIELD, (KX, BY, BZ)],
        u, h, k, *halo, prev,
    )
    first_halo, first_prev = exchange(edges, last)
    factor, g_coarse = call(
        coarse_terms_kernel,
        [(EX, EY, BZ), (6, BX + 2, EY, BZ)],
        kx, *first_halo[2:],
        scratch=[(KX, EY, BZ)],
    )
    rhs1, e0, e1, *edges = call(
        defect_fine_kernel, [two, FIELD, FIELD] + edge_shapes(2), first, h, g, *first_halo, first_prev
    )
    err1_halo, err1_prev = exchange(edges, e1)
    rhs2, err2, *edges = call(
        defect_mid_kernel, [FIELD, FIELD] + edge_shapes(1), e0, e1, rhs1, g, *err1_halo, err1_prev
    )
    err2_halo, err2_prev = exchange(edges, err2)
    (defect2,) = call(defect_last_kernel, [FIELD], err2, rhs2, g, *err2_halo, err2_prev)
    rhs3 = defect2 + across_tm(defect2, lambda i: i ^ 1)
    steps, x_edge, y_edge, corner_a, corner_b = call(
        order_kernel,
        [(COARSE, *FIELD), (COARSE, 2, BY, BZ), (YH, BZ), (COARSE, BZ), (COARSE, BZ)],
        *gather_steps(rhs3),
    )
    mine = jnp.concatenate(
        [
            crossed(x_edge, 1, 0).reshape(XH, BZ),
            crossed(y_edge, 0, 1),
            crossed(corner_a, 1, 1),
            crossed(corner_b, 1, -1),
        ]
    )
    other = across_tm(mine, lambda i: i ^ 1)
    fixed2, *edges = call(
        coarse_kernel,
        [FIELD] + edge_shapes(1),
        steps, mine, other, factor, g_coarse, err2, rhs2, g, *err2_halo, err2_prev,
        scratch=[(COARSE, EX, EY, BZ), (COARSE, EX, EY, BZ), (COARSE + 1, BX + 2, EY, BZ)],
    )
    fixed2_halo, fixed2_prev = exchange(edges, fixed2)
    fixed1a, fixed1b, *edges = call(
        fixed_mid_kernel,
        [FIELD, FIELD] + edge_shapes(2),
        fixed2, *fixed2_halo, fixed2_prev, e0, e1, *err1_halo, err1_prev, rhs1, g,
    )
    fixed1_halo, fixed1_prev = exchange(edges, fixed1b)
    out, *edges, last = call(
        solution_kernel,
        [fine] + edge_shapes(STEPS) + [FIELD],
        fixed1a, fixed1b, *fixed1_halo, fixed1_prev, first, *first_halo, first_prev, h, g,
    )
    out_halo, out_prev = exchange(edges, last)
    (residual,) = call(residual_kernel, [fine], out, h, g, *out_halo, out_prev)
    return out, residual


def solution(mesh):
    placed = (P("tm", "sx", "sy", None), P("sx", "sy", None), P("tm", "sx", "sy", None))
    return jax.shard_map(
        per_device,
        mesh=mesh,
        in_specs=placed,
        out_specs=(P("tm", "sx", "sy", None), P("tm", "sx", "sy", None)),
        check_vma=False,
    )
```

```python
import jax
import jax.numpy as jnp
from jax import lax
from jax.experimental import pallas as pl
from jax.experimental.pallas import tpu as pltpu
from jax.sharding import PartitionSpec as P

relax = 0.8
keep = 1.0 - relax
STEPS, BX, BY, BZ = 4, 16, 16, 128
COARSE = 8
EX, EY = BX + 4, 24
KX = BX + 6
f32 = jnp.float32
FIELD = (BX, BY, BZ)
EDGE = (BX, BZ)
YROWS = STEPS * BX + 3 * KX
YPACK = YROWS + (-YROWS) % 8


def turn(value, axis, by):
    devices = lax.axis_size(axis)
    return lax.ppermute(value, axis, [(i, (i + by) % devices) for i in range(devices)])


def across_tm(value, where):
    return lax.ppermute(value, "tm", [(i, where(i)) for i in range(16)])


def crossed(value, by_x, by_y):
    pairs = []
    for t in range(16):
        sign = 1 if t % 2 else -1
        for i in range(4):
            for j in range(4):
                to = ((t ^ 1) * 4 + (i + sign * by_x) % 4) * 4 + (j + sign * by_y) % 4
                pairs.append(((t * 4 + i) * 4 + j, to))
    return lax.ppermute(value, ("tm", "sx", "sy"), pairs)


def exchange(edges, last):
    x_low, x_high, y_low, y_high = edges
    earlier = turn(last, "tm", 1)
    return (
        turn(x_high, "sx", 1),
        turn(x_low, "sx", -1),
        turn(y_high, "sy", 1),
        turn(y_low, "sy", -1),
    ), earlier


def call(kernel, outs, *args, scratch=()):
    vmem = pl.BlockSpec(memory_space=pltpu.VMEM)
    return pl.pallas_call(
        kernel,
        out_shape=[jax.ShapeDtypeStruct(s, f32) for s in outs],
        in_specs=[vmem] * len(args),
        out_specs=[vmem] * len(outs),
        scratch_shapes=[pltpu.VMEM(s, f32) for s in scratch],
        compiler_params=pltpu.CompilerParams(vmem_limit_bytes=40 * 2**20),
    )(*args)


def inside(condition):
    return jnp.where(condition, f32(1.0), f32(0.0))


def row_index(rows=BY):
    return lax.broadcasted_iota(jnp.int32, (rows, BZ), 0)


def lane_index(rows=BY):
    return lax.broadcasted_iota(jnp.int32, (rows, BZ), 1)


def y_sides(value, low, high, row):
    below = jnp.where(row == 0, low, pltpu.roll(value, 1, 0))
    above = jnp.where(row == BY - 1, high, pltpu.roll(value, BY - 1, 0))
    return below, above


def beside(value, x_below, x_above, y_below, y_above, g):
    total = g[0] * x_below + g[1] * x_above
    total = total + g[2] * y_below + g[3] * y_above
    return total + g[4] * pltpu.roll(value, 1, 1) + g[5] * pltpu.roll(value, BZ - 1, 1)


def row_coefficients(g_ref, x):
    return [g_ref[i, x] for i in range(6)], g_ref[6, x]


def put_edges(refs, n, x, value):
    x_low, x_high, y_low, y_high = refs
    if x == 0:
        x_low[n] = value
    if x == BX - 1:
        x_high[n] = value
    y_low[n, pl.ds(x, 1), :] = value[0:1]
    y_high[n, pl.ds(x, 1), :] = value[BY - 1 : BY]


def edge_shapes(n):
    return [(n, *EDGE)] * 4


def first_edges_kernel(u, k, x_low, x_high, y_low, y_high, last):
    for n in range(STEPS):
        x_low[n] = u[n, 0]
        x_high[n] = u[n, BX - 1]
    for j in range(3):
        x_low[STEPS + j] = k[j]
        x_high[STEPS + j] = k[BX - 3 + j]
    for n in range(STEPS + 1):
        for x in range(BX):
            row = u[n, x] if n < STEPS else k[x]
            y_low[n, pl.ds(x, 1), :] = row[0:1]
            y_high[n, pl.ds(x, 1), :] = row[BY - 1 : BY]
    last[...] = u[STEPS - 1]


def first_kernel(u, h, k, hxl, hxh, hyl, hyh, prev, g_out, first, x_low, x_high, y_low, y_high, last, kx):
    sx, sy, tm = lax.axis_index("sx"), lax.axis_index("sy"), lax.axis_index("tm")
    has_xl, has_xh = inside(sx > 0), inside(sx < 3)
    has_yl, has_yh = inside(sy > 0), inside(sy < 3)
    has_prev = inside(tm > 0)
    row, lane = row_index(), lane_index()
    for j in range(3):
        kx[j] = hxl[STEPS + j] * has_xl
        kx[3 + BX + j] = hxh[STEPS + j] * has_xh
    for x in range(BX):
        kx[3 + x] = k[x]
    for x in range(BX):
        kc = k[x]
        k_yl = hyl[STEPS, pl.ds(x, 1), :] * has_yl
        k_yh = hyh[STEPS, pl.ds(x, 1), :] * has_yh
        k_below, k_above = y_sides(kc, k_yl, k_yh, row)
        z_below = jnp.where(lane == 0, 0.0, pltpu.roll(kc, 1, 1))
        z_above = jnp.where(lane == BZ - 1, 0.0, pltpu.roll(kc, BZ - 1, 1))
        g = [0.5 * (kc + other) for other in (kx[2 + x], kx[4 + x], k_below, k_above, z_below, z_above)]
        coupling = g[0] + g[1] + g[2] + g[3] + g[4] + g[5]
        if x == 0:
            g[0] = g[0] * has_xl
        if x == BX - 1:
            g[1] = g[1] * has_xh
        g[2] = jnp.where(row == 0, g[2] * has_yl, g[2])
        g[3] = jnp.where(row == BY - 1, g[3] * has_yh, g[3])
        g[4] = jnp.where(lane == 0, 0.0, g[4])
        g[5] = jnp.where(lane == BZ - 1, 0.0, g[5])
        for i in range(6):
            g_out[i, x] = g[i]
        g_out[6, x] = coupling
        factor = relax / (1.0 + coupling)
        running = prev[x] * has_prev
        for n in range(STEPS):
            value = u[n, x]
            below = u[n, x - 1] if x > 0 else hxl[n]
            above = u[n, x + 1] if x < BX - 1 else hxh[n]
            sides = y_sides(value, hyl[n, pl.ds(x, 1), :], hyh[n, pl.ds(x, 1), :], row)
            running = keep * value + factor * (h[n, x] + beside(value, below, above, *sides, g) + running)
            first[n, x] = running
            if x == 0:
                x_low[n] = running
            if x == BX - 1:
                x_high[n] = running
            y_low[pl.ds(n * BX + x, 1), :] = running[0:1]
            y_high[pl.ds(n * BX + x, 1), :] = running[BY - 1 : BY]
        last[x] = running
    for x in range(KX):
        kc = kx[x]
        for j in range(3):
            at = STEPS * BX + j * KX + x
            y_low[pl.ds(at, 1), :] = kc[j : j + 1]
            y_high[pl.ds(at, 1), :] = kc[BY - 3 + j : BY - 2 + j]
    if YPACK > YROWS:
        rest = jnp.zeros((YPACK - YROWS, BZ), f32)
        y_low[pl.ds(YROWS, YPACK - YROWS), :] = rest
        y_high[pl.ds(YROWS, YPACK - YROWS), :] = rest


def coarse_terms_kernel(kx, yl, yh, factor, g_out, ke):
    sx, sy = lax.axis_index("sx"), lax.axis_index("sy")
    has_yl, has_yh = inside(sy > 0), inside(sy < 3)
    row, lane = row_index(EY), lane_index(EY)
    for x in range(KX):
        ke[x, pl.ds(0, BY), :] = kx[x]
        ke[x, pl.ds(BY, 8), :] = jnp.zeros((8, BZ), f32)
        for j in range(3):
            at = STEPS * BX + j * KX + x
            ke[x, pl.ds(BY + j, 1), :] = yh[pl.ds(at, 1), :] * has_yh
            ke[x, pl.ds(EY - 3 + j, 1), :] = yl[pl.ds(at, 1), :] * has_yl
    y_in = jnp.where(row < BY, 1.0, jnp.where(row < BY + 4, has_yh, has_yl))
    for x in range(EX):
        kc = ke[x + 1]
        others = (
            ke[x],
            ke[x + 2],
            pltpu.roll(kc, 1, 0),
            pltpu.roll(kc, EY - 1, 0),
            jnp.where(lane == 0, 0.0, pltpu.roll(kc, 1, 1)),
            jnp.where(lane == BZ - 1, 0.0, pltpu.roll(kc, BZ - 1, 1)),
        )
        g = [0.5 * (kc + other) for other in others]
        coupling = g[0] + g[1] + g[2] + g[3] + g[4] + g[5]
        x_in = inside(sx > 0) if x < 2 else inside(sx < 3) if x >= BX + 2 else f32(1.0)
        factor[x] = (relax / (1.0 + 8.0 * coupling)) * (y_in * x_in)
        if 1 <= x <= EX - 2:
            g[4] = jnp.where(lane == 0, 0.0, g[4])
            g[5] = jnp.where(lane == BZ - 1, 0.0, g[5])
            for i in range(6):
                g_out[i, x - 1] = g[i]


def defect_fine_kernel(first, h, g_ref, hxl, hxh, yl, yh, prev, rhs, e0, e1, x_low, x_high, y_low, y_high):
    has_prev = inside(lax.axis_index("tm") > 0)
    row = row_index()
    for x in range(BX):
        g, coupling = row_coefficients(g_ref, x)
        diagonal = 1.0 + coupling
        factor = relax / (1.0 + 2.0 * coupling)
        earlier = prev[x] * has_prev
        parts = []
        for n in range(STEPS):
            value = first[n, x]
            below = first[n, x - 1] if x > 0 else hxl[n]
            above = first[n, x + 1] if x < BX - 1 else hxh[n]
            at = pl.ds(n * BX + x, 1)
            sides = y_sides(value, yl[at, :], yh[at, :], row)
            parts.append(h[n, x] + earlier - diagonal * value + beside(value, below, above, *sides, g))
            earlier = value
        r0, r1 = parts[0] + parts[1], parts[2] + parts[3]
        rhs[0, x] = r0
        rhs[1, x] = r1
        v0 = factor * r0
        v1 = factor * (r1 + v0)
        e0[x] = v0
        e1[x] = v1
        put_edges((x_low, x_high, y_low, y_high), 0, x, v0)
        put_edges((x_low, x_high, y_low, y_high), 1, x, v1)


def defect_mid_kernel(e0, e1, rhs, g_ref, hxl, hxh, hyl, hyh, prev, rhs2, err2, x_low, x_high, y_low, y_high):
    has_prev = inside(lax.axis_index("tm") > 0)
    row = row_index()
    for x in range(BX):
        g, coupling = row_coefficients(g_ref, x)
        diagonal = 1.0 + 2.0 * coupling
        earlier = prev[x] * has_prev
        total = None
        for n, e in enumerate((e0, e1)):
            value = e[x]
            below = e[x - 1] if x > 0 else hxl[n]
            above = e[x + 1] if x < BX - 1 else hxh[n]
            sides = y_sides(value, hyl[n, pl.ds(x, 1), :], hyh[n, pl.ds(x, 1), :], row)
            part = rhs[n, x] + earlier - diagonal * value + 2.0 * beside(value, below, above, *sides, g)
            total = part if total is None else total + part
            earlier = value
        rhs2[x] = total
        value = relax / (1.0 + 4.0 * coupling) * total
        err2[x] = value
        put_edges((x_low, x_high, y_low, y_high), 0, x, value)


def defect_last_kernel(err2, rhs2, g_ref, hxl, hxh, hyl, hyh, prev, out):
    has_prev = inside(lax.axis_index("tm") > 0)
    row = row_index()
    for x in range(BX):
        g, coupling = row_coefficients(g_ref, x)
        value = err2[x]
        below = err2[x - 1] if x > 0 else hxl[0]
        above = err2[x + 1] if x < BX - 1 else hxh[0]
        sides = y_sides(value, hyl[0, pl.ds(x, 1), :], hyh[0, pl.ds(x, 1), :], row)
        near = 4.0 * beside(value, below, above, *sides, g)
        out[x] = rhs2[x] + prev[x] * has_prev - (1.0 + 4.0 * coupling) * value + near


HALF = BX // 2 * BY
XH, YH, CH = HALF, HALF + 2 * BY, HALF + 2 * BY + 2 * BX
SHARE = CH + 8


def coarse_edges_kernel(own, other, half, x_edge, y_edge, corner_a, corner_b, rhs3):
    core = lax.axis_index("tm") % 2
    for x in range(BX):
        rhs3[x] = own[x] + other[x]

    def send(c):
        x_from, y_from = c * (BX - 2), c * (BY - 2)
        for i in range(BX // 2):
            half[pl.ds(i * BY, BY), :] = rhs3[c * (BX // 2) + i]
        for j in range(2):
            x_edge[pl.ds(j * BY, BY), :] = rhs3[x_from + j]
        for x in range(BX):
            y_edge[pl.ds(x * 2, 2), :] = rhs3[x, pl.ds(y_from, 2), :]
        x_end, y_end = c * (BX - 1), c * (BY - 1)
        corner_a[...] = jnp.zeros((8, BZ), f32)
        corner_b[...] = jnp.zeros((8, BZ), f32)
        corner_a[pl.ds(0, 1), :] = rhs3[x_end, pl.ds(y_end, 1), :]
        corner_b[pl.ds(0, 1), :] = rhs3[x_end, pl.ds(BY - 1 - y_end, 1), :]

    pl.when(core == 1)(lambda: send(1))
    pl.when(core == 0)(lambda: send(0))


def share_kernel(half, x_edge, y_edge, corner_a, corner_b, share):
    share[pl.ds(0, HALF), :] = half[...]
    share[pl.ds(XH, 2 * BY), :] = x_edge[...]
    share[pl.ds(YH, 2 * BX), :] = y_edge[...]
    share[pl.ds(CH, 8), :] = corner_a[...]
    share[pl.ds(CH + 1, 1), :] = corner_b[pl.ds(0, 1), :]


def order_kernel(*refs):
    parts, out = refs[:8], refs[8]
    tm = lax.axis_index("tm")
    ring, half = (tm // 2) % 4, tm // 8
    for far in range(2):
        for s in range(4):
            out[(half + far) % 2 * 4 + (ring + 4 - s) % 4] = parts[far * 4 + s][...]


def coarse_kernel(mine, other, factor, ge_ref, err2, rhs2, g_ref, hxl, hxh, hyl, hyh, prev,
                  fixed2, x_low, x_high, y_low, y_high, r, e, err3):
    tm = lax.axis_index("tm")
    core = tm % 2

    def fill(low, high):
        for m in range(COARSE):
            for x in range(EX):
                r[m, x, pl.ds(BY, 8), :] = jnp.zeros((8, BZ), f32)
            for j in range(2):
                r[m, j, pl.ds(0, BY), :] = low[m, pl.ds(XH + j * BY, BY), :]
                r[m, BX + 2 + j, pl.ds(0, BY), :] = high[m, pl.ds(XH + j * BY, BY), :]
            for x in range(BX):
                source = (low, high)[x // (BX // 2)]
                r[m, x + 2, pl.ds(0, BY), :] = source[m, pl.ds(x % (BX // 2) * BY, BY), :]
                r[m, x + 2, pl.ds(BY, 2), :] = high[m, pl.ds(YH + x * 2, 2), :]
                r[m, x + 2, pl.ds(EY - 2, 2), :] = low[m, pl.ds(YH + x * 2, 2), :]
            r[m, 1, pl.ds(EY - 1, 1), :] = low[m, pl.ds(CH, 1), :]
            r[m, 1, pl.ds(BY, 1), :] = low[m, pl.ds(CH + 1, 1), :]
            r[m, BX + 2, pl.ds(BY, 1), :] = high[m, pl.ds(CH, 1), :]
            r[m, BX + 2, pl.ds(EY - 1, 1), :] = high[m, pl.ds(CH + 1, 1), :]

    pl.when(core == 0)(lambda: fill(mine, other))
    pl.when(core == 1)(lambda: fill(other, mine))

    def sweep_one(x, carry):
        w = factor[x]
        running = jnp.zeros((EY, BZ), f32)
        for m in range(COARSE):
            running = w * (r[m, x] + running)
            e[m, x] = running
        return carry

    lax.fori_loop(0, EX, sweep_one, 0)

    def sweep_two(x, carry):
        w = factor[x + 1]
        g = [ge_ref[i, x] for i in range(6)]
        running = jnp.zeros((EY, BZ), f32)
        err3[0, x] = running
        for m in range(COARSE):
            value = e[m, x + 1]
            near = beside(value, e[m, x], e[m, x + 2], pltpu.roll(value, 1, 0), pltpu.roll(value, EY - 1, 0), g)
            running = keep * value + w * (r[m, x + 1] + 8.0 * near + running)
            err3[m + 1, x] = running
        return carry

    lax.fori_loop(0, BX + 2, sweep_two, 0)

    has_prev = inside(tm > 0)
    row = row_index()
    now, before = tm // 2 + 1, (tm + 1) // 2
    for x in range(BX):
        g, coupling = row_coefficients(g_ref, x)
        own = err3[now, x + 1]
        value = err2[x] + own[0:BY]
        below = (err2[x - 1] if x > 0 else hxl[0]) + err3[now, x, pl.ds(0, BY), :]
        above = (err2[x + 1] if x < BX - 1 else hxh[0]) + err3[now, x + 2, pl.ds(0, BY), :]
        low = hyl[0, pl.ds(x, 1), :] + own[EY - 1 : EY]
        high = hyh[0, pl.ds(x, 1), :] + own[BY : BY + 1]
        sides = y_sides(value, low, high, row)
        earlier = prev[x] * has_prev + err3[before, x + 1, pl.ds(0, BY), :]
        near = 4.0 * beside(value, below, above, *sides, g)
        new = keep * value + relax / (1.0 + 4.0 * coupling) * (rhs2[x] + near + earlier)
        fixed2[x] = new
        put_edges((x_low, x_high, y_low, y_high), 0, x, new)


def fixed_mid_kernel(fix, fxl, fxh, fyl, fyh, fprev, e0, e1, exl, exh, eyl, eyh, eprev, rhs, g_ref,
                     out0, out1, x_low, x_high, y_low, y_high):
    has_prev = inside(lax.axis_index("tm") > 0)
    row = row_index()
    for x in range(BX):
        g, coupling = row_coefficients(g_ref, x)
        factor = relax / (1.0 + 2.0 * coupling)
        running = (eprev[x] + fprev[x]) * has_prev
        f_here = fix[x]
        f_below = fix[x - 1] if x > 0 else fxl[0]
        f_above = fix[x + 1] if x < BX - 1 else fxh[0]
        f_low, f_high = fyl[0, pl.ds(x, 1), :], fyh[0, pl.ds(x, 1), :]
        for n, (e, out) in enumerate(((e0, out0), (e1, out1))):
            value = e[x] + f_here
            below = (e[x - 1] if x > 0 else exl[n]) + f_below
            above = (e[x + 1] if x < BX - 1 else exh[n]) + f_above
            sides = y_sides(value, eyl[n, pl.ds(x, 1), :] + f_low, eyh[n, pl.ds(x, 1), :] + f_high, row)
            near = 2.0 * beside(value, below, above, *sides, g)
            running = keep * value + factor * (rhs[n, x] + near + running)
            out[x] = running
            put_edges((x_low, x_high, y_low, y_high), n, x, running)


def solution_kernel(fix0, fix1, fxl, fxh, fyl, fyh, fprev, first, exl, exh, yl, yh, eprev, h, g_ref,
                    out, x_low, x_high, y_low, y_high, last):
    has_prev = inside(lax.axis_index("tm") > 0)
    row = row_index()
    for x in range(BX):
        g, coupling = row_coefficients(g_ref, x)
        factor = relax / (1.0 + coupling)
        running = (eprev[x] + fprev[x]) * has_prev
        for n in range(STEPS):
            fix, c = (fix0, fix1)[n // 2], n // 2
            value = first[n, x] + fix[x]
            below = (first[n, x - 1] + fix[x - 1]) if x > 0 else (exl[n] + fxl[c])
            above = (first[n, x + 1] + fix[x + 1]) if x < BX - 1 else (exh[n] + fxh[c])
            at = pl.ds(n * BX + x, 1)
            low = yl[at, :] + fyl[c, pl.ds(x, 1), :]
            high = yh[at, :] + fyh[c, pl.ds(x, 1), :]
            sides = y_sides(value, low, high, row)
            running = keep * value + factor * (h[n, x] + beside(value, below, above, *sides, g) + running)
            out[n, x] = running
            put_edges((x_low, x_high, y_low, y_high), n, x, running)
        last[x] = running


def copy_kernel(source, target):
    target[...] = source[...]


def residual_kernel(sol, h, g_ref, hxl, hxh, hyl, hyh, prev, out):
    has_prev = inside(lax.axis_index("tm") > 0)
    row = row_index()
    for x in range(BX):
        g, coupling = row_coefficients(g_ref, x)
        diagonal = 1.0 + coupling
        earlier = prev[x] * has_prev
        for n in range(STEPS):
            value = sol[n, x]
            below = sol[n, x - 1] if x > 0 else hxl[n]
            above = sol[n, x + 1] if x < BX - 1 else hxh[n]
            sides = y_sides(value, hyl[n, pl.ds(x, 1), :], hyh[n, pl.ds(x, 1), :], row)
            out[n, x] = h[n, x] + earlier - diagonal * value + beside(value, below, above, *sides, g)
            earlier = value


def gather_steps(own):
    def along(value, s):
        return across_tm(value, lambda i: (i & 9) | ((i + 2 * s) & 6))

    far = across_tm(own, lambda i: i ^ 8)
    near = [own] + [along(own, s) for s in (1, 2, 3)]
    return near + [far] + [along(far, s) for s in (1, 2, 3)]


def per_device(h, k, u):
    fine, two = (STEPS, *FIELD), (2, *FIELD)
    ypack = (YPACK, BZ)
    *edges, last = call(first_edges_kernel, [(STEPS + 3, *EDGE)] * 2 + [(STEPS + 1, *EDGE)] * 2 + [FIELD], u, k)
    (h,) = call(copy_kernel, [fine], h)
    halo, prev = exchange(edges, last)
    g, first, *edges, last, kx = call(
        first_kernel,
        [(7, *FIELD), fine, (STEPS, *EDGE), (STEPS, *EDGE), ypack, ypack, FIELD, (KX, BY, BZ)],
        u, h, k, *halo, prev,
    )
    first_halo, first_prev = exchange(edges, last)
    factor, g_coarse = call(
        coarse_terms_kernel,
        [(EX, EY, BZ), (6, BX + 2, EY, BZ)],
        kx, *first_halo[2:],
        scratch=[(KX, EY, BZ)],
    )
    rhs1, e0, e1, *edges = call(
        defect_fine_kernel, [two, FIELD, FIELD] + edge_shapes(2), first, h, g, *first_halo, first_prev
    )
    err1_halo, err1_prev = exchange(edges, e1)
    rhs2, err2, *edges = call(
        defect_mid_kernel, [FIELD, FIELD] + edge_shapes(1), e0, e1, rhs1, g, *err1_halo, err1_prev
    )
    err2_halo, err2_prev = exchange(edges, err2)
    (defect2,) = call(defect_last_kernel, [FIELD], err2, rhs2, g, *err2_halo, err2_prev)
    sibling = across_tm(defect2, lambda i: i ^ 1)
    corner = (8, BZ)
    half, x_edge, y_edge, corner_a, corner_b = call(
        coarse_edges_kernel,
        [(HALF, BZ), (2 * BY, BZ), (2 * BX, BZ), corner, corner],
        defect2, sibling,
        scratch=[FIELD],
    )
    (share,) = call(
        share_kernel,
        [(SHARE, BZ)],
        half, crossed(x_edge, 1, 0), crossed(y_edge, 0, 1), crossed(corner_a, 1, 1), crossed(corner_b, 1, -1),
    )
    (mine,) = call(order_kernel, [(COARSE, SHARE, BZ)], *gather_steps(share))
    other = across_tm(mine, lambda i: i ^ 1)
    fixed2, *edges = call(
        coarse_kernel,
        [FIELD] + edge_shapes(1),
        mine, other, factor, g_coarse, err2, rhs2, g, *err2_halo, err2_prev,
        scratch=[(COARSE, EX, EY, BZ), (COARSE, EX, EY, BZ), (COARSE + 1, BX + 2, EY, BZ)],
    )
    fixed2_halo, fixed2_prev = exchange(edges, fixed2)
    fixed1a, fixed1b, *edges = call(
        fixed_mid_kernel,
        [FIELD, FIELD] + edge_shapes(2),
        fixed2, *fixed2_halo, fixed2_prev, e0, e1, *err1_halo, err1_prev, rhs1, g,
    )
    fixed1_halo, fixed1_prev = exchange(edges, fixed1b)
    last_iterate, *edges, last = call(
        solution_kernel,
        [fine] + edge_shapes(STEPS) + [FIELD],
        fixed1a, fixed1b, *fixed1_halo, fixed1_prev, first, *first_halo, first_prev, h, g,
    )
    out_halo, out_prev = exchange(edges, last)
    (out,) = call(copy_kernel, [fine], last_iterate)
    (residual,) = call(residual_kernel, [fine], last_iterate, h, g, *out_halo, out_prev)
    return out, residual


def solution(mesh):
    placed = (P("tm", "sx", "sy", None), P("sx", "sy", None), P("tm", "sx", "sy", None))
    return jax.shard_map(
        per_device,
        mesh=mesh,
        in_specs=placed,
        out_specs=(P("tm", "sx", "sy", None), P("tm", "sx", "sy", None)),
        check_vma=False,
    )
```

```python
import jax
import jax.numpy as jnp
from jax import lax
from jax.experimental import pallas as pl
from jax.experimental.pallas import tpu as pltpu
from jax.sharding import PartitionSpec as P

relax = 0.8
keep = 1.0 - relax
STEPS, BX, BY, BZ = 4, 16, 16, 128
COARSE = 8
WIDE = 3
KW = WIDE + 1
EX, EY = BX + 2 * WIDE, BY + 2 * KW
KX = BX + 2 * KW
f32 = jnp.float32
FIELD = (BX, BY, BZ)
EDGE = (BX, BZ)
YROWS = STEPS * BX + KW * KX


def turn(value, axis, by):
    devices = lax.axis_size(axis)
    return lax.ppermute(value, axis, [(i, (i + by) % devices) for i in range(devices)])


def across_tm(value, where):
    return lax.ppermute(value, "tm", [(i, where(i)) for i in range(16)])


def crossed(value, by_x, by_y):
    pairs = []
    for t in range(16):
        sign = 1 if t % 2 else -1
        for i in range(4):
            for j in range(4):
                to = ((t ^ 1) * 4 + (i + sign * by_x) % 4) * 4 + (j + sign * by_y) % 4
                pairs.append(((t * 4 + i) * 4 + j, to))
    return lax.ppermute(value, ("tm", "sx", "sy"), pairs)


def exchange(edges, last):
    x_low, x_high, y_low, y_high = edges
    earlier = turn(last, "tm", 1)
    return (
        turn(x_high, "sx", 1),
        turn(x_low, "sx", -1),
        turn(y_high, "sy", 1),
        turn(y_low, "sy", -1),
    ), earlier


def call(kernel, outs, *args, scratch=()):
    vmem = pl.BlockSpec(memory_space=pltpu.VMEM)
    return pl.pallas_call(
        kernel,
        out_shape=[jax.ShapeDtypeStruct(s, f32) for s in outs],
        in_specs=[vmem] * len(args),
        out_specs=[vmem] * len(outs),
        scratch_shapes=[pltpu.VMEM(s, f32) for s in scratch],
        compiler_params=pltpu.CompilerParams(vmem_limit_bytes=40 * 2**20),
    )(*args)


def inside(condition):
    return jnp.where(condition, f32(1.0), f32(0.0))


def row_index(rows=BY):
    return lax.broadcasted_iota(jnp.int32, (rows, BZ), 0)


def lane_index(rows=BY):
    return lax.broadcasted_iota(jnp.int32, (rows, BZ), 1)


def y_sides(value, low, high, row):
    below = jnp.where(row == 0, low, pltpu.roll(value, 1, 0))
    above = jnp.where(row == BY - 1, high, pltpu.roll(value, BY - 1, 0))
    return below, above


def beside(value, x_below, x_above, y_below, y_above, g):
    total = g[0] * x_below + g[1] * x_above
    total = total + g[2] * y_below + g[3] * y_above
    return total + g[4] * pltpu.roll(value, 1, 1) + g[5] * pltpu.roll(value, BZ - 1, 1)


def row_coefficients(g_ref, x):
    return [g_ref[i, x] for i in range(6)], g_ref[6, x]


def put_edges(refs, n, x, value):
    x_low, x_high, y_low, y_high = refs
    if x == 0:
        x_low[n] = value
    if x == BX - 1:
        x_high[n] = value
    y_low[n, pl.ds(x, 1), :] = value[0:1]
    y_high[n, pl.ds(x, 1), :] = value[BY - 1 : BY]


def edge_shapes(n):
    return [(n, *EDGE)] * 4


def first_edges_kernel(u, k, x_low, x_high, y_low, y_high, last):
    for n in range(STEPS):
        x_low[n] = u[n, 0]
        x_high[n] = u[n, BX - 1]
    for j in range(KW):
        x_low[STEPS + j] = k[j]
        x_high[STEPS + j] = k[BX - KW + j]
    for n in range(STEPS + 1):
        for x in range(BX):
            row = u[n, x] if n < STEPS else k[x]
            y_low[n, pl.ds(x, 1), :] = row[0:1]
            y_high[n, pl.ds(x, 1), :] = row[BY - 1 : BY]
    last[...] = u[STEPS - 1]


def first_kernel(u, h, k, hxl, hxh, hyl, hyh, prev, g_out, first, x_low, x_high, y_low, y_high, last, kx):
    sx, sy, tm = lax.axis_index("sx"), lax.axis_index("sy"), lax.axis_index("tm")
    has_xl, has_xh = inside(sx > 0), inside(sx < 3)
    has_yl, has_yh = inside(sy > 0), inside(sy < 3)
    has_prev = inside(tm > 0)
    row, lane = row_index(), lane_index()
    for j in range(KW):
        kx[j] = hxl[STEPS + j] * has_xl
        kx[KW + BX + j] = hxh[STEPS + j] * has_xh
    for x in range(BX):
        kx[KW + x] = k[x]
    for x in range(BX):
        kc = k[x]
        k_yl = hyl[STEPS, pl.ds(x, 1), :] * has_yl
        k_yh = hyh[STEPS, pl.ds(x, 1), :] * has_yh
        k_below, k_above = y_sides(kc, k_yl, k_yh, row)
        z_below = jnp.where(lane == 0, 0.0, pltpu.roll(kc, 1, 1))
        z_above = jnp.where(lane == BZ - 1, 0.0, pltpu.roll(kc, BZ - 1, 1))
        g = [0.5 * (kc + other) for other in (kx[KW - 1 + x], kx[KW + 1 + x], k_below, k_above, z_below, z_above)]
        coupling = g[0] + g[1] + g[2] + g[3] + g[4] + g[5]
        if x == 0:
            g[0] = g[0] * has_xl
        if x == BX - 1:
            g[1] = g[1] * has_xh
        g[2] = jnp.where(row == 0, g[2] * has_yl, g[2])
        g[3] = jnp.where(row == BY - 1, g[3] * has_yh, g[3])
        g[4] = jnp.where(lane == 0, 0.0, g[4])
        g[5] = jnp.where(lane == BZ - 1, 0.0, g[5])
        for i in range(6):
            g_out[i, x] = g[i]
        g_out[6, x] = coupling
        factor = relax / (1.0 + coupling)
        running = prev[x] * has_prev
        for n in range(STEPS):
            value = u[n, x]
            below = u[n, x - 1] if x > 0 else hxl[n]
            above = u[n, x + 1] if x < BX - 1 else hxh[n]
            sides = y_sides(value, hyl[n, pl.ds(x, 1), :], hyh[n, pl.ds(x, 1), :], row)
            running = keep * value + factor * (h[n, x] + beside(value, below, above, *sides, g) + running)
            first[n, x] = running
            if x == 0:
                x_low[n] = running
            if x == BX - 1:
                x_high[n] = running
            y_low[pl.ds(n * BX + x, 1), :] = running[0:1]
            y_high[pl.ds(n * BX + x, 1), :] = running[BY - 1 : BY]
        last[x] = running
    for x in range(KX):
        kc = kx[x]
        for j in range(KW):
            at = STEPS * BX + j * KX + x
            y_low[pl.ds(at, 1), :] = kc[j : j + 1]
            y_high[pl.ds(at, 1), :] = kc[BY - KW + j : BY - KW + j + 1]


def coarse_terms_kernel(kx, yl, yh, factor, factor4, g_out, ke):
    sx, sy = lax.axis_index("sx"), lax.axis_index("sy")
    has_yl, has_yh = inside(sy > 0), inside(sy < 3)
    row, lane = row_index(EY), lane_index(EY)
    for x in range(KX):
        ke[x, pl.ds(0, BY), :] = kx[x]
        for j in range(KW):
            at = STEPS * BX + j * KX + x
            ke[x, pl.ds(BY + j, 1), :] = yh[pl.ds(at, 1), :] * has_yh
            ke[x, pl.ds(EY - KW + j, 1), :] = yl[pl.ds(at, 1), :] * has_yl
    y_in = jnp.where(row < BY, 1.0, jnp.where(row < BY + KW, has_yh, has_yl))
    for x in range(EX):
        kc = ke[x + 1]
        others = (
            ke[x],
            ke[x + 2],
            pltpu.roll(kc, 1, 0),
            pltpu.roll(kc, EY - 1, 0),
            jnp.where(lane == 0, 0.0, pltpu.roll(kc, 1, 1)),
            jnp.where(lane == BZ - 1, 0.0, pltpu.roll(kc, BZ - 1, 1)),
        )
        g = [0.5 * (kc + other) for other in others]
        coupling = g[0] + g[1] + g[2] + g[3] + g[4] + g[5]
        x_in = inside(sx > 0) if x < WIDE else inside(sx < 3) if x >= BX + WIDE else f32(1.0)
        factor[x] = (relax / (1.0 + 8.0 * coupling)) * (y_in * x_in)
        if 2 <= x <= EX - 3:
            factor4[x - 2] = (relax / (1.0 + 4.0 * coupling)) * (y_in * x_in)
        if 1 <= x <= EX - 2:
            g[4] = jnp.where(lane == 0, 0.0, g[4])
            g[5] = jnp.where(lane == BZ - 1, 0.0, g[5])
            for i in range(6):
                g_out[i, x - 1] = g[i]


def defect_fine_kernel(first, h, g_ref, hxl, hxh, yl, yh, prev, rhs, e0, e1, x_low, x_high, y_low, y_high):
    has_prev = inside(lax.axis_index("tm") > 0)
    row = row_index()
    for x in range(BX):
        g, coupling = row_coefficients(g_ref, x)
        diagonal = 1.0 + coupling
        factor = relax / (1.0 + 2.0 * coupling)
        earlier = prev[x] * has_prev
        parts = []
        for n in range(STEPS):
            value = first[n, x]
            below = first[n, x - 1] if x > 0 else hxl[n]
            above = first[n, x + 1] if x < BX - 1 else hxh[n]
            at = pl.ds(n * BX + x, 1)
            sides = y_sides(value, yl[at, :], yh[at, :], row)
            parts.append(h[n, x] + earlier - diagonal * value + beside(value, below, above, *sides, g))
            earlier = value
        r0, r1 = parts[0] + parts[1], parts[2] + parts[3]
        rhs[0, x] = r0
        rhs[1, x] = r1
        v0 = factor * r0
        v1 = factor * (r1 + v0)
        e0[x] = v0
        e1[x] = v1
        put_edges((x_low, x_high, y_low, y_high), 0, x, v0)
        put_edges((x_low, x_high, y_low, y_high), 1, x, v1)


def defect_mid_kernel(e0, e1, rhs, g_ref, hxl, hxh, hyl, hyh, prev, rhs2, err2, x_low, x_high, y_low, y_high):
    has_prev = inside(lax.axis_index("tm") > 0)
    row = row_index()
    for x in range(BX):
        g, coupling = row_coefficients(g_ref, x)
        diagonal = 1.0 + 2.0 * coupling
        earlier = prev[x] * has_prev
        total = None
        for n, e in enumerate((e0, e1)):
            value = e[x]
            below = e[x - 1] if x > 0 else hxl[n]
            above = e[x + 1] if x < BX - 1 else hxh[n]
            sides = y_sides(value, hyl[n, pl.ds(x, 1), :], hyh[n, pl.ds(x, 1), :], row)
            part = rhs[n, x] + earlier - diagonal * value + 2.0 * beside(value, below, above, *sides, g)
            total = part if total is None else total + part
            earlier = value
        rhs2[x] = total
        value = relax / (1.0 + 4.0 * coupling) * total
        err2[x] = value
        put_edges((x_low, x_high, y_low, y_high), 0, x, value)


def defect_last_kernel(err2, rhs2, g_ref, hxl, hxh, hyl, hyh, prev, out):
    has_prev = inside(lax.axis_index("tm") > 0)
    row = row_index()
    for x in range(BX):
        g, coupling = row_coefficients(g_ref, x)
        value = err2[x]
        below = err2[x - 1] if x > 0 else hxl[0]
        above = err2[x + 1] if x < BX - 1 else hxh[0]
        sides = y_sides(value, hyl[0, pl.ds(x, 1), :], hyh[0, pl.ds(x, 1), :], row)
        near = 4.0 * beside(value, below, above, *sides, g)
        earlier = prev[x] * has_prev
        out[0, x] = rhs2[x] + earlier - (1.0 + 4.0 * coupling) * value + near
        out[1, x] = value
        out[2, x] = earlier


HALF = BX // 2 * BY
XH, YH, CH = HALF, HALF + WIDE * BY, HALF + WIDE * (BY + BX)
SHARE = CH + 8
SIDE = 5 * BY
EXTRA = 2 * SIDE + 8
ALL = COARSE * SHARE


def coarse_edges_kernel(own, other, half, x_edge, y_edge, corner_a, corner_b, rhs3):
    core = lax.axis_index("tm") % 2
    for x in range(BX):
        rhs3[x] = own[0, x] + other[0, x]

    def send(c):
        zero, one = (own, other) if c == 0 else (other, own)
        fields = ((rhs3, WIDE), (zero.at[1], 2), (one.at[1], 2), (zero.at[2], 1))
        for i in range(BX // 2):
            half[pl.ds(i * BY, BY), :] = rhs3[c * (BX // 2) + i]
        at = 0
        for field, width in fields:
            for j in range(width):
                x_edge[pl.ds((at + j) * BY, BY), :] = field[c * (BX - width) + j]
            for x in range(BX):
                y_edge[pl.ds(at * BX + x * width, width), :] = field[x, pl.ds(c * (BY - width), width), :]
            at += width
        near, then = c * (BX - 1), c * (BX - 3) + 1
        for corner, flip in ((corner_a, False), (corner_b, True)):
            near_y, then_y = (BY - 1 - near, BY - 1 - then) if flip else (near, then)
            corner[...] = jnp.zeros((8, BZ), f32)
            cells = ((rhs3, near, near_y), (rhs3, near, then_y), (rhs3, then, near_y),
                     (zero.at[1], near, near_y), (one.at[1], near, near_y))
            for i, (field, x, y) in enumerate(cells):
                corner[pl.ds(i, 1), :] = field[x, pl.ds(y, 1), :]

    pl.when(core == 1)(lambda: send(1))
    pl.when(core == 0)(lambda: send(0))


def share_kernel(half, x_edge, y_edge, corner_a, corner_b, share, extra):
    share[pl.ds(0, HALF), :] = half[...]
    share[pl.ds(XH, WIDE * BY), :] = x_edge[pl.ds(0, WIDE * BY), :]
    share[pl.ds(YH, WIDE * BX), :] = y_edge[pl.ds(0, WIDE * BX), :]
    share[pl.ds(CH, 8), :] = corner_a[...]
    share[pl.ds(CH + 3, 3), :] = corner_b[pl.ds(0, 3), :]
    extra[pl.ds(0, SIDE), :] = x_edge[pl.ds(WIDE * BY, SIDE), :]
    extra[pl.ds(SIDE, SIDE), :] = y_edge[pl.ds(WIDE * BX, SIDE), :]
    extra[pl.ds(2 * SIDE, 8), :] = corner_a[...]
    extra[pl.ds(2 * SIDE, 2), :] = corner_a[pl.ds(3, 2), :]
    extra[pl.ds(2 * SIDE + 2, 2), :] = corner_b[pl.ds(3, 2), :]


def order_kernel(*refs):
    parts, extra, out = refs[:8], refs[8], refs[9]
    tm = lax.axis_index("tm")
    ring, half = (tm // 2) % 4, tm // 8
    for far in range(2):
        for s in range(4):
            step = (half + far) % 2 * 4 + (ring + 4 - s) % 4
            out[pl.ds(pl.multiple_of(step * SHARE, 8), SHARE), :] = parts[far * 4 + s][...]
    out[pl.ds(ALL, EXTRA), :] = extra[...]


def coarse_kernel(mine, other, factor, factor4, ge_ref, err2, prev, second, e0, e1, exl, exh, eyl, eyh, eprev, rhs, g_ref,
                  out0, out1, x_low, x_high, y_low, y_high, r, e, err3, now2, before2, sum2, sum2_before, fixed2):
    sx, sy, tm = lax.axis_index("sx"), lax.axis_index("sy"), lax.axis_index("tm")
    core = tm % 2
    has_xl, has_xh = inside(sx > 0), inside(sx < 3)
    has_yl, has_yh = inside(sy > 0), inside(sy < 3)
    has_prev, has_second = inside(tm > 0), inside(tm > 1)
    nothing = jnp.zeros((8, BZ), f32)

    def fill(c, low, high):
        for m in range(COARSE):
            base = m * SHARE
            for x in range(EX):
                r[m, x, pl.ds(BY, 8), :] = nothing
            for j in range(WIDE):
                r[m, j, pl.ds(0, BY), :] = low[pl.ds(base + XH + j * BY, BY), :]
                r[m, BX + WIDE + j, pl.ds(0, BY), :] = high[pl.ds(base + XH + j * BY, BY), :]
            for x in range(BX):
                source = (low, high)[x // (BX // 2)]
                r[m, x + WIDE, pl.ds(0, BY), :] = source[pl.ds(base + x % (BX // 2) * BY, BY), :]
                r[m, x + WIDE, pl.ds(BY, WIDE), :] = high[pl.ds(base + YH + x * WIDE, WIDE), :]
                r[m, x + WIDE, pl.ds(EY - WIDE, WIDE), :] = low[pl.ds(base + YH + x * WIDE, WIDE), :]
            for i, (dx, dy) in enumerate(((1, 1), (1, 2), (2, 1))):
                below, above = WIDE - dx, BX + WIDE - 1 + dx
                r[m, below, pl.ds(EY - dy, 1), :] = low[pl.ds(base + CH + i, 1), :]
                r[m, below, pl.ds(BY - 1 + dy, 1), :] = low[pl.ds(base + CH + 3 + i, 1), :]
                r[m, above, pl.ds(BY - 1 + dy, 1), :] = high[pl.ds(base + CH + i, 1), :]
                r[m, above, pl.ds(EY - dy, 1), :] = high[pl.ds(base + CH + 3 + i, 1), :]
        xs, ys, cs = ALL, ALL + SIDE, ALL + 2 * SIDE
        for x in range(BX + 4):
            now2[x, pl.ds(BY, 8), :] = nothing
        for x in range(BX + 2):
            before2[x, pl.ds(BY, 8), :] = nothing
        mine_at = c * 2
        for j in range(2):
            now2[j, pl.ds(0, BY), :] = low[pl.ds(xs + (mine_at + j) * BY, BY), :] * has_xl
            now2[BX + 2 + j, pl.ds(0, BY), :] = high[pl.ds(xs + (mine_at + j) * BY, BY), :] * has_xh
        for x in range(BX):
            now2[x + 2, pl.ds(0, BY), :] = err2[x]
            now2[x + 2, pl.ds(BY, 2), :] = high[pl.ds(ys + mine_at * BX + 2 * x, 2), :] * has_yh
            now2[x + 2, pl.ds(EY - 2, 2), :] = low[pl.ds(ys + mine_at * BX + 2 * x, 2), :] * has_yl
        now2[1, pl.ds(EY - 1, 1), :] = low[pl.ds(cs + c, 1), :] * (has_xl * has_yl)
        now2[1, pl.ds(BY, 1), :] = low[pl.ds(cs + 2 + c, 1), :] * (has_xl * has_yh)
        now2[BX + 2, pl.ds(BY, 1), :] = high[pl.ds(cs + c, 1), :] * (has_xh * has_yh)
        now2[BX + 2, pl.ds(EY - 1, 1), :] = high[pl.ds(cs + 2 + c, 1), :] * (has_xh * has_yl)
        at_low, at_high, y_at, step = (4, 4, 4 * BX, 1) if c == 0 else (1, 0, 0, 2)
        before2[0, pl.ds(0, BY), :] = low[pl.ds(xs + at_low * BY, BY), :] * has_xl
        before2[BX + 1, pl.ds(0, BY), :] = high[pl.ds(xs + at_high * BY, BY), :] * has_xh
        for x in range(BX):
            before2[x + 1, pl.ds(0, BY), :] = prev[x] * has_prev
            before2[x + 1, pl.ds(BY, 1), :] = high[pl.ds(ys + y_at + step * x, 1), :] * has_yh
            before2[x + 1, pl.ds(EY - 1, 1), :] = low[pl.ds(ys + y_at + step * x + step - 1, 1), :] * has_yl

    pl.when(core == 0)(lambda: fill(0, mine, other))
    pl.when(core == 1)(lambda: fill(1, other, mine))

    def sweep_one(x, carry):
        w = factor[x]
        running = jnp.zeros((EY, BZ), f32)
        for m in range(COARSE):
            running = w * (r[m, x] + running)
            e[m, x] = running
        return carry

    lax.fori_loop(0, EX, sweep_one, 0)

    def sweep_two(x, carry):
        w = factor[x + 1]
        g = [ge_ref[i, x] for i in range(6)]
        running = jnp.zeros((EY, BZ), f32)
        err3[0, x] = running
        for m in range(COARSE):
            value = e[m, x + 1]
            near = beside(value, e[m, x], e[m, x + 2], pltpu.roll(value, 1, 0), pltpu.roll(value, EY - 1, 0), g)
            running = keep * value + w * (r[m, x + 1] + 8.0 * near + running)
            err3[m + 1, x] = running
        return carry

    lax.fori_loop(0, BX + 4, sweep_two, 0)

    row = row_index()
    now, before, earliest = tm // 2 + 1, (tm + 1) // 2, tm // 2

    def turned(value):
        return pltpu.roll(value, 1, 0), pltpu.roll(value, EY - 1, 0)

    for x in range(BX + 4):
        sum2[x] = now2[x] + err3[now, x]
    for x in range(BX + 2):
        sum2_before[x] = before2[x] + err3[before, x + 1]
    for x in range(BX + 2):
        value = sum2[x + 1]
        near = beside(value, sum2[x], sum2[x + 2], *turned(value), [ge_ref[i, x + 1] for i in range(6)])
        fixed2[x] = keep * value + now2[x + 1] + factor4[x] * (4.0 * near + sum2_before[x])
    for x in range(BX):
        value = sum2_before[x + 1]
        near = beside(value, sum2_before[x], sum2_before[x + 2], *turned(value), [ge_ref[i, x + 2] for i in range(6)])
        two_before = second[x] * has_second + err3[earliest, x + 2, pl.ds(0, BY), :]
        fixed_before = (keep * value + before2[x + 1] + factor4[x + 1] * (4.0 * near))[0:BY]
        fixed_before = fixed_before + factor4[x + 1, pl.ds(0, BY), :] * two_before
        g, coupling = row_coefficients(g_ref, x)
        weight = relax / (1.0 + 2.0 * coupling)
        running = (eprev[x] + fixed_before) * has_prev
        here = fixed2[x + 1]
        f_below, f_above = fixed2[x, pl.ds(0, BY), :], fixed2[x + 2, pl.ds(0, BY), :]
        for n, (err, out) in enumerate(((e0, out0), (e1, out1))):
            value = err[x] + here[0:BY]
            below = (err[x - 1] if x > 0 else exl[n]) + f_below
            above = (err[x + 1] if x < BX - 1 else exh[n]) + f_above
            low = eyl[n, pl.ds(x, 1), :] + here[EY - 1 : EY]
            high = eyh[n, pl.ds(x, 1), :] + here[BY : BY + 1]
            near = 2.0 * beside(value, below, above, *y_sides(value, low, high, row), g)
            running = keep * value + weight * (rhs[n, x] + near + running)
            out[x] = running
            put_edges((x_low, x_high, y_low, y_high), n, x, running)


def solution_kernel(fix0, fix1, fxl, fxh, fyl, fyh, fprev, first, exl, exh, yl, yh, eprev, h, g_ref,
                    out, x_low, x_high, y_low, y_high, last):
    has_prev = inside(lax.axis_index("tm") > 0)
    row = row_index()
    for x in range(BX):
        g, coupling = row_coefficients(g_ref, x)
        factor = relax / (1.0 + coupling)
        running = (eprev[x] + fprev[x]) * has_prev
        for n in range(STEPS):
            fix, c = (fix0, fix1)[n // 2], n // 2
            value = first[n, x] + fix[x]
            below = (first[n, x - 1] + fix[x - 1]) if x > 0 else (exl[n] + fxl[c])
            above = (first[n, x + 1] + fix[x + 1]) if x < BX - 1 else (exh[n] + fxh[c])
            at = pl.ds(n * BX + x, 1)
            low = yl[at, :] + fyl[c, pl.ds(x, 1), :]
            high = yh[at, :] + fyh[c, pl.ds(x, 1), :]
            sides = y_sides(value, low, high, row)
            running = keep * value + factor * (h[n, x] + beside(value, below, above, *sides, g) + running)
            out[n, x] = running
            put_edges((x_low, x_high, y_low, y_high), n, x, running)
        last[x] = running


def copy_kernel(source, target):
    target[...] = source[...]


def residual_kernel(sol, h, g_ref, hxl, hxh, hyl, hyh, prev, out):
    has_prev = inside(lax.axis_index("tm") > 0)
    row = row_index()
    for x in range(BX):
        g, coupling = row_coefficients(g_ref, x)
        diagonal = 1.0 + coupling
        earlier = prev[x] * has_prev
        for n in range(STEPS):
            value = sol[n, x]
            below = sol[n, x - 1] if x > 0 else hxl[n]
            above = sol[n, x + 1] if x < BX - 1 else hxh[n]
            sides = y_sides(value, hyl[n, pl.ds(x, 1), :], hyh[n, pl.ds(x, 1), :], row)
            out[n, x] = h[n, x] + earlier - diagonal * value + beside(value, below, above, *sides, g)
            earlier = value


def gather_steps(own):
    def along(value, s):
        return across_tm(value, lambda i: (i & 9) | ((i + 2 * s) & 6))

    far = across_tm(own, lambda i: i ^ 8)
    near = [own] + [along(own, s) for s in (1, 2, 3)]
    return near + [far] + [along(far, s) for s in (1, 2, 3)]


def per_device(h, k, u):
    fine, two = (STEPS, *FIELD), (2, *FIELD)
    ypack = (YROWS, BZ)
    *edges, last = call(first_edges_kernel, [(STEPS + KW, *EDGE)] * 2 + [(STEPS + 1, *EDGE)] * 2 + [FIELD], u, k)
    (h,) = call(copy_kernel, [fine], h)
    halo, prev = exchange(edges, last)
    g, first, *edges, last, kx = call(
        first_kernel,
        [(7, *FIELD), fine, (STEPS, *EDGE), (STEPS, *EDGE), ypack, ypack, FIELD, (KX, BY, BZ)],
        u, h, k, *halo, prev,
    )
    first_halo, first_prev = exchange(edges, last)
    factor, factor4, g_coarse = call(
        coarse_terms_kernel,
        [(EX, EY, BZ), (BX + 2, EY, BZ), (6, BX + 4, EY, BZ)],
        kx, *first_halo[2:],
        scratch=[(KX, EY, BZ)],
    )
    rhs1, e0, e1, *edges = call(
        defect_fine_kernel, [two, FIELD, FIELD] + edge_shapes(2), first, h, g, *first_halo, first_prev
    )
    err1_halo, err1_prev = exchange(edges, e1)
    rhs2, err2, *edges = call(
        defect_mid_kernel, [FIELD, FIELD] + edge_shapes(1), e0, e1, rhs1, g, *err1_halo, err1_prev
    )
    err2_halo, err2_prev = exchange(edges, err2)
    (ends,) = call(defect_last_kernel, [(3, *FIELD)], err2, rhs2, g, *err2_halo, err2_prev)
    sibling = across_tm(ends, lambda i: i ^ 1)
    half, x_edge, y_edge, corner_a, corner_b = call(
        coarse_edges_kernel,
        [(HALF, BZ), (WIDE * BY + SIDE, BZ), (WIDE * BX + SIDE, BZ), (8, BZ), (8, BZ)],
        ends, sibling,
        scratch=[FIELD],
    )
    share, extra = call(
        share_kernel,
        [(SHARE, BZ), (EXTRA, BZ)],
        half, crossed(x_edge, 1, 0), crossed(y_edge, 0, 1), crossed(corner_a, 1, 1), crossed(corner_b, 1, -1),
    )
    err2_second = turn(err2_prev, "tm", 1)
    (mine,) = call(order_kernel, [(ALL + EXTRA, BZ)], *gather_steps(share), extra)
    other = across_tm(mine, lambda i: i ^ 1)
    fixed1a, fixed1b, *edges = call(
        coarse_kernel,
        [FIELD, FIELD] + edge_shapes(2),
        mine, other, factor, factor4, g_coarse, err2, err2_prev, err2_second,
        e0, e1, *err1_halo, err1_prev, rhs1, g,
        scratch=[
            (COARSE, EX, EY, BZ), (COARSE, EX, EY, BZ), (COARSE + 1, BX + 4, EY, BZ),
            (BX + 4, EY, BZ), (BX + 2, EY, BZ), (BX + 4, EY, BZ), (BX + 2, EY, BZ), (BX + 2, EY, BZ),
        ],
    )
    fixed1_halo, fixed1_prev = exchange(edges, fixed1b)
    last_iterate, *edges, last = call(
        solution_kernel,
        [fine] + edge_shapes(STEPS) + [FIELD],
        fixed1a, fixed1b, *fixed1_halo, fixed1_prev, first, *first_halo, first_prev, h, g,
    )
    out_halo, out_prev = exchange(edges, last)
    (out,) = call(copy_kernel, [fine], last_iterate)
    (residual,) = call(residual_kernel, [fine], last_iterate, h, g, *out_halo, out_prev)
    return out, residual


def solution(mesh):
    placed = (P("tm", "sx", "sy", None), P("sx", "sy", None), P("tm", "sx", "sy", None))
    return jax.shard_map(
        per_device,
        mesh=mesh,
        in_specs=placed,
        out_specs=(P("tm", "sx", "sy", None), P("tm", "sx", "sy", None)),
        check_vma=False,
    )
```

```python
import jax
import jax.numpy as jnp
from jax import lax
from jax.experimental import pallas as pl
from jax.experimental.pallas import tpu as pltpu
from jax.sharding import PartitionSpec as P

relax = 0.8
keep = 1.0 - relax
STEPS, BX, BY, BZ = 4, 16, 16, 128
COARSE = 8
WIDE = 3
KW = WIDE + 1
EX, EY = BX + 2 * WIDE, BY + 2 * KW
KX = BX + 2 * KW
f32 = jnp.float32
FIELD = (BX, BY, BZ)
EDGE = (BX, BZ)
YROWS = STEPS * BX + KW * KX


def turn(value, axis, by):
    devices = lax.axis_size(axis)
    return lax.ppermute(value, axis, [(i, (i + by) % devices) for i in range(devices)])


def across_tm(value, where):
    return lax.ppermute(value, "tm", [(i, where(i)) for i in range(16)])


def crossed(value, by_x, by_y):
    pairs = []
    for t in range(16):
        sign = 1 if t % 2 else -1
        for i in range(4):
            for j in range(4):
                to = ((t ^ 1) * 4 + (i + sign * by_x) % 4) * 4 + (j + sign * by_y) % 4
                pairs.append(((t * 4 + i) * 4 + j, to))
    return lax.ppermute(value, ("tm", "sx", "sy"), pairs)


def exchange(edges, last):
    x_low, x_high, y_low, y_high = edges
    earlier = turn(last, "tm", 1)
    return (
        turn(x_high, "sx", 1),
        turn(x_low, "sx", -1),
        turn(y_high, "sy", 1),
        turn(y_low, "sy", -1),
    ), earlier


def call(kernel, outs, *args, scratch=()):
    vmem = pl.BlockSpec(memory_space=pltpu.VMEM)
    return pl.pallas_call(
        kernel,
        out_shape=[jax.ShapeDtypeStruct(s, f32) for s in outs],
        in_specs=[vmem] * len(args),
        out_specs=[vmem] * len(outs),
        scratch_shapes=[pltpu.VMEM(s, f32) for s in scratch],
        compiler_params=pltpu.CompilerParams(vmem_limit_bytes=40 * 2**20),
    )(*args)


def inside(condition):
    return jnp.where(condition, f32(1.0), f32(0.0))


def row_index(rows=BY):
    return lax.broadcasted_iota(jnp.int32, (rows, BZ), 0)


def lane_index(rows=BY):
    return lax.broadcasted_iota(jnp.int32, (rows, BZ), 1)


def y_sides(value, low, high, row):
    below = jnp.where(row == 0, low, pltpu.roll(value, 1, 0))
    above = jnp.where(row == BY - 1, high, pltpu.roll(value, BY - 1, 0))
    return below, above


def beside(value, x_below, x_above, y_below, y_above, g):
    total = g[0] * x_below + g[1] * x_above
    total = total + g[2] * y_below + g[3] * y_above
    return total + g[4] * pltpu.roll(value, 1, 1) + g[5] * pltpu.roll(value, BZ - 1, 1)


def row_coefficients(g_ref, x):
    return [g_ref[i, x] for i in range(6)], g_ref[6, x]


def put_edges(refs, n, x, value):
    x_low, x_high, y_low, y_high = refs
    if x == 0:
        x_low[n] = value
    if x == BX - 1:
        x_high[n] = value
    y_low[n, pl.ds(x, 1), :] = value[0:1]
    y_high[n, pl.ds(x, 1), :] = value[BY - 1 : BY]


def edge_shapes(n):
    return [(n, *EDGE)] * 4


def first_edges_kernel(u, k, x_low, x_high, y_low, y_high, last):
    for n in range(STEPS):
        x_low[n] = u[n, 0]
        x_high[n] = u[n, BX - 1]
    for j in range(KW):
        x_low[STEPS + j] = k[j]
        x_high[STEPS + j] = k[BX - KW + j]
    for n in range(STEPS + 1):
        for x in range(BX):
            row = u[n, x] if n < STEPS else k[x]
            y_low[n, pl.ds(x, 1), :] = row[0:1]
            y_high[n, pl.ds(x, 1), :] = row[BY - 1 : BY]
    last[...] = u[STEPS - 1]


def first_kernel(u, h, k, hxl, hxh, hyl, hyh, prev, g_out, first, x_low, x_high, y_low, y_high, last, kx):
    sx, sy, tm = lax.axis_index("sx"), lax.axis_index("sy"), lax.axis_index("tm")
    has_xl, has_xh = inside(sx > 0), inside(sx < 3)
    has_yl, has_yh = inside(sy > 0), inside(sy < 3)
    has_prev = inside(tm > 0)
    row, lane = row_index(), lane_index()
    for j in range(KW):
        kx[j] = hxl[STEPS + j] * has_xl
        kx[KW + BX + j] = hxh[STEPS + j] * has_xh
    for x in range(BX):
        kx[KW + x] = k[x]
    for x in range(BX):
        kc = k[x]
        k_yl = hyl[STEPS, pl.ds(x, 1), :] * has_yl
        k_yh = hyh[STEPS, pl.ds(x, 1), :] * has_yh
        k_below, k_above = y_sides(kc, k_yl, k_yh, row)
        z_below = jnp.where(lane == 0, 0.0, pltpu.roll(kc, 1, 1))
        z_above = jnp.where(lane == BZ - 1, 0.0, pltpu.roll(kc, BZ - 1, 1))
        g = [0.5 * (kc + other) for other in (kx[KW - 1 + x], kx[KW + 1 + x], k_below, k_above, z_below, z_above)]
        coupling = g[0] + g[1] + g[2] + g[3] + g[4] + g[5]
        if x == 0:
            g[0] = g[0] * has_xl
        if x == BX - 1:
            g[1] = g[1] * has_xh
        g[2] = jnp.where(row == 0, g[2] * has_yl, g[2])
        g[3] = jnp.where(row == BY - 1, g[3] * has_yh, g[3])
        g[4] = jnp.where(lane == 0, 0.0, g[4])
        g[5] = jnp.where(lane == BZ - 1, 0.0, g[5])
        for i in range(6):
            g_out[i, x] = g[i]
        g_out[6, x] = coupling
        factor = relax / (1.0 + coupling)
        running = prev[x] * has_prev
        for n in range(STEPS):
            value = u[n, x]
            below = u[n, x - 1] if x > 0 else hxl[n]
            above = u[n, x + 1] if x < BX - 1 else hxh[n]
            sides = y_sides(value, hyl[n, pl.ds(x, 1), :], hyh[n, pl.ds(x, 1), :], row)
            running = keep * value + factor * (h[n, x] + beside(value, below, above, *sides, g) + running)
            first[n, x] = running
            if x == 0:
                x_low[n] = running
            if x == BX - 1:
                x_high[n] = running
            y_low[pl.ds(n * BX + x, 1), :] = running[0:1]
            y_high[pl.ds(n * BX + x, 1), :] = running[BY - 1 : BY]
        last[x] = running
    for x in range(KX):
        kc = kx[x]
        for j in range(KW):
            at = STEPS * BX + j * KX + x
            y_low[pl.ds(at, 1), :] = kc[j : j + 1]
            y_high[pl.ds(at, 1), :] = kc[BY - KW + j : BY - KW + j + 1]


def coarse_terms_kernel(kx, yl, yh, factor, factor4, g_out, ke):
    sx, sy = lax.axis_index("sx"), lax.axis_index("sy")
    has_yl, has_yh = inside(sy > 0), inside(sy < 3)
    row, lane = row_index(EY), lane_index(EY)
    for x in range(KX):
        ke[x, pl.ds(0, BY), :] = kx[x]
        for j in range(KW):
            at = STEPS * BX + j * KX + x
            ke[x, pl.ds(BY + j, 1), :] = yh[pl.ds(at, 1), :] * has_yh
            ke[x, pl.ds(EY - KW + j, 1), :] = yl[pl.ds(at, 1), :] * has_yl
    y_in = jnp.where(row < BY, 1.0, jnp.where(row < BY + KW, has_yh, has_yl))
    for x in range(EX):
        kc = ke[x + 1]
        others = (
            ke[x],
            ke[x + 2],
            pltpu.roll(kc, 1, 0),
            pltpu.roll(kc, EY - 1, 0),
            jnp.where(lane == 0, 0.0, pltpu.roll(kc, 1, 1)),
            jnp.where(lane == BZ - 1, 0.0, pltpu.roll(kc, BZ - 1, 1)),
        )
        g = [0.5 * (kc + other) for other in others]
        coupling = g[0] + g[1] + g[2] + g[3] + g[4] + g[5]
        x_in = inside(sx > 0) if x < WIDE else inside(sx < 3) if x >= BX + WIDE else f32(1.0)
        factor[x] = (relax / (1.0 + 8.0 * coupling)) * (y_in * x_in)
        if 2 <= x <= EX - 3:
            factor4[x - 2] = (relax / (1.0 + 4.0 * coupling)) * (y_in * x_in)
        if 1 <= x <= EX - 2:
            g[4] = jnp.where(lane == 0, 0.0, g[4])
            g[5] = jnp.where(lane == BZ - 1, 0.0, g[5])
            for i in range(6):
                g_out[i, x - 1] = g[i]


def defect_fine_kernel(first, h, g_ref, hxl, hxh, yl, yh, prev, rhs, e0, e1, x_low, x_high, y_low, y_high):
    has_prev = inside(lax.axis_index("tm") > 0)
    row = row_index()
    for x in range(BX):
        g, coupling = row_coefficients(g_ref, x)
        diagonal = 1.0 + coupling
        factor = relax / (1.0 + 2.0 * coupling)
        earlier = prev[x] * has_prev
        parts = []
        for n in range(STEPS):
            value = first[n, x]
            below = first[n, x - 1] if x > 0 else hxl[n]
            above = first[n, x + 1] if x < BX - 1 else hxh[n]
            at = pl.ds(n * BX + x, 1)
            sides = y_sides(value, yl[at, :], yh[at, :], row)
            parts.append(h[n, x] + earlier - diagonal * value + beside(value, below, above, *sides, g))
            earlier = value
        r0, r1 = parts[0] + parts[1], parts[2] + parts[3]
        rhs[0, x] = r0
        rhs[1, x] = r1
        v0 = factor * r0
        v1 = factor * (r1 + v0)
        e0[x] = v0
        e1[x] = v1
        put_edges((x_low, x_high, y_low, y_high), 0, x, v0)
        put_edges((x_low, x_high, y_low, y_high), 1, x, v1)


def defect_mid_kernel(e0, e1, rhs, g_ref, hxl, hxh, hyl, hyh, prev, rhs2, err2, x_low, x_high, y_low, y_high):
    has_prev = inside(lax.axis_index("tm") > 0)
    row = row_index()
    for x in range(BX):
        g, coupling = row_coefficients(g_ref, x)
        diagonal = 1.0 + 2.0 * coupling
        earlier = prev[x] * has_prev
        total = None
        for n, e in enumerate((e0, e1)):
            value = e[x]
            below = e[x - 1] if x > 0 else hxl[n]
            above = e[x + 1] if x < BX - 1 else hxh[n]
            sides = y_sides(value, hyl[n, pl.ds(x, 1), :], hyh[n, pl.ds(x, 1), :], row)
            part = rhs[n, x] + earlier - diagonal * value + 2.0 * beside(value, below, above, *sides, g)
            total = part if total is None else total + part
            earlier = value
        rhs2[x] = total
        value = relax / (1.0 + 4.0 * coupling) * total
        err2[x] = value
        put_edges((x_low, x_high, y_low, y_high), 0, x, value)


def defect_last_kernel(err2, rhs2, g_ref, hxl, hxh, hyl, hyh, prev, out):
    has_prev = inside(lax.axis_index("tm") > 0)
    row = row_index()
    for x in range(BX):
        g, coupling = row_coefficients(g_ref, x)
        value = err2[x]
        below = err2[x - 1] if x > 0 else hxl[0]
        above = err2[x + 1] if x < BX - 1 else hxh[0]
        sides = y_sides(value, hyl[0, pl.ds(x, 1), :], hyh[0, pl.ds(x, 1), :], row)
        near = 4.0 * beside(value, below, above, *sides, g)
        earlier = prev[x] * has_prev
        out[0, x] = rhs2[x] + earlier - (1.0 + 4.0 * coupling) * value + near
        out[1, x] = value
        out[2, x] = earlier


HALF = BX // 2 * BY
XH, YH, CH = HALF, HALF + WIDE * BY, HALF + WIDE * (BY + BX)
SHARE = CH + 8
SIDE = 5 * BY
EXTRA = 2 * SIDE + 8
ALL = COARSE * SHARE


def coarse_edges_kernel(own, other, half, x_edge, y_edge, corner_a, corner_b, rhs3):
    core = lax.axis_index("tm") % 2
    for x in range(BX):
        rhs3[x] = own[0, x] + other[0, x]

    def send(c):
        zero, one = (own, other) if c == 0 else (other, own)
        fields = ((rhs3, WIDE), (zero.at[1], 2), (one.at[1], 2), (zero.at[2], 1))
        for i in range(BX // 2):
            half[pl.ds(i * BY, BY), :] = rhs3[c * (BX // 2) + i]
        at = 0
        for field, width in fields:
            for j in range(width):
                x_edge[pl.ds((at + j) * BY, BY), :] = field[c * (BX - width) + j]
            for x in range(BX):
                y_edge[pl.ds(at * BX + x * width, width), :] = field[x, pl.ds(c * (BY - width), width), :]
            at += width
        near, then = c * (BX - 1), c * (BX - 3) + 1
        for corner, flip in ((corner_a, False), (corner_b, True)):
            near_y, then_y = (BY - 1 - near, BY - 1 - then) if flip else (near, then)
            corner[...] = jnp.zeros((8, BZ), f32)
            cells = ((rhs3, near, near_y), (rhs3, near, then_y), (rhs3, then, near_y),
                     (zero.at[1], near, near_y), (one.at[1], near, near_y))
            for i, (field, x, y) in enumerate(cells):
                corner[pl.ds(i, 1), :] = field[x, pl.ds(y, 1), :]

    pl.when(core == 1)(lambda: send(1))
    pl.when(core == 0)(lambda: send(0))


def share_kernel(half, x_edge, y_edge, corner_a, corner_b, share, extra):
    share[pl.ds(0, HALF), :] = half[...]
    share[pl.ds(XH, WIDE * BY), :] = x_edge[pl.ds(0, WIDE * BY), :]
    share[pl.ds(YH, WIDE * BX), :] = y_edge[pl.ds(0, WIDE * BX), :]
    share[pl.ds(CH, 8), :] = corner_a[...]
    share[pl.ds(CH + 3, 3), :] = corner_b[pl.ds(0, 3), :]
    extra[pl.ds(0, SIDE), :] = x_edge[pl.ds(WIDE * BY, SIDE), :]
    extra[pl.ds(SIDE, SIDE), :] = y_edge[pl.ds(WIDE * BX, SIDE), :]
    extra[pl.ds(2 * SIDE, 8), :] = corner_a[...]
    extra[pl.ds(2 * SIDE, 2), :] = corner_a[pl.ds(3, 2), :]
    extra[pl.ds(2 * SIDE + 2, 2), :] = corner_b[pl.ds(3, 2), :]


def order_kernel(*refs):
    parts, extra, out = refs[:8], refs[8], refs[9]
    tm = lax.axis_index("tm")
    ring, half = (tm // 2) % 4, tm // 8
    for far in range(2):
        for s in range(4):
            step = (half + far) % 2 * 4 + (ring + 4 - s) % 4
            out[pl.ds(pl.multiple_of(step * SHARE, 8), SHARE), :] = parts[far * 4 + s][...]
    out[pl.ds(ALL, EXTRA), :] = extra[...]


def coarse_kernel(mine, other, factor, factor4, ge_ref, err2, prev, second, e0, e1, exl, exh, eyl, eyh, eprev, rhs, g_ref,
                  out0, out1, x_low, x_high, y_low, y_high, r, e, err3, now2, before2, sum2, sum2_before, fixed2):
    sx, sy, tm = lax.axis_index("sx"), lax.axis_index("sy"), lax.axis_index("tm")
    core = tm % 2
    has_xl, has_xh = inside(sx > 0), inside(sx < 3)
    has_yl, has_yh = inside(sy > 0), inside(sy < 3)
    has_prev, has_second = inside(tm > 0), inside(tm > 1)
    nothing = jnp.zeros((8, BZ), f32)

    def fill(c, low, high):
        for m in range(COARSE):
            base = m * SHARE
            for x in range(EX):
                r[m, x, pl.ds(BY, 8), :] = nothing
            for j in range(WIDE):
                r[m, j, pl.ds(0, BY), :] = low[pl.ds(base + XH + j * BY, BY), :]
                r[m, BX + WIDE + j, pl.ds(0, BY), :] = high[pl.ds(base + XH + j * BY, BY), :]
            for x in range(BX):
                source = (low, high)[x // (BX // 2)]
                r[m, x + WIDE, pl.ds(0, BY), :] = source[pl.ds(base + x % (BX // 2) * BY, BY), :]
                r[m, x + WIDE, pl.ds(BY, WIDE), :] = high[pl.ds(base + YH + x * WIDE, WIDE), :]
                r[m, x + WIDE, pl.ds(EY - WIDE, WIDE), :] = low[pl.ds(base + YH + x * WIDE, WIDE), :]
            for i, (dx, dy) in enumerate(((1, 1), (1, 2), (2, 1))):
                below, above = WIDE - dx, BX + WIDE - 1 + dx
                r[m, below, pl.ds(EY - dy, 1), :] = low[pl.ds(base + CH + i, 1), :]
                r[m, below, pl.ds(BY - 1 + dy, 1), :] = low[pl.ds(base + CH + 3 + i, 1), :]
                r[m, above, pl.ds(BY - 1 + dy, 1), :] = high[pl.ds(base + CH + i, 1), :]
                r[m, above, pl.ds(EY - dy, 1), :] = high[pl.ds(base + CH + 3 + i, 1), :]
        xs, ys, cs = ALL, ALL + SIDE, ALL + 2 * SIDE
        for x in range(BX + 4):
            now2[x, pl.ds(BY, 8), :] = nothing
        for x in range(BX + 2):
            before2[x, pl.ds(BY, 8), :] = nothing
        mine_at = c * 2
        for j in range(2):
            now2[j, pl.ds(0, BY), :] = low[pl.ds(xs + (mine_at + j) * BY, BY), :] * has_xl
            now2[BX + 2 + j, pl.ds(0, BY), :] = high[pl.ds(xs + (mine_at + j) * BY, BY), :] * has_xh
        for x in range(BX):
            now2[x + 2, pl.ds(0, BY), :] = err2[x]
            now2[x + 2, pl.ds(BY, 2), :] = high[pl.ds(ys + mine_at * BX + 2 * x, 2), :] * has_yh
            now2[x + 2, pl.ds(EY - 2, 2), :] = low[pl.ds(ys + mine_at * BX + 2 * x, 2), :] * has_yl
        now2[1, pl.ds(EY - 1, 1), :] = low[pl.ds(cs + c, 1), :] * (has_xl * has_yl)
        now2[1, pl.ds(BY, 1), :] = low[pl.ds(cs + 2 + c, 1), :] * (has_xl * has_yh)
        now2[BX + 2, pl.ds(BY, 1), :] = high[pl.ds(cs + c, 1), :] * (has_xh * has_yh)
        now2[BX + 2, pl.ds(EY - 1, 1), :] = high[pl.ds(cs + 2 + c, 1), :] * (has_xh * has_yl)
        at_low, at_high, y_at, step = (4, 4, 4 * BX, 1) if c == 0 else (1, 0, 0, 2)
        before2[0, pl.ds(0, BY), :] = low[pl.ds(xs + at_low * BY, BY), :] * has_xl
        before2[BX + 1, pl.ds(0, BY), :] = high[pl.ds(xs + at_high * BY, BY), :] * has_xh
        for x in range(BX):
            before2[x + 1, pl.ds(0, BY), :] = prev[x] * has_prev
            before2[x + 1, pl.ds(BY, 1), :] = high[pl.ds(ys + y_at + step * x, 1), :] * has_yh
            before2[x + 1, pl.ds(EY - 1, 1), :] = low[pl.ds(ys + y_at + step * x + step - 1, 1), :] * has_yl

    pl.when(core == 0)(lambda: fill(0, mine, other))
    pl.when(core == 1)(lambda: fill(1, other, mine))

    def sweep_one(x, carry):
        w = factor[x]
        running = jnp.zeros((EY, BZ), f32)
        for m in range(COARSE):
            running = w * (r[m, x] + running)
            e[m, x] = running
        return carry

    for x in range(EX):
        sweep_one(x, 0)

    def sweep_two(x, carry):
        w = factor[x + 1]
        g = [ge_ref[i, x] for i in range(6)]
        running = jnp.zeros((EY, BZ), f32)
        err3[0, x] = running
        for m in range(COARSE):
            value = e[m, x + 1]
            near = beside(value, e[m, x], e[m, x + 2], pltpu.roll(value, 1, 0), pltpu.roll(value, EY - 1, 0), g)
            running = keep * value + w * (r[m, x + 1] + 8.0 * near) + w * running
            err3[m + 1, x] = running
        return carry

    lax.fori_loop(0, BX + 4, sweep_two, 0, unroll=2)

    row = row_index()
    now, before, earliest = tm // 2 + 1, (tm + 1) // 2, tm // 2

    def turned(value):
        return pltpu.roll(value, 1, 0), pltpu.roll(value, EY - 1, 0)

    for x in range(BX + 4):
        sum2[x] = now2[x] + err3[now, x]
    for x in range(BX + 2):
        sum2_before[x] = before2[x] + err3[before, x + 1]
    for x in range(BX + 2):
        value = sum2[x + 1]
        near = beside(value, sum2[x], sum2[x + 2], *turned(value), [ge_ref[i, x + 1] for i in range(6)])
        fixed2[x] = keep * value + now2[x + 1] + factor4[x] * (4.0 * near + sum2_before[x])
    for x in range(BX):
        value = sum2_before[x + 1]
        near = beside(value, sum2_before[x], sum2_before[x + 2], *turned(value), [ge_ref[i, x + 2] for i in range(6)])
        two_before = second[x] * has_second + err3[earliest, x + 2, pl.ds(0, BY), :]
        fixed_before = (keep * value + before2[x + 1] + factor4[x + 1] * (4.0 * near))[0:BY]
        fixed_before = fixed_before + factor4[x + 1, pl.ds(0, BY), :] * two_before
        g, coupling = row_coefficients(g_ref, x)
        weight = relax / (1.0 + 2.0 * coupling)
        running = (eprev[x] + fixed_before) * has_prev
        here = fixed2[x + 1]
        f_below, f_above = fixed2[x, pl.ds(0, BY), :], fixed2[x + 2, pl.ds(0, BY), :]
        for n, (err, out) in enumerate(((e0, out0), (e1, out1))):
            value = err[x] + here[0:BY]
            below = (err[x - 1] if x > 0 else exl[n]) + f_below
            above = (err[x + 1] if x < BX - 1 else exh[n]) + f_above
            low = eyl[n, pl.ds(x, 1), :] + here[EY - 1 : EY]
            high = eyh[n, pl.ds(x, 1), :] + here[BY : BY + 1]
            near = 2.0 * beside(value, below, above, *y_sides(value, low, high, row), g)
            running = keep * value + weight * (rhs[n, x] + near + running)
            out[x] = running
            put_edges((x_low, x_high, y_low, y_high), n, x, running)


def solution_kernel(fix0, fix1, fxl, fxh, fyl, fyh, fprev, first, exl, exh, yl, yh, eprev, h, g_ref,
                    out, x_low, x_high, y_low, y_high, last):
    has_prev = inside(lax.axis_index("tm") > 0)
    row = row_index()
    for x in range(BX):
        g, coupling = row_coefficients(g_ref, x)
        factor = relax / (1.0 + coupling)
        running = (eprev[x] + fprev[x]) * has_prev
        for n in range(STEPS):
            fix, c = (fix0, fix1)[n // 2], n // 2
            value = first[n, x] + fix[x]
            below = (first[n, x - 1] + fix[x - 1]) if x > 0 else (exl[n] + fxl[c])
            above = (first[n, x + 1] + fix[x + 1]) if x < BX - 1 else (exh[n] + fxh[c])
            at = pl.ds(n * BX + x, 1)
            low = yl[at, :] + fyl[c, pl.ds(x, 1), :]
            high = yh[at, :] + fyh[c, pl.ds(x, 1), :]
            sides = y_sides(value, low, high, row)
            running = keep * value + factor * (h[n, x] + beside(value, below, above, *sides, g) + running)
            out[n, x] = running
            put_edges((x_low, x_high, y_low, y_high), n, x, running)
        last[x] = running


def copy_kernel(source, target):
    target[...] = source[...]


def residual_kernel(sol, h, g_ref, hxl, hxh, hyl, hyh, prev, out):
    has_prev = inside(lax.axis_index("tm") > 0)
    row = row_index()
    for x in range(BX):
        g, coupling = row_coefficients(g_ref, x)
        diagonal = 1.0 + coupling
        earlier = prev[x] * has_prev
        for n in range(STEPS):
            value = sol[n, x]
            below = sol[n, x - 1] if x > 0 else hxl[n]
            above = sol[n, x + 1] if x < BX - 1 else hxh[n]
            sides = y_sides(value, hyl[n, pl.ds(x, 1), :], hyh[n, pl.ds(x, 1), :], row)
            out[n, x] = h[n, x] + earlier - diagonal * value + beside(value, below, above, *sides, g)
            earlier = value


def gather_steps(own):
    def along(value, s):
        return across_tm(value, lambda i: (i & 9) | ((i + 2 * s) & 6))

    far = across_tm(own, lambda i: i ^ 8)
    near = [own] + [along(own, s) for s in (1, 2, 3)]
    return near + [far] + [along(far, s) for s in (1, 2, 3)]


def per_device(h, k, u):
    fine, two = (STEPS, *FIELD), (2, *FIELD)
    ypack = (YROWS, BZ)
    *edges, last = call(first_edges_kernel, [(STEPS + KW, *EDGE)] * 2 + [(STEPS + 1, *EDGE)] * 2 + [FIELD], u, k)
    (h,) = call(copy_kernel, [fine], h)
    halo, prev = exchange(edges, last)
    g, first, *edges, last, kx = call(
        first_kernel,
        [(7, *FIELD), fine, (STEPS, *EDGE), (STEPS, *EDGE), ypack, ypack, FIELD, (KX, BY, BZ)],
        u, h, k, *halo, prev,
    )
    first_halo, first_prev = exchange(edges, last)
    factor, factor4, g_coarse = call(
        coarse_terms_kernel,
        [(EX, EY, BZ), (BX + 2, EY, BZ), (6, BX + 4, EY, BZ)],
        kx, *first_halo[2:],
        scratch=[(KX, EY, BZ)],
    )
    rhs1, e0, e1, *edges = call(
        defect_fine_kernel, [two, FIELD, FIELD] + edge_shapes(2), first, h, g, *first_halo, first_prev
    )
    err1_halo, err1_prev = exchange(edges, e1)
    rhs2, err2, *edges = call(
        defect_mid_kernel, [FIELD, FIELD] + edge_shapes(1), e0, e1, rhs1, g, *err1_halo, err1_prev
    )
    err2_halo, err2_prev = exchange(edges, err2)
    (ends,) = call(defect_last_kernel, [(3, *FIELD)], err2, rhs2, g, *err2_halo, err2_prev)
    sibling = across_tm(ends, lambda i: i ^ 1)
    half, x_edge, y_edge, corner_a, corner_b = call(
        coarse_edges_kernel,
        [(HALF, BZ), (WIDE * BY + SIDE, BZ), (WIDE * BX + SIDE, BZ), (8, BZ), (8, BZ)],
        ends, sibling,
        scratch=[FIELD],
    )
    share, extra = call(
        share_kernel,
        [(SHARE, BZ), (EXTRA, BZ)],
        half, crossed(x_edge, 1, 0), crossed(y_edge, 0, 1), crossed(corner_a, 1, 1), crossed(corner_b, 1, -1),
    )
    share, err2_second = lax.optimization_barrier((share, turn(err2_prev, "tm", 1)))
    (mine,) = call(order_kernel, [(ALL + EXTRA, BZ)], *gather_steps(share), extra)
    other = across_tm(mine, lambda i: i ^ 1)
    fixed1a, fixed1b, *edges = call(
        coarse_kernel,
        [FIELD, FIELD] + edge_shapes(2),
        mine, other, factor, factor4, g_coarse, err2, err2_prev, err2_second,
        e0, e1, *err1_halo, err1_prev, rhs1, g,
        scratch=[
            (COARSE, EX, EY, BZ), (COARSE, EX, EY, BZ), (COARSE + 1, BX + 4, EY, BZ),
            (BX + 4, EY, BZ), (BX + 2, EY, BZ), (BX + 4, EY, BZ), (BX + 2, EY, BZ), (BX + 2, EY, BZ),
        ],
    )
    fixed1_halo, fixed1_prev = exchange(edges, fixed1b)
    last_iterate, *edges, last = call(
        solution_kernel,
        [fine] + edge_shapes(STEPS) + [FIELD],
        fixed1a, fixed1b, *fixed1_halo, fixed1_prev, first, *first_halo, first_prev, h, g,
    )
    out_halo, out_prev = exchange(edges, last)
    (out,) = call(copy_kernel, [fine], last_iterate)
    (residual,) = call(residual_kernel, [fine], last_iterate, h, g, *out_halo, out_prev)
    return out, residual


def solution(mesh):
    placed = (P("tm", "sx", "sy", None), P("sx", "sy", None), P("tm", "sx", "sy", None))
    return jax.shard_map(
        per_device,
        mesh=mesh,
        in_specs=placed,
        out_specs=(P("tm", "sx", "sy", None), P("tm", "sx", "sy", None)),
        check_vma=False,
    )
```

```python
import jax
import jax.numpy as jnp
from jax import lax
from jax.experimental import pallas as pl
from jax.experimental.pallas import tpu as pltpu
from jax.sharding import PartitionSpec as P

relax = 0.8
keep = 1.0 - relax
STEPS, BX, BY, BZ = 4, 16, 16, 128
COARSE = 8
WIDE = 3
KW = WIDE + 1
EX, EY = BX + 2 * WIDE, BY + 2 * KW
KX = BX + 2 * KW
f32 = jnp.float32
FIELD = (BX, BY, BZ)
EDGE = (BX, BZ)
YROWS = STEPS * BX + KW * KX


def turn(value, axis, by):
    devices = lax.axis_size(axis)
    return lax.ppermute(value, axis, [(i, (i + by) % devices) for i in range(devices)])


def across_tm(value, where):
    return lax.ppermute(value, "tm", [(i, where(i)) for i in range(16)])


def crossed(value, by_x, by_y):
    pairs = []
    for t in range(16):
        sign = 1 if t % 2 else -1
        for i in range(4):
            for j in range(4):
                to = ((t ^ 1) * 4 + (i + sign * by_x) % 4) * 4 + (j + sign * by_y) % 4
                pairs.append(((t * 4 + i) * 4 + j, to))
    return lax.ppermute(value, ("tm", "sx", "sy"), pairs)


def exchange(edges, last, steps=1):
    x_low, x_high, y_low, y_high = edges
    earlier = turn(last, "tm", steps)
    return (
        turn(x_high, "sx", 1),
        turn(x_low, "sx", -1),
        turn(y_high, "sy", 1),
        turn(y_low, "sy", -1),
    ), earlier


def call(kernel, outs, *args, scratch=()):
    vmem = pl.BlockSpec(memory_space=pltpu.VMEM)
    return pl.pallas_call(
        kernel,
        out_shape=[jax.ShapeDtypeStruct(s, f32) for s in outs],
        in_specs=[vmem] * len(args),
        out_specs=[vmem] * len(outs),
        scratch_shapes=[pltpu.VMEM(s, f32) for s in scratch],
        compiler_params=pltpu.CompilerParams(vmem_limit_bytes=40 * 2**20),
    )(*args)


def inside(condition):
    return jnp.where(condition, f32(1.0), f32(0.0))


def row_index(rows=BY):
    return lax.broadcasted_iota(jnp.int32, (rows, BZ), 0)


def lane_index(rows=BY):
    return lax.broadcasted_iota(jnp.int32, (rows, BZ), 1)


def y_sides(value, low, high, row):
    below = jnp.where(row == 0, low, pltpu.roll(value, 1, 0))
    above = jnp.where(row == BY - 1, high, pltpu.roll(value, BY - 1, 0))
    return below, above


def beside(value, x_below, x_above, y_below, y_above, g):
    total = g[0] * x_below + g[1] * x_above
    total = total + g[2] * y_below + g[3] * y_above
    return total + g[4] * pltpu.roll(value, 1, 1) + g[5] * pltpu.roll(value, BZ - 1, 1)


def row_coefficients(g_ref, x):
    return [g_ref[i, x] for i in range(6)], g_ref[6, x]


def put_edges(refs, n, x, value):
    x_low, x_high, y_low, y_high = refs
    if x == 0:
        x_low[n] = value
    if x == BX - 1:
        x_high[n] = value
    y_low[n, pl.ds(x, 1), :] = value[0:1]
    y_high[n, pl.ds(x, 1), :] = value[BY - 1 : BY]


def edge_shapes(n):
    return [(n, *EDGE)] * 4


def first_edges_kernel(u, k, x_low, x_high, y_low, y_high, last):
    for n in range(STEPS):
        x_low[n] = u[n, 0]
        x_high[n] = u[n, BX - 1]
    for j in range(KW):
        x_low[STEPS + j] = k[j]
        x_high[STEPS + j] = k[BX - KW + j]
    for n in range(STEPS + 1):
        for x in range(BX):
            row = u[n, x] if n < STEPS else k[x]
            y_low[n, pl.ds(x, 1), :] = row[0:1]
            y_high[n, pl.ds(x, 1), :] = row[BY - 1 : BY]
    last[...] = u[STEPS - 1]


def first_kernel(u, h, k, hxl, hxh, hyl, hyh, prev, g_out, first, x_low, x_high, y_low, y_high, last, kx):
    sx, sy, tm = lax.axis_index("sx"), lax.axis_index("sy"), lax.axis_index("tm")
    has_xl, has_xh = inside(sx > 0), inside(sx < 3)
    has_yl, has_yh = inside(sy > 0), inside(sy < 3)
    has_prev = inside(tm > 0)
    row, lane = row_index(), lane_index()
    for j in range(KW):
        kx[j] = hxl[STEPS + j] * has_xl
        kx[KW + BX + j] = hxh[STEPS + j] * has_xh
    for x in range(BX):
        kx[KW + x] = k[x]
    for x in range(BX):
        kc = k[x]
        k_yl = hyl[STEPS, pl.ds(x, 1), :] * has_yl
        k_yh = hyh[STEPS, pl.ds(x, 1), :] * has_yh
        k_below, k_above = y_sides(kc, k_yl, k_yh, row)
        z_below = jnp.where(lane == 0, 0.0, pltpu.roll(kc, 1, 1))
        z_above = jnp.where(lane == BZ - 1, 0.0, pltpu.roll(kc, BZ - 1, 1))
        g = [0.5 * (kc + other) for other in (kx[KW - 1 + x], kx[KW + 1 + x], k_below, k_above, z_below, z_above)]
        coupling = g[0] + g[1] + g[2] + g[3] + g[4] + g[5]
        if x == 0:
            g[0] = g[0] * has_xl
        if x == BX - 1:
            g[1] = g[1] * has_xh
        g[2] = jnp.where(row == 0, g[2] * has_yl, g[2])
        g[3] = jnp.where(row == BY - 1, g[3] * has_yh, g[3])
        g[4] = jnp.where(lane == 0, 0.0, g[4])
        g[5] = jnp.where(lane == BZ - 1, 0.0, g[5])
        for i in range(6):
            g_out[i, x] = g[i]
        g_out[6, x] = coupling
        factor = relax / (1.0 + coupling)
        running = prev[x] * has_prev
        for n in range(STEPS):
            value = u[n, x]
            below = u[n, x - 1] if x > 0 else hxl[n]
            above = u[n, x + 1] if x < BX - 1 else hxh[n]
            sides = y_sides(value, hyl[n, pl.ds(x, 1), :], hyh[n, pl.ds(x, 1), :], row)
            running = keep * value + factor * (h[n, x] + beside(value, below, above, *sides, g) + running)
            first[n, x] = running
            if x == 0:
                x_low[n] = running
            if x == BX - 1:
                x_high[n] = running
            y_low[pl.ds(n * BX + x, 1), :] = running[0:1]
            y_high[pl.ds(n * BX + x, 1), :] = running[BY - 1 : BY]
        last[x] = running
    for x in range(KX):
        kc = kx[x]
        for j in range(KW):
            at = STEPS * BX + j * KX + x
            y_low[pl.ds(at, 1), :] = kc[j : j + 1]
            y_high[pl.ds(at, 1), :] = kc[BY - KW + j : BY - KW + j + 1]


def coarse_terms_kernel(kx, yl, yh, factor, factor4, g_out, ke):
    sx, sy = lax.axis_index("sx"), lax.axis_index("sy")
    has_yl, has_yh = inside(sy > 0), inside(sy < 3)
    row, lane = row_index(EY), lane_index(EY)
    for x in range(KX):
        ke[x, pl.ds(0, BY), :] = kx[x]
        for j in range(KW):
            at = STEPS * BX + j * KX + x
            ke[x, pl.ds(BY + j, 1), :] = yh[pl.ds(at, 1), :] * has_yh
            ke[x, pl.ds(EY - KW + j, 1), :] = yl[pl.ds(at, 1), :] * has_yl
    y_in = jnp.where(row < BY, 1.0, jnp.where(row < BY + KW, has_yh, has_yl))
    for x in range(EX):
        kc = ke[x + 1]
        others = (
            ke[x],
            ke[x + 2],
            pltpu.roll(kc, 1, 0),
            pltpu.roll(kc, EY - 1, 0),
            jnp.where(lane == 0, 0.0, pltpu.roll(kc, 1, 1)),
            jnp.where(lane == BZ - 1, 0.0, pltpu.roll(kc, BZ - 1, 1)),
        )
        g = [0.5 * (kc + other) for other in others]
        coupling = g[0] + g[1] + g[2] + g[3] + g[4] + g[5]
        x_in = inside(sx > 0) if x < WIDE else inside(sx < 3) if x >= BX + WIDE else f32(1.0)
        factor[x] = (relax / (1.0 + 8.0 * coupling)) * (y_in * x_in)
        if 2 <= x <= EX - 3:
            factor4[x - 2] = (relax / (1.0 + 4.0 * coupling)) * (y_in * x_in)
        if 1 <= x <= EX - 2:
            g[4] = jnp.where(lane == 0, 0.0, g[4])
            g[5] = jnp.where(lane == BZ - 1, 0.0, g[5])
            for i in range(6):
                g_out[i, x - 1] = g[i]


def defect_fine_kernel(first, h, g_ref, hxl, hxh, yl, yh, prev, rhs, e0, e1, x_low, x_high, y_low, y_high):
    has_prev = inside(lax.axis_index("tm") > 0)
    row = row_index()
    for x in range(BX):
        g, coupling = row_coefficients(g_ref, x)
        diagonal = 1.0 + coupling
        factor = relax / (1.0 + 2.0 * coupling)
        earlier = prev[x] * has_prev
        parts = []
        for n in range(STEPS):
            value = first[n, x]
            below = first[n, x - 1] if x > 0 else hxl[n]
            above = first[n, x + 1] if x < BX - 1 else hxh[n]
            at = pl.ds(n * BX + x, 1)
            sides = y_sides(value, yl[at, :], yh[at, :], row)
            parts.append(h[n, x] + earlier - diagonal * value + beside(value, below, above, *sides, g))
            earlier = value
        r0, r1 = parts[0] + parts[1], parts[2] + parts[3]
        rhs[0, x] = r0
        rhs[1, x] = r1
        v0 = factor * r0
        v1 = factor * (r1 + v0)
        e0[x] = v0
        e1[x] = v1
        put_edges((x_low, x_high, y_low, y_high), 0, x, v0)
        put_edges((x_low, x_high, y_low, y_high), 1, x, v1)


def defect_mid_kernel(e0, e1, rhs, g_ref, hxl, hxh, hyl, hyh, prev, rhs2, err2, x_low, x_high, y_low, y_high):
    has_prev = inside(lax.axis_index("tm") > 0)
    row = row_index()
    for x in range(BX):
        g, coupling = row_coefficients(g_ref, x)
        diagonal = 1.0 + 2.0 * coupling
        earlier = prev[x] * has_prev
        total = None
        for n, e in enumerate((e0, e1)):
            value = e[x]
            below = e[x - 1] if x > 0 else hxl[n]
            above = e[x + 1] if x < BX - 1 else hxh[n]
            sides = y_sides(value, hyl[n, pl.ds(x, 1), :], hyh[n, pl.ds(x, 1), :], row)
            part = rhs[n, x] + earlier - diagonal * value + 2.0 * beside(value, below, above, *sides, g)
            total = part if total is None else total + part
            earlier = value
        rhs2[x] = total
        value = relax / (1.0 + 4.0 * coupling) * total
        err2[x] = value
        put_edges((x_low, x_high, y_low, y_high), 0, x, value)


def defect_last_kernel(err2, rhs2, g_ref, hxl, hxh, hyl, hyh, chip_before, out):
    has_chip = inside(lax.axis_index("tm") > 1)
    row = row_index()
    for x in range(BX):
        g, coupling = row_coefficients(g_ref, x)
        value = err2[x]
        below = err2[x - 1] if x > 0 else hxl[0]
        above = err2[x + 1] if x < BX - 1 else hxh[0]
        sides = y_sides(value, hyl[0, pl.ds(x, 1), :], hyh[0, pl.ds(x, 1), :], row)
        near = 4.0 * beside(value, below, above, *sides, g)
        out[0, x] = rhs2[x] - (1.0 + 4.0 * coupling) * value + near
        out[1, x] = value
        out[2, x] = chip_before[x] * has_chip


HALF = BX // 2 * BY
XH, YH, CH = HALF, HALF + WIDE * BY, HALF + WIDE * (BY + BX)
SHARE = CH + 8
SIDE = 5 * BY
EXTRA = 2 * SIDE + 8
ALL = COARSE * SHARE


def coarse_edges_kernel(own, other, half, x_edge, y_edge, corner_a, corner_b, rhs3):
    core = lax.axis_index("tm") % 2

    def send(c):
        zero, one = (own, other) if c == 0 else (other, own)
        for x in range(BX):
            rhs3[x] = zero[0, x] + one[0, x] + (zero[1, x] + one[2, x])
        fields = ((rhs3, WIDE), (zero.at[1], 2), (one.at[1], 2), (one.at[2], 1))
        for i in range(BX // 2):
            half[pl.ds(i * BY, BY), :] = rhs3[c * (BX // 2) + i]
        at = 0
        for field, width in fields:
            for j in range(width):
                x_edge[pl.ds((at + j) * BY, BY), :] = field[c * (BX - width) + j]
            for x in range(BX):
                y_edge[pl.ds(at * BX + x * width, width), :] = field[x, pl.ds(c * (BY - width), width), :]
            at += width
        near, then = c * (BX - 1), c * (BX - 3) + 1
        for corner, flip in ((corner_a, False), (corner_b, True)):
            near_y, then_y = (BY - 1 - near, BY - 1 - then) if flip else (near, then)
            corner[...] = jnp.zeros((8, BZ), f32)
            cells = ((rhs3, near, near_y), (rhs3, near, then_y), (rhs3, then, near_y),
                     (zero.at[1], near, near_y), (one.at[1], near, near_y))
            for i, (field, x, y) in enumerate(cells):
                corner[pl.ds(i, 1), :] = field[x, pl.ds(y, 1), :]

    pl.when(core == 1)(lambda: send(1))
    pl.when(core == 0)(lambda: send(0))


def share_kernel(half, x_edge, y_edge, corner_a, corner_b, share, extra):
    share[pl.ds(0, HALF), :] = half[...]
    share[pl.ds(XH, WIDE * BY), :] = x_edge[pl.ds(0, WIDE * BY), :]
    share[pl.ds(YH, WIDE * BX), :] = y_edge[pl.ds(0, WIDE * BX), :]
    share[pl.ds(CH, 8), :] = corner_a[...]
    share[pl.ds(CH + 3, 3), :] = corner_b[pl.ds(0, 3), :]
    extra[pl.ds(0, SIDE), :] = x_edge[pl.ds(WIDE * BY, SIDE), :]
    extra[pl.ds(SIDE, SIDE), :] = y_edge[pl.ds(WIDE * BX, SIDE), :]
    extra[pl.ds(2 * SIDE, 8), :] = corner_a[...]
    extra[pl.ds(2 * SIDE, 2), :] = corner_a[pl.ds(3, 2), :]
    extra[pl.ds(2 * SIDE + 2, 2), :] = corner_b[pl.ds(3, 2), :]


def order_kernel(*refs):
    parts, extra, out = refs[:8], refs[8], refs[9]
    tm = lax.axis_index("tm")
    ring, half = (tm // 2) % 4, tm // 8
    for far in range(2):
        for s in range(4):
            step = (half + far) % 2 * 4 + (ring + 4 - s) % 4
            out[pl.ds(pl.multiple_of(step * SHARE, 8), SHARE), :] = parts[far * 4 + s][...]
    out[pl.ds(ALL, EXTRA), :] = extra[...]


def coarse_kernel(mine, other, factor, factor4, ge_ref, ends, sibling, e0, e1, exl, exh, eyl, eyh, eprev, rhs, g_ref,
                  out0, out1, x_low, x_high, y_low, y_high, r, e, err3, now2, before2, sum2, sum2_before, fixed2):
    sx, sy, tm = lax.axis_index("sx"), lax.axis_index("sy"), lax.axis_index("tm")
    core = tm % 2
    has_xl, has_xh = inside(sx > 0), inside(sx < 3)
    has_yl, has_yh = inside(sy > 0), inside(sy < 3)
    has_prev = inside(tm > 0)
    nothing = jnp.zeros((8, BZ), f32)

    def fill(c, low, high):
        for m in range(COARSE):
            base = m * SHARE
            for x in range(EX):
                r[m, x, pl.ds(BY, 8), :] = nothing
            for j in range(WIDE):
                r[m, j, pl.ds(0, BY), :] = low[pl.ds(base + XH + j * BY, BY), :]
                r[m, BX + WIDE + j, pl.ds(0, BY), :] = high[pl.ds(base + XH + j * BY, BY), :]
            for x in range(BX):
                source = (low, high)[x // (BX // 2)]
                r[m, x + WIDE, pl.ds(0, BY), :] = source[pl.ds(base + x % (BX // 2) * BY, BY), :]
                r[m, x + WIDE, pl.ds(BY, WIDE), :] = high[pl.ds(base + YH + x * WIDE, WIDE), :]
                r[m, x + WIDE, pl.ds(EY - WIDE, WIDE), :] = low[pl.ds(base + YH + x * WIDE, WIDE), :]
            for i, (dx, dy) in enumerate(((1, 1), (1, 2), (2, 1))):
                below, above = WIDE - dx, BX + WIDE - 1 + dx
                r[m, below, pl.ds(EY - dy, 1), :] = low[pl.ds(base + CH + i, 1), :]
                r[m, below, pl.ds(BY - 1 + dy, 1), :] = low[pl.ds(base + CH + 3 + i, 1), :]
                r[m, above, pl.ds(BY - 1 + dy, 1), :] = high[pl.ds(base + CH + i, 1), :]
                r[m, above, pl.ds(EY - dy, 1), :] = high[pl.ds(base + CH + 3 + i, 1), :]
        xs, ys, cs = ALL, ALL + SIDE, ALL + 2 * SIDE
        for x in range(BX + 4):
            now2[x, pl.ds(BY, 8), :] = nothing
        for x in range(BX + 2):
            before2[x, pl.ds(BY, 8), :] = nothing
        mine_at = c * 2
        for j in range(2):
            now2[j, pl.ds(0, BY), :] = low[pl.ds(xs + (mine_at + j) * BY, BY), :] * has_xl
            now2[BX + 2 + j, pl.ds(0, BY), :] = high[pl.ds(xs + (mine_at + j) * BY, BY), :] * has_xh
        for x in range(BX):
            now2[x + 2, pl.ds(0, BY), :] = ends[1, x]
            now2[x + 2, pl.ds(BY, 2), :] = high[pl.ds(ys + mine_at * BX + 2 * x, 2), :] * has_yh
            now2[x + 2, pl.ds(EY - 2, 2), :] = low[pl.ds(ys + mine_at * BX + 2 * x, 2), :] * has_yl
        now2[1, pl.ds(EY - 1, 1), :] = low[pl.ds(cs + c, 1), :] * (has_xl * has_yl)
        now2[1, pl.ds(BY, 1), :] = low[pl.ds(cs + 2 + c, 1), :] * (has_xl * has_yh)
        now2[BX + 2, pl.ds(BY, 1), :] = high[pl.ds(cs + c, 1), :] * (has_xh * has_yh)
        now2[BX + 2, pl.ds(EY - 1, 1), :] = high[pl.ds(cs + 2 + c, 1), :] * (has_xh * has_yl)
        at_low, at_high, y_at, step = (4, 4, 4 * BX, 1) if c == 0 else (1, 0, 0, 2)
        before2[0, pl.ds(0, BY), :] = low[pl.ds(xs + at_low * BY, BY), :] * has_xl
        before2[BX + 1, pl.ds(0, BY), :] = high[pl.ds(xs + at_high * BY, BY), :] * has_xh
        for x in range(BX):
            before2[x + 1, pl.ds(0, BY), :] = sibling[2 - c, x]
            before2[x + 1, pl.ds(BY, 1), :] = high[pl.ds(ys + y_at + step * x, 1), :] * has_yh
            before2[x + 1, pl.ds(EY - 1, 1), :] = low[pl.ds(ys + y_at + step * x + step - 1, 1), :] * has_yl

    pl.when(core == 0)(lambda: fill(0, mine, other))
    pl.when(core == 1)(lambda: fill(1, other, mine))

    def sweep_one(x, carry):
        w = factor[x]
        running = jnp.zeros((EY, BZ), f32)
        for m in range(COARSE):
            running = w * (r[m, x] + running)
            e[m, x] = running
        return carry

    for x in range(EX):
        sweep_one(x, 0)

    def sweep_two(x, carry):
        w = factor[x + 1]
        g = [ge_ref[i, x] for i in range(6)]
        running = jnp.zeros((EY, BZ), f32)
        err3[0, x] = running
        for m in range(COARSE):
            value = e[m, x + 1]
            near = beside(value, e[m, x], e[m, x + 2], pltpu.roll(value, 1, 0), pltpu.roll(value, EY - 1, 0), g)
            running = keep * value + w * (r[m, x + 1] + 8.0 * near) + w * running
            err3[m + 1, x] = running
        return carry

    lax.fori_loop(0, BX + 4, sweep_two, 0, unroll=2)

    row = row_index()
    now, before, earliest = tm // 2 + 1, (tm + 1) // 2, tm // 2

    def turned(value):
        return pltpu.roll(value, 1, 0), pltpu.roll(value, EY - 1, 0)

    for x in range(BX + 4):
        sum2[x] = now2[x] + err3[now, x]
    for x in range(BX + 2):
        sum2_before[x] = before2[x] + err3[before, x + 1]
    for x in range(BX + 2):
        value = sum2[x + 1]
        near = beside(value, sum2[x], sum2[x + 2], *turned(value), [ge_ref[i, x + 1] for i in range(6)])
        fixed2[x] = keep * value + now2[x + 1] + factor4[x] * (4.0 * near + sum2_before[x])
    for x in range(BX):
        value = sum2_before[x + 1]
        near = beside(value, sum2_before[x], sum2_before[x + 2], *turned(value), [ge_ref[i, x + 2] for i in range(6)])
        two_before = ends[2, x] + err3[earliest, x + 2, pl.ds(0, BY), :]
        fixed_before = (keep * value + before2[x + 1] + factor4[x + 1] * (4.0 * near))[0:BY]
        fixed_before = fixed_before + factor4[x + 1, pl.ds(0, BY), :] * two_before
        g, coupling = row_coefficients(g_ref, x)
        weight = relax / (1.0 + 2.0 * coupling)
        running = (eprev[x] + fixed_before) * has_prev
        here = fixed2[x + 1]
        f_below, f_above = fixed2[x, pl.ds(0, BY), :], fixed2[x + 2, pl.ds(0, BY), :]
        for n, (err, out) in enumerate(((e0, out0), (e1, out1))):
            value = err[x] + here[0:BY]
            below = (err[x - 1] if x > 0 else exl[n]) + f_below
            above = (err[x + 1] if x < BX - 1 else exh[n]) + f_above
            low = eyl[n, pl.ds(x, 1), :] + here[EY - 1 : EY]
            high = eyh[n, pl.ds(x, 1), :] + here[BY : BY + 1]
            near = 2.0 * beside(value, below, above, *y_sides(value, low, high, row), g)
            running = keep * value + weight * (rhs[n, x] + near + running)
            out[x] = running
            put_edges((x_low, x_high, y_low, y_high), n, x, running)


def solution_kernel(fix0, fix1, fxl, fxh, fyl, fyh, fprev, first, exl, exh, yl, yh, eprev, h, g_ref,
                    out, x_low, x_high, y_low, y_high, last):
    has_prev = inside(lax.axis_index("tm") > 0)
    row = row_index()
    for x in range(BX):
        g, coupling = row_coefficients(g_ref, x)
        factor = relax / (1.0 + coupling)
        running = (eprev[x] + fprev[x]) * has_prev
        for n in range(STEPS):
            fix, c = (fix0, fix1)[n // 2], n // 2
            value = first[n, x] + fix[x]
            below = (first[n, x - 1] + fix[x - 1]) if x > 0 else (exl[n] + fxl[c])
            above = (first[n, x + 1] + fix[x + 1]) if x < BX - 1 else (exh[n] + fxh[c])
            at = pl.ds(n * BX + x, 1)
            low = yl[at, :] + fyl[c, pl.ds(x, 1), :]
            high = yh[at, :] + fyh[c, pl.ds(x, 1), :]
            sides = y_sides(value, low, high, row)
            running = keep * value + factor * (h[n, x] + beside(value, below, above, *sides, g) + running)
            out[n, x] = running
            put_edges((x_low, x_high, y_low, y_high), n, x, running)
        last[x] = running


def copy_kernel(source, target):
    target[...] = source[...]


def residual_kernel(sol, h, g_ref, hxl, hxh, hyl, hyh, prev, out):
    has_prev = inside(lax.axis_index("tm") > 0)
    row = row_index()
    for x in range(BX):
        g, coupling = row_coefficients(g_ref, x)
        diagonal = 1.0 + coupling
        earlier = prev[x] * has_prev
        for n in range(STEPS):
            value = sol[n, x]
            below = sol[n, x - 1] if x > 0 else hxl[n]
            above = sol[n, x + 1] if x < BX - 1 else hxh[n]
            sides = y_sides(value, hyl[n, pl.ds(x, 1), :], hyh[n, pl.ds(x, 1), :], row)
            out[n, x] = h[n, x] + earlier - diagonal * value + beside(value, below, above, *sides, g)
            earlier = value


def gather_steps(own):
    def along(value, s):
        return across_tm(value, lambda i: (i & 9) | ((i + 2 * s) & 6))

    far = across_tm(own, lambda i: i ^ 8)
    near = [own] + [along(own, s) for s in (1, 2, 3)]
    return near + [far] + [along(far, s) for s in (1, 2, 3)]


def per_device(h, k, u):
    fine, two = (STEPS, *FIELD), (2, *FIELD)
    ypack = (YROWS, BZ)
    *edges, last = call(first_edges_kernel, [(STEPS + KW, *EDGE)] * 2 + [(STEPS + 1, *EDGE)] * 2 + [FIELD], u, k)
    (h,) = call(copy_kernel, [fine], h)
    halo, prev = exchange(edges, last)
    g, first, *edges, last, kx = call(
        first_kernel,
        [(7, *FIELD), fine, (STEPS, *EDGE), (STEPS, *EDGE), ypack, ypack, FIELD, (KX, BY, BZ)],
        u, h, k, *halo, prev,
    )
    first_halo, first_prev = exchange(edges, last)
    factor, factor4, g_coarse = call(
        coarse_terms_kernel,
        [(EX, EY, BZ), (BX + 2, EY, BZ), (6, BX + 4, EY, BZ)],
        kx, *first_halo[2:],
        scratch=[(KX, EY, BZ)],
    )
    rhs1, e0, e1, *edges = call(
        defect_fine_kernel, [two, FIELD, FIELD] + edge_shapes(2), first, h, g, *first_halo, first_prev
    )
    err1_halo, err1_prev = exchange(edges, e1)
    rhs2, err2, *edges = call(
        defect_mid_kernel, [FIELD, FIELD] + edge_shapes(1), e0, e1, rhs1, g, *err1_halo, err1_prev
    )
    err2_halo, chip_before = exchange(edges, err2, 2)
    (ends,) = call(defect_last_kernel, [(3, *FIELD)], err2, rhs2, g, *err2_halo, chip_before)
    sibling = across_tm(ends, lambda i: i ^ 1)
    half, x_edge, y_edge, corner_a, corner_b = call(
        coarse_edges_kernel,
        [(HALF, BZ), (WIDE * BY + SIDE, BZ), (WIDE * BX + SIDE, BZ), (8, BZ), (8, BZ)],
        ends, sibling,
        scratch=[FIELD],
    )
    share, extra = call(
        share_kernel,
        [(SHARE, BZ), (EXTRA, BZ)],
        half, crossed(x_edge, 1, 0), crossed(y_edge, 0, 1), crossed(corner_a, 1, 1), crossed(corner_b, 1, -1),
    )
    (mine,) = call(order_kernel, [(ALL + EXTRA, BZ)], *gather_steps(share), extra)
    other = across_tm(mine, lambda i: i ^ 1)
    fixed1a, fixed1b, *edges = call(
        coarse_kernel,
        [FIELD, FIELD] + edge_shapes(2),
        mine, other, factor, factor4, g_coarse, ends, sibling,
        e0, e1, *err1_halo, err1_prev, rhs1, g,
        scratch=[
            (COARSE, EX, EY, BZ), (COARSE, EX, EY, BZ), (COARSE + 1, BX + 4, EY, BZ),
            (BX + 4, EY, BZ), (BX + 2, EY, BZ), (BX + 4, EY, BZ), (BX + 2, EY, BZ), (BX + 2, EY, BZ),
        ],
    )
    fixed1_halo, fixed1_prev = exchange(edges, fixed1b)
    last_iterate, *edges, last = call(
        solution_kernel,
        [fine] + edge_shapes(STEPS) + [FIELD],
        fixed1a, fixed1b, *fixed1_halo, fixed1_prev, first, *first_halo, first_prev, h, g,
    )
    out_halo, out_prev = exchange(edges, last)
    (out,) = call(copy_kernel, [fine], last_iterate)
    (residual,) = call(residual_kernel, [fine], last_iterate, h, g, *out_halo, out_prev)
    return out, residual


def solution(mesh):
    placed = (P("tm", "sx", "sy", None), P("sx", "sy", None), P("tm", "sx", "sy", None))
    return jax.shard_map(
        per_device,
        mesh=mesh,
        in_specs=placed,
        out_specs=(P("tm", "sx", "sy", None), P("tm", "sx", "sy", None)),
        check_vma=False,
    )
```

```python
import jax
import jax.numpy as jnp
from jax import lax
from jax.experimental import pallas as pl
from jax.experimental.pallas import tpu as pltpu
from jax.sharding import PartitionSpec as P

relax = 0.8
keep = 1.0 - relax
STEPS, BX, BY, BZ = 4, 16, 16, 128
COARSE = 8
WIDE = 3
KW = WIDE + 1
EX, EY = BX + 2 * WIDE, BY + 2 * KW
KX = BX + 2 * KW
f32 = jnp.float32
FIELD = (BX, BY, BZ)
EDGE = (BX, BZ)
YROWS = STEPS * BX + KW * KX


def turn(value, axis, by):
    devices = lax.axis_size(axis)
    return lax.ppermute(value, axis, [(i, (i + by) % devices) for i in range(devices)])


def across_tm(value, where):
    return lax.ppermute(value, "tm", [(i, where(i)) for i in range(16)])


def crossed(value, by_x, by_y):
    pairs = []
    for t in range(16):
        sign = 1 if t % 2 else -1
        for i in range(4):
            for j in range(4):
                to = ((t ^ 1) * 4 + (i + sign * by_x) % 4) * 4 + (j + sign * by_y) % 4
                pairs.append(((t * 4 + i) * 4 + j, to))
    return lax.ppermute(value, ("tm", "sx", "sy"), pairs)


def exchange(edges, last, steps=1):
    x_low, x_high, y_low, y_high = edges
    earlier = turn(last, "tm", steps)
    return (
        turn(x_high, "sx", 1),
        turn(x_low, "sx", -1),
        turn(y_high, "sy", 1),
        turn(y_low, "sy", -1),
    ), earlier


def call(kernel, outs, *args, scratch=()):
    vmem = pl.BlockSpec(memory_space=pltpu.VMEM)
    return pl.pallas_call(
        kernel,
        out_shape=[jax.ShapeDtypeStruct(s, f32) for s in outs],
        in_specs=[vmem] * len(args),
        out_specs=[vmem] * len(outs),
        scratch_shapes=[pltpu.VMEM(s, f32) for s in scratch],
        compiler_params=pltpu.CompilerParams(vmem_limit_bytes=40 * 2**20),
    )(*args)


def inside(condition):
    return jnp.where(condition, f32(1.0), f32(0.0))


def row_index(rows=BY):
    return lax.broadcasted_iota(jnp.int32, (rows, BZ), 0)


def lane_index(rows=BY):
    return lax.broadcasted_iota(jnp.int32, (rows, BZ), 1)


def y_sides(value, low, high, row):
    below = jnp.where(row == 0, low, pltpu.roll(value, 1, 0))
    above = jnp.where(row == BY - 1, high, pltpu.roll(value, BY - 1, 0))
    return below, above


def beside(value, x_below, x_above, y_below, y_above, g):
    total = g[0] * x_below + g[1] * x_above
    total = total + g[2] * y_below + g[3] * y_above
    return total + g[4] * pltpu.roll(value, 1, 1) + g[5] * pltpu.roll(value, BZ - 1, 1)


def row_coefficients(g_ref, x):
    return [g_ref[i, x] for i in range(6)], g_ref[6, x]


def put_edges(refs, n, x, value):
    x_low, x_high, y_low, y_high = refs
    if x == 0:
        x_low[n] = value
    if x == BX - 1:
        x_high[n] = value
    y_low[n, pl.ds(x, 1), :] = value[0:1]
    y_high[n, pl.ds(x, 1), :] = value[BY - 1 : BY]


def edge_shapes(n):
    return [(n, *EDGE)] * 4


def last_step_kernel(u, last):
    last[...] = u[STEPS - 1]


def first_edges_kernel(u, k, x_low, x_high, y_low, y_high):
    for n in range(STEPS):
        x_low[n] = u[n, 0]
        x_high[n] = u[n, BX - 1]
    for j in range(KW):
        x_low[STEPS + j] = k[j]
        x_high[STEPS + j] = k[BX - KW + j]
    for n in range(STEPS + 1):
        for x in range(BX):
            row = u[n, x] if n < STEPS else k[x]
            y_low[n, pl.ds(x, 1), :] = row[0:1]
            y_high[n, pl.ds(x, 1), :] = row[BY - 1 : BY]


def first_kernel(u, h, k, hxl, hxh, hyl, hyh, prev, g_out, first, x_low, x_high, y_low, y_high, last, kx):
    sx, sy, tm = lax.axis_index("sx"), lax.axis_index("sy"), lax.axis_index("tm")
    has_xl, has_xh = inside(sx > 0), inside(sx < 3)
    has_yl, has_yh = inside(sy > 0), inside(sy < 3)
    has_prev = inside(tm > 0)
    row, lane = row_index(), lane_index()
    for j in range(KW):
        kx[j] = hxl[STEPS + j] * has_xl
        kx[KW + BX + j] = hxh[STEPS + j] * has_xh
    for x in range(BX):
        kx[KW + x] = k[x]
    for x in range(BX):
        kc = k[x]
        k_yl = hyl[STEPS, pl.ds(x, 1), :] * has_yl
        k_yh = hyh[STEPS, pl.ds(x, 1), :] * has_yh
        k_below, k_above = y_sides(kc, k_yl, k_yh, row)
        z_below = jnp.where(lane == 0, 0.0, pltpu.roll(kc, 1, 1))
        z_above = jnp.where(lane == BZ - 1, 0.0, pltpu.roll(kc, BZ - 1, 1))
        g = [0.5 * (kc + other) for other in (kx[KW - 1 + x], kx[KW + 1 + x], k_below, k_above, z_below, z_above)]
        coupling = g[0] + g[1] + g[2] + g[3] + g[4] + g[5]
        if x == 0:
            g[0] = g[0] * has_xl
        if x == BX - 1:
            g[1] = g[1] * has_xh
        g[2] = jnp.where(row == 0, g[2] * has_yl, g[2])
        g[3] = jnp.where(row == BY - 1, g[3] * has_yh, g[3])
        g[4] = jnp.where(lane == 0, 0.0, g[4])
        g[5] = jnp.where(lane == BZ - 1, 0.0, g[5])
        for i in range(6):
            g_out[i, x] = g[i]
        g_out[6, x] = coupling
        factor = relax / (1.0 + coupling)
        running = prev[x] * has_prev
        for n in range(STEPS):
            value = u[n, x]
            below = u[n, x - 1] if x > 0 else hxl[n]
            above = u[n, x + 1] if x < BX - 1 else hxh[n]
            sides = y_sides(value, hyl[n, pl.ds(x, 1), :], hyh[n, pl.ds(x, 1), :], row)
            running = keep * value + factor * (h[n, x] + beside(value, below, above, *sides, g) + running)
            first[n, x] = running
            if x == 0:
                x_low[n] = running
            if x == BX - 1:
                x_high[n] = running
            y_low[pl.ds(n * BX + x, 1), :] = running[0:1]
            y_high[pl.ds(n * BX + x, 1), :] = running[BY - 1 : BY]
        last[x] = running
    for x in range(KX):
        kc = kx[x]
        for j in range(KW):
            at = STEPS * BX + j * KX + x
            y_low[pl.ds(at, 1), :] = kc[j : j + 1]
            y_high[pl.ds(at, 1), :] = kc[BY - KW + j : BY - KW + j + 1]


def coarse_terms_kernel(kx, yl, yh, factor, factor4, g_out, ke):
    sx, sy = lax.axis_index("sx"), lax.axis_index("sy")
    has_yl, has_yh = inside(sy > 0), inside(sy < 3)
    row, lane = row_index(EY), lane_index(EY)
    for x in range(KX):
        ke[x, pl.ds(0, BY), :] = kx[x]
        for j in range(KW):
            at = STEPS * BX + j * KX + x
            ke[x, pl.ds(BY + j, 1), :] = yh[pl.ds(at, 1), :] * has_yh
            ke[x, pl.ds(EY - KW + j, 1), :] = yl[pl.ds(at, 1), :] * has_yl
    y_in = jnp.where(row < BY, 1.0, jnp.where(row < BY + KW, has_yh, has_yl))
    for x in range(EX):
        kc = ke[x + 1]
        others = (
            ke[x],
            ke[x + 2],
            pltpu.roll(kc, 1, 0),
            pltpu.roll(kc, EY - 1, 0),
            jnp.where(lane == 0, 0.0, pltpu.roll(kc, 1, 1)),
            jnp.where(lane == BZ - 1, 0.0, pltpu.roll(kc, BZ - 1, 1)),
        )
        g = [0.5 * (kc + other) for other in others]
        coupling = g[0] + g[1] + g[2] + g[3] + g[4] + g[5]
        x_in = inside(sx > 0) if x < WIDE else inside(sx < 3) if x >= BX + WIDE else f32(1.0)
        factor[x] = (relax / (1.0 + 8.0 * coupling)) * (y_in * x_in)
        if 2 <= x <= EX - 3:
            factor4[x - 2] = (relax / (1.0 + 4.0 * coupling)) * (y_in * x_in)
        if 1 <= x <= EX - 2:
            g[4] = jnp.where(lane == 0, 0.0, g[4])
            g[5] = jnp.where(lane == BZ - 1, 0.0, g[5])
            for i in range(6):
                g_out[i, x - 1] = g[i]


def defect_fine_kernel(first, h, g_ref, hxl, hxh, yl, yh, prev, rhs, e0, e1, x_low, x_high, y_low, y_high):
    has_prev = inside(lax.axis_index("tm") > 0)
    row = row_index()
    for x in range(BX):
        g, coupling = row_coefficients(g_ref, x)
        diagonal = 1.0 + coupling
        factor = relax / (1.0 + 2.0 * coupling)
        earlier = prev[x] * has_prev
        parts = []
        for n in range(STEPS):
            value = first[n, x]
            below = first[n, x - 1] if x > 0 else hxl[n]
            above = first[n, x + 1] if x < BX - 1 else hxh[n]
            at = pl.ds(n * BX + x, 1)
            sides = y_sides(value, yl[at, :], yh[at, :], row)
            parts.append(h[n, x] + earlier - diagonal * value + beside(value, below, above, *sides, g))
            earlier = value
        r0, r1 = parts[0] + parts[1], parts[2] + parts[3]
        rhs[0, x] = r0
        rhs[1, x] = r1
        v0 = factor * r0
        v1 = factor * (r1 + v0)
        e0[x] = v0
        e1[x] = v1
        put_edges((x_low, x_high, y_low, y_high), 0, x, v0)
        put_edges((x_low, x_high, y_low, y_high), 1, x, v1)


def defect_mid_kernel(e0, e1, rhs, g_ref, hxl, hxh, hyl, hyh, prev, rhs2, err2, x_low, x_high, y_low, y_high):
    has_prev = inside(lax.axis_index("tm") > 0)
    row = row_index()
    for x in range(BX):
        g, coupling = row_coefficients(g_ref, x)
        diagonal = 1.0 + 2.0 * coupling
        earlier = prev[x] * has_prev
        total = None
        for n, e in enumerate((e0, e1)):
            value = e[x]
            below = e[x - 1] if x > 0 else hxl[n]
            above = e[x + 1] if x < BX - 1 else hxh[n]
            sides = y_sides(value, hyl[n, pl.ds(x, 1), :], hyh[n, pl.ds(x, 1), :], row)
            part = rhs[n, x] + earlier - diagonal * value + 2.0 * beside(value, below, above, *sides, g)
            total = part if total is None else total + part
            earlier = value
        rhs2[x] = total
        value = relax / (1.0 + 4.0 * coupling) * total
        err2[x] = value
        put_edges((x_low, x_high, y_low, y_high), 0, x, value)


def defect_last_kernel(err2, rhs2, g_ref, hxl, hxh, hyl, hyh, chip_before, out):
    has_chip = inside(lax.axis_index("tm") > 1)
    row = row_index()
    for x in range(BX):
        g, coupling = row_coefficients(g_ref, x)
        value = err2[x]
        below = err2[x - 1] if x > 0 else hxl[0]
        above = err2[x + 1] if x < BX - 1 else hxh[0]
        sides = y_sides(value, hyl[0, pl.ds(x, 1), :], hyh[0, pl.ds(x, 1), :], row)
        near = 4.0 * beside(value, below, above, *sides, g)
        out[0, x] = rhs2[x] - (1.0 + 4.0 * coupling) * value + near
        out[1, x] = value
        out[2, x] = chip_before[x] * has_chip


HALF = BX // 2 * BY
XH, YH, CH = HALF, HALF + WIDE * BY, HALF + WIDE * (BY + BX)
SHARE = CH + 8
SIDE = 5 * BY
EXTRA = 2 * SIDE + 8
ALL = COARSE * SHARE


def coarse_edges_kernel(own, other, half, x_edge, y_edge, corner_a, corner_b, rhs3):
    core = lax.axis_index("tm") % 2

    def send(c):
        zero, one = (own, other) if c == 0 else (other, own)
        for x in range(BX):
            rhs3[x] = zero[0, x] + one[0, x] + (zero[1, x] + one[2, x])
        fields = ((rhs3, WIDE), (zero.at[1], 2), (one.at[1], 2), (one.at[2], 1))
        for i in range(BX // 2):
            half[pl.ds(i * BY, BY), :] = rhs3[c * (BX // 2) + i]
        at = 0
        for field, width in fields:
            for j in range(width):
                x_edge[pl.ds((at + j) * BY, BY), :] = field[c * (BX - width) + j]
            for x in range(BX):
                y_edge[pl.ds(at * BX + x * width, width), :] = field[x, pl.ds(c * (BY - width), width), :]
            at += width
        near, then = c * (BX - 1), c * (BX - 3) + 1
        for corner, flip in ((corner_a, False), (corner_b, True)):
            near_y, then_y = (BY - 1 - near, BY - 1 - then) if flip else (near, then)
            corner[...] = jnp.zeros((8, BZ), f32)
            cells = ((rhs3, near, near_y), (rhs3, near, then_y), (rhs3, then, near_y),
                     (zero.at[1], near, near_y), (one.at[1], near, near_y))
            for i, (field, x, y) in enumerate(cells):
                corner[pl.ds(i, 1), :] = field[x, pl.ds(y, 1), :]

    pl.when(core == 1)(lambda: send(1))
    pl.when(core == 0)(lambda: send(0))


def share_kernel(half, x_edge, y_edge, corner_a, corner_b, share, extra):
    share[pl.ds(0, HALF), :] = half[...]
    share[pl.ds(XH, WIDE * BY), :] = x_edge[pl.ds(0, WIDE * BY), :]
    share[pl.ds(YH, WIDE * BX), :] = y_edge[pl.ds(0, WIDE * BX), :]
    share[pl.ds(CH, 8), :] = corner_a[...]
    share[pl.ds(CH + 3, 3), :] = corner_b[pl.ds(0, 3), :]
    extra[pl.ds(0, SIDE), :] = x_edge[pl.ds(WIDE * BY, SIDE), :]
    extra[pl.ds(SIDE, SIDE), :] = y_edge[pl.ds(WIDE * BX, SIDE), :]
    extra[pl.ds(2 * SIDE, 8), :] = corner_a[...]
    extra[pl.ds(2 * SIDE, 2), :] = corner_a[pl.ds(3, 2), :]
    extra[pl.ds(2 * SIDE + 2, 2), :] = corner_b[pl.ds(3, 2), :]


def order_kernel(*refs):
    parts, extra, out = refs[:8], refs[8], refs[9]
    tm = lax.axis_index("tm")
    ring, half = (tm // 2) % 4, tm // 8
    for far in range(2):
        for s in range(4):
            step = (half + far) % 2 * 4 + (ring + 4 - s) % 4
            out[pl.ds(pl.multiple_of(step * SHARE, 8), SHARE), :] = parts[far * 4 + s][...]
    out[pl.ds(ALL, EXTRA), :] = extra[...]


def coarse_kernel(mine, other, factor, factor4, ge_ref, ends, sibling, e0, e1, exl, exh, eyl, eyh, eprev, rhs, g_ref,
                  out0, out1, x_low, x_high, y_low, y_high, r, e, err3, now2, before2, sum2, sum2_before, fixed2):
    sx, sy, tm = lax.axis_index("sx"), lax.axis_index("sy"), lax.axis_index("tm")
    core = tm % 2
    has_xl, has_xh = inside(sx > 0), inside(sx < 3)
    has_yl, has_yh = inside(sy > 0), inside(sy < 3)
    has_prev = inside(tm > 0)
    nothing = jnp.zeros((8, BZ), f32)

    def fill(c, low, high):
        for m in range(COARSE):
            base = m * SHARE
            for x in range(EX):
                r[m, x, pl.ds(BY, 8), :] = nothing
            for j in range(WIDE):
                r[m, j, pl.ds(0, BY), :] = low[pl.ds(base + XH + j * BY, BY), :]
                r[m, BX + WIDE + j, pl.ds(0, BY), :] = high[pl.ds(base + XH + j * BY, BY), :]
            for x in range(BX):
                source = (low, high)[x // (BX // 2)]
                r[m, x + WIDE, pl.ds(0, BY), :] = source[pl.ds(base + x % (BX // 2) * BY, BY), :]
                r[m, x + WIDE, pl.ds(BY, WIDE), :] = high[pl.ds(base + YH + x * WIDE, WIDE), :]
                r[m, x + WIDE, pl.ds(EY - WIDE, WIDE), :] = low[pl.ds(base + YH + x * WIDE, WIDE), :]
            for i, (dx, dy) in enumerate(((1, 1), (1, 2), (2, 1))):
                below, above = WIDE - dx, BX + WIDE - 1 + dx
                r[m, below, pl.ds(EY - dy, 1), :] = low[pl.ds(base + CH + i, 1), :]
                r[m, below, pl.ds(BY - 1 + dy, 1), :] = low[pl.ds(base + CH + 3 + i, 1), :]
                r[m, above, pl.ds(BY - 1 + dy, 1), :] = high[pl.ds(base + CH + i, 1), :]
                r[m, above, pl.ds(EY - dy, 1), :] = high[pl.ds(base + CH + 3 + i, 1), :]
        xs, ys, cs = ALL, ALL + SIDE, ALL + 2 * SIDE
        for x in range(BX + 4):
            now2[x, pl.ds(BY, 8), :] = nothing
        for x in range(BX + 2):
            before2[x, pl.ds(BY, 8), :] = nothing
        mine_at = c * 2
        for j in range(2):
            now2[j, pl.ds(0, BY), :] = low[pl.ds(xs + (mine_at + j) * BY, BY), :] * has_xl
            now2[BX + 2 + j, pl.ds(0, BY), :] = high[pl.ds(xs + (mine_at + j) * BY, BY), :] * has_xh
        for x in range(BX):
            now2[x + 2, pl.ds(0, BY), :] = ends[1, x]
            now2[x + 2, pl.ds(BY, 2), :] = high[pl.ds(ys + mine_at * BX + 2 * x, 2), :] * has_yh
            now2[x + 2, pl.ds(EY - 2, 2), :] = low[pl.ds(ys + mine_at * BX + 2 * x, 2), :] * has_yl
        now2[1, pl.ds(EY - 1, 1), :] = low[pl.ds(cs + c, 1), :] * (has_xl * has_yl)
        now2[1, pl.ds(BY, 1), :] = low[pl.ds(cs + 2 + c, 1), :] * (has_xl * has_yh)
        now2[BX + 2, pl.ds(BY, 1), :] = high[pl.ds(cs + c, 1), :] * (has_xh * has_yh)
        now2[BX + 2, pl.ds(EY - 1, 1), :] = high[pl.ds(cs + 2 + c, 1), :] * (has_xh * has_yl)
        at_low, at_high, y_at, step = (4, 4, 4 * BX, 1) if c == 0 else (1, 0, 0, 2)
        before2[0, pl.ds(0, BY), :] = low[pl.ds(xs + at_low * BY, BY), :] * has_xl
        before2[BX + 1, pl.ds(0, BY), :] = high[pl.ds(xs + at_high * BY, BY), :] * has_xh
        for x in range(BX):
            before2[x + 1, pl.ds(0, BY), :] = sibling[2 - c, x]
            before2[x + 1, pl.ds(BY, 1), :] = high[pl.ds(ys + y_at + step * x, 1), :] * has_yh
            before2[x + 1, pl.ds(EY - 1, 1), :] = low[pl.ds(ys + y_at + step * x + step - 1, 1), :] * has_yl

    pl.when(core == 0)(lambda: fill(0, mine, other))
    pl.when(core == 1)(lambda: fill(1, other, mine))

    def sweep_one(x, carry):
        w = factor[x]
        running = jnp.zeros((EY, BZ), f32)
        for m in range(COARSE):
            running = w * (r[m, x] + running)
            e[m, x] = running
        return carry

    for x in range(EX):
        sweep_one(x, 0)

    def sweep_two(x, carry):
        w = factor[x + 1]
        g = [ge_ref[i, x] for i in range(6)]
        running = jnp.zeros((EY, BZ), f32)
        err3[0, x] = running
        for m in range(COARSE):
            value = e[m, x + 1]
            near = beside(value, e[m, x], e[m, x + 2], pltpu.roll(value, 1, 0), pltpu.roll(value, EY - 1, 0), g)
            running = keep * value + w * (r[m, x + 1] + 8.0 * near) + w * running
            err3[m + 1, x] = running
        return carry

    lax.fori_loop(0, BX + 4, sweep_two, 0, unroll=2)

    row = row_index()
    now, before, earliest = tm // 2 + 1, (tm + 1) // 2, tm // 2

    def turned(value):
        return pltpu.roll(value, 1, 0), pltpu.roll(value, EY - 1, 0)

    for x in range(BX + 4):
        sum2[x] = now2[x] + err3[now, x]
    for x in range(BX + 2):
        sum2_before[x] = before2[x] + err3[before, x + 1]
    for x in range(BX + 2):
        value = sum2[x + 1]
        near = beside(value, sum2[x], sum2[x + 2], *turned(value), [ge_ref[i, x + 1] for i in range(6)])
        fixed2[x] = keep * value + now2[x + 1] + factor4[x] * (4.0 * near + sum2_before[x])
    for x in range(BX):
        value = sum2_before[x + 1]
        near = beside(value, sum2_before[x], sum2_before[x + 2], *turned(value), [ge_ref[i, x + 2] for i in range(6)])
        two_before = ends[2, x] + err3[earliest, x + 2, pl.ds(0, BY), :]
        fixed_before = (keep * value + before2[x + 1] + factor4[x + 1] * (4.0 * near))[0:BY]
        fixed_before = fixed_before + factor4[x + 1, pl.ds(0, BY), :] * two_before
        g, coupling = row_coefficients(g_ref, x)
        weight = relax / (1.0 + 2.0 * coupling)
        running = (eprev[x] + fixed_before) * has_prev
        here = fixed2[x + 1]
        f_below, f_above = fixed2[x, pl.ds(0, BY), :], fixed2[x + 2, pl.ds(0, BY), :]
        for n, (err, out) in enumerate(((e0, out0), (e1, out1))):
            value = err[x] + here[0:BY]
            below = (err[x - 1] if x > 0 else exl[n]) + f_below
            above = (err[x + 1] if x < BX - 1 else exh[n]) + f_above
            low = eyl[n, pl.ds(x, 1), :] + here[EY - 1 : EY]
            high = eyh[n, pl.ds(x, 1), :] + here[BY : BY + 1]
            near = 2.0 * beside(value, below, above, *y_sides(value, low, high, row), g)
            running = keep * value + weight * (rhs[n, x] + near + running)
            out[x] = running
            put_edges((x_low, x_high, y_low, y_high), n, x, running)


def solution_kernel(fix0, fix1, fxl, fxh, fyl, fyh, fprev, first, exl, exh, yl, yh, eprev, h, g_ref,
                    out, x_low, x_high, y_low, y_high, last):
    has_prev = inside(lax.axis_index("tm") > 0)
    row = row_index()
    for x in range(BX):
        g, coupling = row_coefficients(g_ref, x)
        factor = relax / (1.0 + coupling)
        running = (eprev[x] + fprev[x]) * has_prev
        for n in range(STEPS):
            fix, c = (fix0, fix1)[n // 2], n // 2
            value = first[n, x] + fix[x]
            below = (first[n, x - 1] + fix[x - 1]) if x > 0 else (exl[n] + fxl[c])
            above = (first[n, x + 1] + fix[x + 1]) if x < BX - 1 else (exh[n] + fxh[c])
            at = pl.ds(n * BX + x, 1)
            low = yl[at, :] + fyl[c, pl.ds(x, 1), :]
            high = yh[at, :] + fyh[c, pl.ds(x, 1), :]
            sides = y_sides(value, low, high, row)
            running = keep * value + factor * (h[n, x] + beside(value, below, above, *sides, g) + running)
            out[n, x] = running
            put_edges((x_low, x_high, y_low, y_high), n, x, running)
        last[x] = running


def copy_kernel(source, target):
    target[...] = source[...]


def residual_kernel(sol, h, g_ref, hxl, hxh, hyl, hyh, prev, out):
    has_prev = inside(lax.axis_index("tm") > 0)
    row = row_index()
    for x in range(BX):
        g, coupling = row_coefficients(g_ref, x)
        diagonal = 1.0 + coupling
        earlier = prev[x] * has_prev
        for n in range(STEPS):
            value = sol[n, x]
            below = sol[n, x - 1] if x > 0 else hxl[n]
            above = sol[n, x + 1] if x < BX - 1 else hxh[n]
            sides = y_sides(value, hyl[n, pl.ds(x, 1), :], hyh[n, pl.ds(x, 1), :], row)
            out[n, x] = h[n, x] + earlier - diagonal * value + beside(value, below, above, *sides, g)
            earlier = value


def gather_steps(own):
    def along(value, s):
        return across_tm(value, lambda i: (i & 9) | ((i + 2 * s) & 6))

    far = across_tm(own, lambda i: i ^ 8)
    near = [own] + [along(own, s) for s in (1, 2, 3)]
    return near + [far] + [along(far, s) for s in (1, 2, 3)]


def per_device(h, k, u):
    fine, two = (STEPS, *FIELD), (2, *FIELD)
    ypack = (YROWS, BZ)
    (last,) = call(last_step_kernel, [FIELD], u)
    edges = call(first_edges_kernel, [(STEPS + KW, *EDGE)] * 2 + [(STEPS + 1, *EDGE)] * 2, u, k)
    (h,) = call(copy_kernel, [fine], h)
    halo, prev = exchange(edges, last)
    g, first, *edges, last, kx = call(
        first_kernel,
        [(7, *FIELD), fine, (STEPS, *EDGE), (STEPS, *EDGE), ypack, ypack, FIELD, (KX, BY, BZ)],
        u, h, k, *halo, prev,
    )
    first_halo, first_prev = exchange(edges, last)
    factor, factor4, g_coarse = call(
        coarse_terms_kernel,
        [(EX, EY, BZ), (BX + 2, EY, BZ), (6, BX + 4, EY, BZ)],
        kx, *first_halo[2:],
        scratch=[(KX, EY, BZ)],
    )
    rhs1, e0, e1, *edges = call(
        defect_fine_kernel, [two, FIELD, FIELD] + edge_shapes(2), first, h, g, *first_halo, first_prev
    )
    err1_halo, err1_prev = exchange(edges, e1)
    rhs2, err2, *edges = call(
        defect_mid_kernel, [FIELD, FIELD] + edge_shapes(1), e0, e1, rhs1, g, *err1_halo, err1_prev
    )
    err2_halo, chip_before = exchange(edges, err2, 2)
    (ends,) = call(defect_last_kernel, [(3, *FIELD)], err2, rhs2, g, *err2_halo, chip_before)
    sibling = across_tm(ends, lambda i: i ^ 1)
    half, x_edge, y_edge, corner_a, corner_b = call(
        coarse_edges_kernel,
        [(HALF, BZ), (WIDE * BY + SIDE, BZ), (WIDE * BX + SIDE, BZ), (8, BZ), (8, BZ)],
        ends, sibling,
        scratch=[FIELD],
    )
    share, extra = call(
        share_kernel,
        [(SHARE, BZ), (EXTRA, BZ)],
        half, crossed(x_edge, 1, 0), crossed(y_edge, 0, 1), crossed(corner_a, 1, 1), crossed(corner_b, 1, -1),
    )
    (mine,) = call(order_kernel, [(ALL + EXTRA, BZ)], *gather_steps(share), extra)
    other = across_tm(mine, lambda i: i ^ 1)
    fixed1a, fixed1b, *edges = call(
        coarse_kernel,
        [FIELD, FIELD] + edge_shapes(2),
        mine, other, factor, factor4, g_coarse, ends, sibling,
        e0, e1, *err1_halo, err1_prev, rhs1, g,
        scratch=[
            (COARSE, EX, EY, BZ), (COARSE, EX, EY, BZ), (COARSE + 1, BX + 4, EY, BZ),
            (BX + 4, EY, BZ), (BX + 2, EY, BZ), (BX + 4, EY, BZ), (BX + 2, EY, BZ), (BX + 2, EY, BZ),
        ],
    )
    fixed1_halo, fixed1_prev = exchange(edges, fixed1b)
    last_iterate, *edges, last = call(
        solution_kernel,
        [fine] + edge_shapes(STEPS) + [FIELD],
        fixed1a, fixed1b, *fixed1_halo, fixed1_prev, first, *first_halo, first_prev, h, g,
    )
    out_halo, out_prev = exchange(edges, last)
    (out,) = call(copy_kernel, [fine], last_iterate)
    (residual,) = call(residual_kernel, [fine], last_iterate, h, g, *out_halo, out_prev)
    return out, residual


def solution(mesh):
    placed = (P("tm", "sx", "sy", None), P("sx", "sy", None), P("tm", "sx", "sy", None))
    return jax.shard_map(
        per_device,
        mesh=mesh,
        in_specs=placed,
        out_specs=(P("tm", "sx", "sy", None), P("tm", "sx", "sy", None)),
        check_vma=False,
    )
```

```python
import jax
import jax.numpy as jnp
from jax import lax
from jax.experimental import pallas as pl
from jax.experimental.pallas import tpu as pltpu
from jax.sharding import PartitionSpec as P

relax = 0.8
keep = 1.0 - relax
STEPS, BX, BY, BZ = 4, 16, 16, 128
COARSE = 8
WIDE = 3
KW = WIDE + 1
EX, EY = BX + 2 * WIDE, BY + 2 * KW
KX = BX + 2 * KW
f32 = jnp.float32
FIELD = (BX, BY, BZ)
EDGE = (BX, BZ)
YROWS = STEPS * BX + KW * KX


def turn(value, axis, by):
    devices = lax.axis_size(axis)
    return lax.ppermute(value, axis, [(i, (i + by) % devices) for i in range(devices)])


def across_tm(value, where):
    return lax.ppermute(value, "tm", [(i, where(i)) for i in range(16)])


def crossed(value, by_x, by_y):
    pairs = []
    for t in range(16):
        sign = 1 if t % 2 else -1
        for i in range(4):
            for j in range(4):
                to = ((t ^ 1) * 4 + (i + sign * by_x) % 4) * 4 + (j + sign * by_y) % 4
                pairs.append(((t * 4 + i) * 4 + j, to))
    return lax.ppermute(value, ("tm", "sx", "sy"), pairs)


def exchange(edges, last, steps=1):
    x_low, x_high, y_low, y_high = edges
    earlier = turn(last, "tm", steps)
    return (
        turn(x_high, "sx", 1),
        turn(x_low, "sx", -1),
        turn(y_high, "sy", 1),
        turn(y_low, "sy", -1),
    ), earlier


def call(kernel, outs, *args, scratch=()):
    vmem = pl.BlockSpec(memory_space=pltpu.VMEM)
    return pl.pallas_call(
        kernel,
        out_shape=[jax.ShapeDtypeStruct(s, f32) for s in outs],
        in_specs=[vmem] * len(args),
        out_specs=[vmem] * len(outs),
        scratch_shapes=[pltpu.VMEM(s, f32) for s in scratch],
        compiler_params=pltpu.CompilerParams(vmem_limit_bytes=40 * 2**20),
    )(*args)


def inside(condition):
    return jnp.where(condition, f32(1.0), f32(0.0))


def row_index(rows=BY):
    return lax.broadcasted_iota(jnp.int32, (rows, BZ), 0)


def lane_index(rows=BY):
    return lax.broadcasted_iota(jnp.int32, (rows, BZ), 1)


def y_sides(value, low, high, row):
    below = jnp.where(row == 0, low, pltpu.roll(value, 1, 0))
    above = jnp.where(row == BY - 1, high, pltpu.roll(value, BY - 1, 0))
    return below, above


def beside(value, x_below, x_above, y_below, y_above, g):
    total = g[0] * x_below + g[1] * x_above
    total = total + g[2] * y_below + g[3] * y_above
    return total + g[4] * pltpu.roll(value, 1, 1) + g[5] * pltpu.roll(value, BZ - 1, 1)


def row_coefficients(g_ref, x):
    return [g_ref[i, x] for i in range(6)], g_ref[6, x]


def put_edges(refs, n, x, value):
    x_low, x_high, y_low, y_high = refs
    if x == 0:
        x_low[n] = value
    if x == BX - 1:
        x_high[n] = value
    y_low[n, pl.ds(x, 1), :] = value[0:1]
    y_high[n, pl.ds(x, 1), :] = value[BY - 1 : BY]


def edge_shapes(n):
    return [(n, *EDGE)] * 4


def last_step_kernel(u, last):
    last[...] = u[STEPS - 1]


def first_edges_kernel(u, k, x_low, x_high, y_low, y_high):
    for n in range(STEPS):
        x_low[n] = u[n, 0]
        x_high[n] = u[n, BX - 1]
    for j in range(KW):
        x_low[STEPS + j] = k[j]
        x_high[STEPS + j] = k[BX - KW + j]
    for n in range(STEPS + 1):
        for x in range(BX):
            row = u[n, x] if n < STEPS else k[x]
            y_low[n, pl.ds(x, 1), :] = row[0:1]
            y_high[n, pl.ds(x, 1), :] = row[BY - 1 : BY]


def first_kernel(u, h, k, hxl, hxh, hyl, hyh, prev, g_out, first, x_low, x_high, y_low, y_high, last, kx):
    sx, sy, tm = lax.axis_index("sx"), lax.axis_index("sy"), lax.axis_index("tm")
    has_xl, has_xh = inside(sx > 0), inside(sx < 3)
    has_yl, has_yh = inside(sy > 0), inside(sy < 3)
    has_prev = inside(tm > 0)
    row, lane = row_index(), lane_index()
    for j in range(KW):
        kx[j] = hxl[STEPS + j] * has_xl
        kx[KW + BX + j] = hxh[STEPS + j] * has_xh
    for x in range(BX):
        kx[KW + x] = k[x]
    for x in range(BX):
        kc = k[x]
        k_yl = hyl[STEPS, pl.ds(x, 1), :] * has_yl
        k_yh = hyh[STEPS, pl.ds(x, 1), :] * has_yh
        k_below, k_above = y_sides(kc, k_yl, k_yh, row)
        z_below = jnp.where(lane == 0, 0.0, pltpu.roll(kc, 1, 1))
        z_above = jnp.where(lane == BZ - 1, 0.0, pltpu.roll(kc, BZ - 1, 1))
        g = [0.5 * (kc + other) for other in (kx[KW - 1 + x], kx[KW + 1 + x], k_below, k_above, z_below, z_above)]
        coupling = g[0] + g[1] + g[2] + g[3] + g[4] + g[5]
        if x == 0:
            g[0] = g[0] * has_xl
        if x == BX - 1:
            g[1] = g[1] * has_xh
        g[2] = jnp.where(row == 0, g[2] * has_yl, g[2])
        g[3] = jnp.where(row == BY - 1, g[3] * has_yh, g[3])
        g[4] = jnp.where(lane == 0, 0.0, g[4])
        g[5] = jnp.where(lane == BZ - 1, 0.0, g[5])
        for i in range(6):
            g_out[i, x] = g[i]
        g_out[6, x] = coupling
        factor = relax / (1.0 + coupling)
        running = prev[x] * has_prev
        for n in range(STEPS):
            value = u[n, x]
            below = u[n, x - 1] if x > 0 else hxl[n]
            above = u[n, x + 1] if x < BX - 1 else hxh[n]
            sides = y_sides(value, hyl[n, pl.ds(x, 1), :], hyh[n, pl.ds(x, 1), :], row)
            running = keep * value + factor * (h[n, x] + beside(value, below, above, *sides, g) + running)
            first[n, x] = running
            if x == 0:
                x_low[n] = running
            if x == BX - 1:
                x_high[n] = running
            y_low[pl.ds(n * BX + x, 1), :] = running[0:1]
            y_high[pl.ds(n * BX + x, 1), :] = running[BY - 1 : BY]
        last[x] = running
    for x in range(KX):
        kc = kx[x]
        for j in range(KW):
            at = STEPS * BX + j * KX + x
            y_low[pl.ds(at, 1), :] = kc[j : j + 1]
            y_high[pl.ds(at, 1), :] = kc[BY - KW + j : BY - KW + j + 1]


def coarse_terms_kernel(kx, yl, yh, factor, factor4, g_out, ke):
    sx, sy = lax.axis_index("sx"), lax.axis_index("sy")
    has_yl, has_yh = inside(sy > 0), inside(sy < 3)
    row, lane = row_index(EY), lane_index(EY)
    for x in range(KX):
        ke[x, pl.ds(0, BY), :] = kx[x]
        for j in range(KW):
            at = STEPS * BX + j * KX + x
            ke[x, pl.ds(BY + j, 1), :] = yh[pl.ds(at, 1), :] * has_yh
            ke[x, pl.ds(EY - KW + j, 1), :] = yl[pl.ds(at, 1), :] * has_yl
    y_in = jnp.where(row < BY, 1.0, jnp.where(row < BY + KW, has_yh, has_yl))
    for x in range(EX):
        kc = ke[x + 1]
        others = (
            ke[x],
            ke[x + 2],
            pltpu.roll(kc, 1, 0),
            pltpu.roll(kc, EY - 1, 0),
            jnp.where(lane == 0, 0.0, pltpu.roll(kc, 1, 1)),
            jnp.where(lane == BZ - 1, 0.0, pltpu.roll(kc, BZ - 1, 1)),
        )
        g = [0.5 * (kc + other) for other in others]
        coupling = g[0] + g[1] + g[2] + g[3] + g[4] + g[5]
        x_in = inside(sx > 0) if x < WIDE else inside(sx < 3) if x >= BX + WIDE else f32(1.0)
        factor[x] = (relax / (1.0 + 8.0 * coupling)) * (y_in * x_in)
        if 2 <= x <= EX - 3:
            factor4[x - 2] = (relax / (1.0 + 4.0 * coupling)) * (y_in * x_in)
        if 1 <= x <= EX - 2:
            g[4] = jnp.where(lane == 0, 0.0, g[4])
            g[5] = jnp.where(lane == BZ - 1, 0.0, g[5])
            for i in range(6):
                g_out[i, x - 1] = g[i]


def defect_fine_kernel(first, h, g_ref, hxl, hxh, yl, yh, prev, rhs, e0, e1, x_low, x_high, y_low, y_high):
    has_prev = inside(lax.axis_index("tm") > 0)
    row = row_index()
    for x in range(BX):
        g, coupling = row_coefficients(g_ref, x)
        diagonal = 1.0 + coupling
        factor = relax / (1.0 + 2.0 * coupling)
        earlier = prev[x] * has_prev
        parts = []
        for n in range(STEPS):
            value = first[n, x]
            below = first[n, x - 1] if x > 0 else hxl[n]
            above = first[n, x + 1] if x < BX - 1 else hxh[n]
            at = pl.ds(n * BX + x, 1)
            sides = y_sides(value, yl[at, :], yh[at, :], row)
            parts.append(h[n, x] + earlier - diagonal * value + beside(value, below, above, *sides, g))
            earlier = value
        r0, r1 = parts[0] + parts[1], parts[2] + parts[3]
        rhs[0, x] = r0
        rhs[1, x] = r1
        v0 = factor * r0
        v1 = factor * (r1 + v0)
        e0[x] = v0
        e1[x] = v1
        put_edges((x_low, x_high, y_low, y_high), 0, x, v0)
        put_edges((x_low, x_high, y_low, y_high), 1, x, v1)


def defect_mid_kernel(e0, e1, rhs, g_ref, hxl, hxh, hyl, hyh, prev, rhs2, err2, x_low, x_high, y_low, y_high):
    has_prev = inside(lax.axis_index("tm") > 0)
    row = row_index()
    for x in range(BX):
        g, coupling = row_coefficients(g_ref, x)
        diagonal = 1.0 + 2.0 * coupling
        earlier = prev[x] * has_prev
        total = None
        for n, e in enumerate((e0, e1)):
            value = e[x]
            below = e[x - 1] if x > 0 else hxl[n]
            above = e[x + 1] if x < BX - 1 else hxh[n]
            sides = y_sides(value, hyl[n, pl.ds(x, 1), :], hyh[n, pl.ds(x, 1), :], row)
            part = rhs[n, x] + earlier - diagonal * value + 2.0 * beside(value, below, above, *sides, g)
            total = part if total is None else total + part
            earlier = value
        rhs2[x] = total
        value = relax / (1.0 + 4.0 * coupling) * total
        err2[x] = value
        put_edges((x_low, x_high, y_low, y_high), 0, x, value)


def defect_last_kernel(err2, rhs2, g_ref, hxl, hxh, hyl, hyh, chip_before, out):
    has_chip = inside(lax.axis_index("tm") > 1)
    row = row_index()
    for x in range(BX):
        g, coupling = row_coefficients(g_ref, x)
        value = err2[x]
        below = err2[x - 1] if x > 0 else hxl[0]
        above = err2[x + 1] if x < BX - 1 else hxh[0]
        sides = y_sides(value, hyl[0, pl.ds(x, 1), :], hyh[0, pl.ds(x, 1), :], row)
        near = 4.0 * beside(value, below, above, *sides, g)
        out[0, x] = rhs2[x] - (1.0 + 4.0 * coupling) * value + near
        out[1, x] = value
        out[2, x] = chip_before[x] * has_chip


HALF = BX // 2 * BY
XH, YH, CH = HALF, HALF + WIDE * BY, HALF + WIDE * (BY + BX)
SHARE = CH + 8
SIDE = 5 * BY
EXTRA = 2 * SIDE + 8
ALL = COARSE * SHARE


def coarse_edges_kernel(own, other, half, x_edge, y_edge, corner_a, corner_b, rhs3):
    core = lax.axis_index("tm") % 2

    def send(c):
        zero, one = (own, other) if c == 0 else (other, own)
        for x in range(BX):
            rhs3[x] = zero[0, x] + one[0, x] + (zero[1, x] + one[2, x])
        fields = ((rhs3, WIDE), (zero.at[1], 2), (one.at[1], 2), (one.at[2], 1))
        for i in range(BX // 2):
            half[pl.ds(i * BY, BY), :] = rhs3[c * (BX // 2) + i]
        at = 0
        for field, width in fields:
            for j in range(width):
                x_edge[pl.ds((at + j) * BY, BY), :] = field[c * (BX - width) + j]
            for x in range(BX):
                y_edge[pl.ds(at * BX + x * width, width), :] = field[x, pl.ds(c * (BY - width), width), :]
            at += width
        near, then = c * (BX - 1), c * (BX - 3) + 1
        for corner, flip in ((corner_a, False), (corner_b, True)):
            near_y, then_y = (BY - 1 - near, BY - 1 - then) if flip else (near, then)
            corner[...] = jnp.zeros((8, BZ), f32)
            cells = ((rhs3, near, near_y), (rhs3, near, then_y), (rhs3, then, near_y),
                     (zero.at[1], near, near_y), (one.at[1], near, near_y))
            for i, (field, x, y) in enumerate(cells):
                corner[pl.ds(i, 1), :] = field[x, pl.ds(y, 1), :]

    pl.when(core == 1)(lambda: send(1))
    pl.when(core == 0)(lambda: send(0))


def share_kernel(half, x_edge, y_edge, corner_a, corner_b, share, extra):
    share[pl.ds(0, HALF), :] = half[...]
    share[pl.ds(XH, WIDE * BY), :] = x_edge[pl.ds(0, WIDE * BY), :]
    share[pl.ds(YH, WIDE * BX), :] = y_edge[pl.ds(0, WIDE * BX), :]
    share[pl.ds(CH, 8), :] = corner_a[...]
    share[pl.ds(CH + 3, 3), :] = corner_b[pl.ds(0, 3), :]
    extra[pl.ds(0, SIDE), :] = x_edge[pl.ds(WIDE * BY, SIDE), :]
    extra[pl.ds(SIDE, SIDE), :] = y_edge[pl.ds(WIDE * BX, SIDE), :]
    extra[pl.ds(2 * SIDE, 8), :] = corner_a[...]
    extra[pl.ds(2 * SIDE, 2), :] = corner_a[pl.ds(3, 2), :]
    extra[pl.ds(2 * SIDE + 2, 2), :] = corner_b[pl.ds(3, 2), :]


def order_kernel(*refs):
    parts, extra, out = refs[:8], refs[8], refs[9]
    tm = lax.axis_index("tm")
    ring, half = (tm // 2) % 4, tm // 8
    for far in range(2):
        for s in range(4):
            step = (half + far) % 2 * 4 + (ring + 4 - s) % 4
            out[pl.ds(pl.multiple_of(step * SHARE, 8), SHARE), :] = parts[far * 4 + s][...]
    out[pl.ds(ALL, EXTRA), :] = extra[...]


def coarse_kernel(mine, other, factor, factor4, ge_ref, ends, sibling, e0, e1, exl, exh, eyl, eyh, eprev, rhs, g_ref,
                  out0, out1, x_low, x_high, y_low, y_high, r, e, err3, now2, before2, sum2, sum2_before, fixed2):
    sx, sy, tm = lax.axis_index("sx"), lax.axis_index("sy"), lax.axis_index("tm")
    core = tm % 2
    has_xl, has_xh = inside(sx > 0), inside(sx < 3)
    has_yl, has_yh = inside(sy > 0), inside(sy < 3)
    has_prev = inside(tm > 0)
    nothing = jnp.zeros((8, BZ), f32)

    def fill(c, low, high):
        for m in range(COARSE):
            base = m * SHARE
            for x in range(EX):
                r[m, x, pl.ds(BY, 8), :] = nothing
            for j in range(WIDE):
                r[m, j, pl.ds(0, BY), :] = low[pl.ds(base + XH + j * BY, BY), :]
                r[m, BX + WIDE + j, pl.ds(0, BY), :] = high[pl.ds(base + XH + j * BY, BY), :]
            for x in range(BX):
                source = (low, high)[x // (BX // 2)]
                r[m, x + WIDE, pl.ds(0, BY), :] = source[pl.ds(base + x % (BX // 2) * BY, BY), :]
                r[m, x + WIDE, pl.ds(BY, WIDE), :] = high[pl.ds(base + YH + x * WIDE, WIDE), :]
                r[m, x + WIDE, pl.ds(EY - WIDE, WIDE), :] = low[pl.ds(base + YH + x * WIDE, WIDE), :]
            for i, (dx, dy) in enumerate(((1, 1), (1, 2), (2, 1))):
                below, above = WIDE - dx, BX + WIDE - 1 + dx
                r[m, below, pl.ds(EY - dy, 1), :] = low[pl.ds(base + CH + i, 1), :]
                r[m, below, pl.ds(BY - 1 + dy, 1), :] = low[pl.ds(base + CH + 3 + i, 1), :]
                r[m, above, pl.ds(BY - 1 + dy, 1), :] = high[pl.ds(base + CH + i, 1), :]
                r[m, above, pl.ds(EY - dy, 1), :] = high[pl.ds(base + CH + 3 + i, 1), :]
        xs, ys, cs = ALL, ALL + SIDE, ALL + 2 * SIDE
        for x in range(BX + 4):
            now2[x, pl.ds(BY, 8), :] = nothing
        for x in range(BX + 2):
            before2[x, pl.ds(BY, 8), :] = nothing
        mine_at = c * 2
        for j in range(2):
            now2[j, pl.ds(0, BY), :] = low[pl.ds(xs + (mine_at + j) * BY, BY), :] * has_xl
            now2[BX + 2 + j, pl.ds(0, BY), :] = high[pl.ds(xs + (mine_at + j) * BY, BY), :] * has_xh
        for x in range(BX):
            now2[x + 2, pl.ds(0, BY), :] = ends[1, x]
            now2[x + 2, pl.ds(BY, 2), :] = high[pl.ds(ys + mine_at * BX + 2 * x, 2), :] * has_yh
            now2[x + 2, pl.ds(EY - 2, 2), :] = low[pl.ds(ys + mine_at * BX + 2 * x, 2), :] * has_yl
        now2[1, pl.ds(EY - 1, 1), :] = low[pl.ds(cs + c, 1), :] * (has_xl * has_yl)
        now2[1, pl.ds(BY, 1), :] = low[pl.ds(cs + 2 + c, 1), :] * (has_xl * has_yh)
        now2[BX + 2, pl.ds(BY, 1), :] = high[pl.ds(cs + c, 1), :] * (has_xh * has_yh)
        now2[BX + 2, pl.ds(EY - 1, 1), :] = high[pl.ds(cs + 2 + c, 1), :] * (has_xh * has_yl)
        at_low, at_high, y_at, step = (4, 4, 4 * BX, 1) if c == 0 else (1, 0, 0, 2)
        before2[0, pl.ds(0, BY), :] = low[pl.ds(xs + at_low * BY, BY), :] * has_xl
        before2[BX + 1, pl.ds(0, BY), :] = high[pl.ds(xs + at_high * BY, BY), :] * has_xh
        for x in range(BX):
            before2[x + 1, pl.ds(0, BY), :] = sibling[2 - c, x]
            before2[x + 1, pl.ds(BY, 1), :] = high[pl.ds(ys + y_at + step * x, 1), :] * has_yh
            before2[x + 1, pl.ds(EY - 1, 1), :] = low[pl.ds(ys + y_at + step * x + step - 1, 1), :] * has_yl

    pl.when(core == 0)(lambda: fill(0, mine, other))
    pl.when(core == 1)(lambda: fill(1, other, mine))

    def sweep_one(x, carry):
        w = factor[x]
        running = jnp.zeros((EY, BZ), f32)
        for m in range(COARSE):
            running = w * (r[m, x] + running)
            e[m, x] = running
        return carry

    for x in range(EX):
        sweep_one(x, 0)

    def sweep_two(x, carry):
        w = factor[x + 1]
        g = [ge_ref[i, x] for i in range(6)]
        running = jnp.zeros((EY, BZ), f32)
        err3[0, x] = running
        for m in range(COARSE):
            value = e[m, x + 1]
            near = beside(value, e[m, x], e[m, x + 2], pltpu.roll(value, 1, 0), pltpu.roll(value, EY - 1, 0), g)
            running = keep * value + w * (r[m, x + 1] + 8.0 * near) + w * running
            err3[m + 1, x] = running
        return carry

    lax.fori_loop(0, BX + 4, sweep_two, 0, unroll=5)

    row = row_index()
    now, before, earliest = tm // 2 + 1, (tm + 1) // 2, tm // 2

    def turned(value):
        return pltpu.roll(value, 1, 0), pltpu.roll(value, EY - 1, 0)

    for x in range(BX + 4):
        sum2[x] = now2[x] + err3[now, x]
    for x in range(BX + 2):
        sum2_before[x] = before2[x] + err3[before, x + 1]
    for x in range(BX + 2):
        value = sum2[x + 1]
        near = beside(value, sum2[x], sum2[x + 2], *turned(value), [ge_ref[i, x + 1] for i in range(6)])
        fixed2[x] = keep * value + now2[x + 1] + factor4[x] * (4.0 * near + sum2_before[x])
    for x in range(BX):
        value = sum2_before[x + 1]
        near = beside(value, sum2_before[x], sum2_before[x + 2], *turned(value), [ge_ref[i, x + 2] for i in range(6)])
        two_before = ends[2, x] + err3[earliest, x + 2, pl.ds(0, BY), :]
        fixed_before = (keep * value + before2[x + 1] + factor4[x + 1] * (4.0 * near))[0:BY]
        fixed_before = fixed_before + factor4[x + 1, pl.ds(0, BY), :] * two_before
        g, coupling = row_coefficients(g_ref, x)
        weight = relax / (1.0 + 2.0 * coupling)
        running = (eprev[x] + fixed_before) * has_prev
        here = fixed2[x + 1]
        f_below, f_above = fixed2[x, pl.ds(0, BY), :], fixed2[x + 2, pl.ds(0, BY), :]
        for n, (err, out) in enumerate(((e0, out0), (e1, out1))):
            value = err[x] + here[0:BY]
            below = (err[x - 1] if x > 0 else exl[n]) + f_below
            above = (err[x + 1] if x < BX - 1 else exh[n]) + f_above
            low = eyl[n, pl.ds(x, 1), :] + here[EY - 1 : EY]
            high = eyh[n, pl.ds(x, 1), :] + here[BY : BY + 1]
            near = 2.0 * beside(value, below, above, *y_sides(value, low, high, row), g)
            running = keep * value + weight * (rhs[n, x] + near + running)
            out[x] = running
            put_edges((x_low, x_high, y_low, y_high), n, x, running)


def solution_kernel(fix0, fix1, fxl, fxh, fyl, fyh, fprev, first, exl, exh, yl, yh, eprev, h, g_ref,
                    out, x_low, x_high, y_low, y_high, last):
    has_prev = inside(lax.axis_index("tm") > 0)
    row = row_index()
    for x in range(BX):
        g, coupling = row_coefficients(g_ref, x)
        factor = relax / (1.0 + coupling)
        running = (eprev[x] + fprev[x]) * has_prev
        for n in range(STEPS):
            fix, c = (fix0, fix1)[n // 2], n // 2
            value = first[n, x] + fix[x]
            below = (first[n, x - 1] + fix[x - 1]) if x > 0 else (exl[n] + fxl[c])
            above = (first[n, x + 1] + fix[x + 1]) if x < BX - 1 else (exh[n] + fxh[c])
            at = pl.ds(n * BX + x, 1)
            low = yl[at, :] + fyl[c, pl.ds(x, 1), :]
            high = yh[at, :] + fyh[c, pl.ds(x, 1), :]
            sides = y_sides(value, low, high, row)
            running = keep * value + factor * (h[n, x] + beside(value, below, above, *sides, g) + running)
            out[n, x] = running
            put_edges((x_low, x_high, y_low, y_high), n, x, running)
        last[x] = running


def copy_kernel(source, target):
    target[...] = source[...]


def residual_kernel(sol, h, g_ref, hxl, hxh, hyl, hyh, prev, out):
    has_prev = inside(lax.axis_index("tm") > 0)
    row = row_index()
    for x in range(BX):
        g, coupling = row_coefficients(g_ref, x)
        diagonal = 1.0 + coupling
        earlier = prev[x] * has_prev
        for n in range(STEPS):
            value = sol[n, x]
            below = sol[n, x - 1] if x > 0 else hxl[n]
            above = sol[n, x + 1] if x < BX - 1 else hxh[n]
            sides = y_sides(value, hyl[n, pl.ds(x, 1), :], hyh[n, pl.ds(x, 1), :], row)
            out[n, x] = h[n, x] + earlier - diagonal * value + beside(value, below, above, *sides, g)
            earlier = value


def gather_steps(own):
    def along(value, s):
        return across_tm(value, lambda i: (i & 9) | ((i + 2 * s) & 6))

    far = across_tm(own, lambda i: i ^ 8)
    near = [own] + [along(own, s) for s in (1, 2, 3)]
    return near + [far] + [along(far, s) for s in (1, 2, 3)]


def per_device(h, k, u):
    fine, two = (STEPS, *FIELD), (2, *FIELD)
    ypack = (YROWS, BZ)
    (last,) = call(last_step_kernel, [FIELD], u)
    edges = call(first_edges_kernel, [(STEPS + KW, *EDGE)] * 2 + [(STEPS + 1, *EDGE)] * 2, u, k)
    (h,) = call(copy_kernel, [fine], h)
    halo, prev = exchange(edges, last)
    g, first, *edges, last, kx = call(
        first_kernel,
        [(7, *FIELD), fine, (STEPS, *EDGE), (STEPS, *EDGE), ypack, ypack, FIELD, (KX, BY, BZ)],
        u, h, k, *halo, prev,
    )
    first_halo, first_prev = exchange(edges, last)
    factor, factor4, g_coarse = call(
        coarse_terms_kernel,
        [(EX, EY, BZ), (BX + 2, EY, BZ), (6, BX + 4, EY, BZ)],
        kx, *first_halo[2:],
        scratch=[(KX, EY, BZ)],
    )
    rhs1, e0, e1, *edges = call(
        defect_fine_kernel, [two, FIELD, FIELD] + edge_shapes(2), first, h, g, *first_halo, first_prev
    )
    err1_halo, err1_prev = exchange(edges, e1)
    rhs2, err2, *edges = call(
        defect_mid_kernel, [FIELD, FIELD] + edge_shapes(1), e0, e1, rhs1, g, *err1_halo, err1_prev
    )
    err2_halo, chip_before = exchange(edges, err2, 2)
    (ends,) = call(defect_last_kernel, [(3, *FIELD)], err2, rhs2, g, *err2_halo, chip_before)
    sibling = across_tm(ends, lambda i: i ^ 1)
    half, x_edge, y_edge, corner_a, corner_b = call(
        coarse_edges_kernel,
        [(HALF, BZ), (WIDE * BY + SIDE, BZ), (WIDE * BX + SIDE, BZ), (8, BZ), (8, BZ)],
        ends, sibling,
        scratch=[FIELD],
    )
    share, extra = call(
        share_kernel,
        [(SHARE, BZ), (EXTRA, BZ)],
        half, crossed(x_edge, 1, 0), crossed(y_edge, 0, 1), crossed(corner_a, 1, 1), crossed(corner_b, 1, -1),
    )
    (mine,) = call(order_kernel, [(ALL + EXTRA, BZ)], *gather_steps(share), extra)
    other = across_tm(mine, lambda i: i ^ 1)
    fixed1a, fixed1b, *edges = call(
        coarse_kernel,
        [FIELD, FIELD] + edge_shapes(2),
        mine, other, factor, factor4, g_coarse, ends, sibling,
        e0, e1, *err1_halo, err1_prev, rhs1, g,
        scratch=[
            (COARSE, EX, EY, BZ), (COARSE, EX, EY, BZ), (COARSE + 1, BX + 4, EY, BZ),
            (BX + 4, EY, BZ), (BX + 2, EY, BZ), (BX + 4, EY, BZ), (BX + 2, EY, BZ), (BX + 2, EY, BZ),
        ],
    )
    fixed1_halo, fixed1_prev = exchange(edges, fixed1b)
    last_iterate, *edges, last = call(
        solution_kernel,
        [fine] + edge_shapes(STEPS) + [FIELD],
        fixed1a, fixed1b, *fixed1_halo, fixed1_prev, first, *first_halo, first_prev, h, g,
    )
    out_halo, out_prev = exchange(edges, last)
    (out,) = call(copy_kernel, [fine], last_iterate)
    (residual,) = call(residual_kernel, [fine], last_iterate, h, g, *out_halo, out_prev)
    return out, residual


def solution(mesh):
    placed = (P("tm", "sx", "sy", None), P("sx", "sy", None), P("tm", "sx", "sy", None))
    return jax.shard_map(
        per_device,
        mesh=mesh,
        in_specs=placed,
        out_specs=(P("tm", "sx", "sy", None), P("tm", "sx", "sy", None)),
        check_vma=False,
    )
```

```python
import jax
import jax.numpy as jnp
from jax import lax
from jax.experimental import pallas as pl
from jax.experimental.pallas import tpu as pltpu
from jax.sharding import PartitionSpec as P

relax = 0.8
keep = 1.0 - relax
STEPS, BX, BY, BZ = 4, 16, 16, 128
COARSE = 8
WIDE = 3
KW = WIDE + 1
EX, EY = BX + 2 * WIDE, BY + 2 * KW
KX = BX + 2 * KW
f32 = jnp.float32
FIELD = (BX, BY, BZ)
EDGE = (BX, BZ)
YROWS = STEPS * BX + KW * KX


def turn(value, axis, by):
    devices = lax.axis_size(axis)
    return lax.ppermute(value, axis, [(i, (i + by) % devices) for i in range(devices)])


def across_tm(value, where):
    return lax.ppermute(value, "tm", [(i, where(i)) for i in range(16)])


def crossed(value, by_x, by_y):
    pairs = []
    for t in range(16):
        sign = 1 if t % 2 else -1
        for i in range(4):
            for j in range(4):
                to = ((t ^ 1) * 4 + (i + sign * by_x) % 4) * 4 + (j + sign * by_y) % 4
                pairs.append(((t * 4 + i) * 4 + j, to))
    return lax.ppermute(value, ("tm", "sx", "sy"), pairs)


def exchange(edges, last, steps=1):
    x_low, x_high, y_low, y_high = edges
    earlier = turn(last, "tm", steps)
    return (
        turn(x_high, "sx", 1),
        turn(x_low, "sx", -1),
        turn(y_high, "sy", 1),
        turn(y_low, "sy", -1),
    ), earlier


def call(kernel, outs, *args, scratch=()):
    vmem = pl.BlockSpec(memory_space=pltpu.VMEM)
    return pl.pallas_call(
        kernel,
        out_shape=[jax.ShapeDtypeStruct(s, f32) for s in outs],
        in_specs=[vmem] * len(args),
        out_specs=[vmem] * len(outs),
        scratch_shapes=[pltpu.VMEM(s, f32) for s in scratch],
        compiler_params=pltpu.CompilerParams(vmem_limit_bytes=40 * 2**20),
    )(*args)


def inside(condition):
    return jnp.where(condition, f32(1.0), f32(0.0))


def row_index(rows=BY):
    return lax.broadcasted_iota(jnp.int32, (rows, BZ), 0)


def lane_index(rows=BY):
    return lax.broadcasted_iota(jnp.int32, (rows, BZ), 1)


def y_sides(value, low, high, row):
    below = jnp.where(row == 0, low, pltpu.roll(value, 1, 0))
    above = jnp.where(row == BY - 1, high, pltpu.roll(value, BY - 1, 0))
    return below, above


def beside(value, x_below, x_above, y_below, y_above, g):
    total = g[0] * x_below + g[1] * x_above
    total = total + g[2] * y_below + g[3] * y_above
    return total + g[4] * pltpu.roll(value, 1, 1) + g[5] * pltpu.roll(value, BZ - 1, 1)


def row_coefficients(g_ref, x):
    return [g_ref[i, x] for i in range(6)], g_ref[6, x]


def put_edges(refs, n, x, value):
    x_low, x_high, y_low, y_high = refs
    if x == 0:
        x_low[n] = value
    if x == BX - 1:
        x_high[n] = value
    y_low[n, pl.ds(x, 1), :] = value[0:1]
    y_high[n, pl.ds(x, 1), :] = value[BY - 1 : BY]


def edge_shapes(n):
    return [(n, *EDGE)] * 4


def last_step_kernel(u, last):
    last[...] = u[STEPS - 1]


def first_edges_kernel(u, k, x_low, x_high, y_low, y_high):
    for n in range(STEPS):
        x_low[n] = u[n, 0]
        x_high[n] = u[n, BX - 1]
    for j in range(KW):
        x_low[STEPS + j] = k[j]
        x_high[STEPS + j] = k[BX - KW + j]
    for n in range(STEPS + 1):
        for x in range(BX):
            row = u[n, x] if n < STEPS else k[x]
            y_low[n, pl.ds(x, 1), :] = row[0:1]
            y_high[n, pl.ds(x, 1), :] = row[BY - 1 : BY]


def first_kernel(u, h, k, hxl, hxh, hyl, hyh, prev, g_out, first, x_low, x_high, y_low, y_high, last, kx):
    sx, sy, tm = lax.axis_index("sx"), lax.axis_index("sy"), lax.axis_index("tm")
    has_xl, has_xh = inside(sx > 0), inside(sx < 3)
    has_yl, has_yh = inside(sy > 0), inside(sy < 3)
    has_prev = inside(tm > 0)
    row, lane = row_index(), lane_index()
    for j in range(KW):
        kx[j] = hxl[STEPS + j] * has_xl
        kx[KW + BX + j] = hxh[STEPS + j] * has_xh
    for x in range(BX):
        kx[KW + x] = k[x]
    for x in range(BX):
        kc = k[x]
        k_yl = hyl[STEPS, pl.ds(x, 1), :] * has_yl
        k_yh = hyh[STEPS, pl.ds(x, 1), :] * has_yh
        k_below, k_above = y_sides(kc, k_yl, k_yh, row)
        z_below = jnp.where(lane == 0, 0.0, pltpu.roll(kc, 1, 1))
        z_above = jnp.where(lane == BZ - 1, 0.0, pltpu.roll(kc, BZ - 1, 1))
        g = [0.5 * (kc + other) for other in (kx[KW - 1 + x], kx[KW + 1 + x], k_below, k_above, z_below, z_above)]
        coupling = g[0] + g[1] + g[2] + g[3] + g[4] + g[5]
        if x == 0:
            g[0] = g[0] * has_xl
        if x == BX - 1:
            g[1] = g[1] * has_xh
        g[2] = jnp.where(row == 0, g[2] * has_yl, g[2])
        g[3] = jnp.where(row == BY - 1, g[3] * has_yh, g[3])
        g[4] = jnp.where(lane == 0, 0.0, g[4])
        g[5] = jnp.where(lane == BZ - 1, 0.0, g[5])
        for i in range(6):
            g_out[i, x] = g[i]
        g_out[6, x] = coupling
        factor = relax / (1.0 + coupling)
        running = prev[x] * has_prev
        for n in range(STEPS):
            value = u[n, x]
            below = u[n, x - 1] if x > 0 else hxl[n]
            above = u[n, x + 1] if x < BX - 1 else hxh[n]
            sides = y_sides(value, hyl[n, pl.ds(x, 1), :], hyh[n, pl.ds(x, 1), :], row)
            running = keep * value + factor * (h[n, x] + beside(value, below, above, *sides, g) + running)
            first[n, x] = running
            if x == 0:
                x_low[n] = running
            if x == BX - 1:
                x_high[n] = running
            y_low[pl.ds(n * BX + x, 1), :] = running[0:1]
            y_high[pl.ds(n * BX + x, 1), :] = running[BY - 1 : BY]
        last[x] = running
    for x in range(KX):
        kc = kx[x]
        for j in range(KW):
            at = STEPS * BX + j * KX + x
            y_low[pl.ds(at, 1), :] = kc[j : j + 1]
            y_high[pl.ds(at, 1), :] = kc[BY - KW + j : BY - KW + j + 1]


def coarse_terms_kernel(kx, yl, yh, factor, factor4, g_out, ke):
    sx, sy = lax.axis_index("sx"), lax.axis_index("sy")
    has_yl, has_yh = inside(sy > 0), inside(sy < 3)
    row, lane = row_index(EY), lane_index(EY)
    for x in range(KX):
        ke[x, pl.ds(0, BY), :] = kx[x]
        for j in range(KW):
            at = STEPS * BX + j * KX + x
            ke[x, pl.ds(BY + j, 1), :] = yh[pl.ds(at, 1), :] * has_yh
            ke[x, pl.ds(EY - KW + j, 1), :] = yl[pl.ds(at, 1), :] * has_yl
    y_in = jnp.where(row < BY, 1.0, jnp.where(row < BY + KW, has_yh, has_yl))
    for x in range(EX):
        kc = ke[x + 1]
        others = (
            ke[x],
            ke[x + 2],
            pltpu.roll(kc, 1, 0),
            pltpu.roll(kc, EY - 1, 0),
            jnp.where(lane == 0, 0.0, pltpu.roll(kc, 1, 1)),
            jnp.where(lane == BZ - 1, 0.0, pltpu.roll(kc, BZ - 1, 1)),
        )
        g = [0.5 * (kc + other) for other in others]
        coupling = g[0] + g[1] + g[2] + g[3] + g[4] + g[5]
        x_in = inside(sx > 0) if x < WIDE else inside(sx < 3) if x >= BX + WIDE else f32(1.0)
        factor[x] = (relax / (1.0 + 8.0 * coupling)) * (y_in * x_in)
        if 2 <= x <= EX - 3:
            factor4[x - 2] = (relax / (1.0 + 4.0 * coupling)) * (y_in * x_in)
        if 1 <= x <= EX - 2:
            g[4] = jnp.where(lane == 0, 0.0, g[4])
            g[5] = jnp.where(lane == BZ - 1, 0.0, g[5])
            for i in range(6):
                g_out[i, x - 1] = g[i]


def defect_fine_kernel(first, h, g_ref, hxl, hxh, yl, yh, prev, rhs, e0, e1, x_low, x_high, y_low, y_high):
    has_prev = inside(lax.axis_index("tm") > 0)
    row = row_index()
    for x in range(BX):
        g, coupling = row_coefficients(g_ref, x)
        diagonal = 1.0 + coupling
        factor = relax / (1.0 + 2.0 * coupling)
        earlier = prev[x] * has_prev
        parts = []
        for n in range(STEPS):
            value = first[n, x]
            below = first[n, x - 1] if x > 0 else hxl[n]
            above = first[n, x + 1] if x < BX - 1 else hxh[n]
            at = pl.ds(n * BX + x, 1)
            sides = y_sides(value, yl[at, :], yh[at, :], row)
            parts.append(h[n, x] + earlier - diagonal * value + beside(value, below, above, *sides, g))
            earlier = value
        r0, r1 = parts[0] + parts[1], parts[2] + parts[3]
        rhs[0, x] = r0
        rhs[1, x] = r1
        v0 = factor * r0
        v1 = factor * (r1 + v0)
        e0[x] = v0
        e1[x] = v1
        put_edges((x_low, x_high, y_low, y_high), 0, x, v0)
        put_edges((x_low, x_high, y_low, y_high), 1, x, v1)


def defect_mid_kernel(e0, e1, rhs, g_ref, hxl, hxh, hyl, hyh, prev, rhs2, err2, x_low, x_high, y_low, y_high):
    has_prev = inside(lax.axis_index("tm") > 0)
    row = row_index()
    for x in range(BX):
        g, coupling = row_coefficients(g_ref, x)
        diagonal = 1.0 + 2.0 * coupling
        earlier = prev[x] * has_prev
        total = None
        for n, e in enumerate((e0, e1)):
            value = e[x]
            below = e[x - 1] if x > 0 else hxl[n]
            above = e[x + 1] if x < BX - 1 else hxh[n]
            sides = y_sides(value, hyl[n, pl.ds(x, 1), :], hyh[n, pl.ds(x, 1), :], row)
            part = rhs[n, x] + earlier - diagonal * value + 2.0 * beside(value, below, above, *sides, g)
            total = part if total is None else total + part
            earlier = value
        rhs2[x] = total
        value = relax / (1.0 + 4.0 * coupling) * total
        err2[x] = value
        put_edges((x_low, x_high, y_low, y_high), 0, x, value)


def defect_last_kernel(err2, rhs2, g_ref, hxl, hxh, hyl, hyh, chip_before, out):
    has_chip = inside(lax.axis_index("tm") > 1)
    row = row_index()
    for x in range(BX):
        g, coupling = row_coefficients(g_ref, x)
        value = err2[x]
        below = err2[x - 1] if x > 0 else hxl[0]
        above = err2[x + 1] if x < BX - 1 else hxh[0]
        sides = y_sides(value, hyl[0, pl.ds(x, 1), :], hyh[0, pl.ds(x, 1), :], row)
        near = 4.0 * beside(value, below, above, *sides, g)
        out[0, x] = rhs2[x] - (1.0 + 4.0 * coupling) * value + near
        out[1, x] = value
        out[2, x] = chip_before[x] * has_chip


HALF = BX // 2 * BY
XH, YH, CH = HALF, HALF + WIDE * BY, HALF + WIDE * (BY + BX)
SHARE = CH + 8
SIDE = 5 * BY
EXTRA = 2 * SIDE + 8
ALL = COARSE * SHARE


def coarse_edges_kernel(own, other, half, x_edge, y_edge, corner_a, corner_b, rhs3):
    core = lax.axis_index("tm") % 2

    def send(c):
        zero, one = (own, other) if c == 0 else (other, own)
        for x in range(BX):
            rhs3[x] = zero[0, x] + one[0, x] + (zero[1, x] + one[2, x])
        fields = ((rhs3, WIDE), (zero.at[1], 2), (one.at[1], 2), (one.at[2], 1))
        for i in range(BX // 2):
            half[pl.ds(i * BY, BY), :] = rhs3[c * (BX // 2) + i]
        at = 0
        for field, width in fields:
            for j in range(width):
                x_edge[pl.ds((at + j) * BY, BY), :] = field[c * (BX - width) + j]
            for x in range(BX):
                y_edge[pl.ds(at * BX + x * width, width), :] = field[x, pl.ds(c * (BY - width), width), :]
            at += width
        near, then = c * (BX - 1), c * (BX - 3) + 1
        for corner, flip in ((corner_a, False), (corner_b, True)):
            near_y, then_y = (BY - 1 - near, BY - 1 - then) if flip else (near, then)
            corner[...] = jnp.zeros((8, BZ), f32)
            cells = ((rhs3, near, near_y), (rhs3, near, then_y), (rhs3, then, near_y),
                     (zero.at[1], near, near_y), (one.at[1], near, near_y))
            for i, (field, x, y) in enumerate(cells):
                corner[pl.ds(i, 1), :] = field[x, pl.ds(y, 1), :]

    pl.when(core == 1)(lambda: send(1))
    pl.when(core == 0)(lambda: send(0))


def share_kernel(half, x_edge, y_edge, corner_a, corner_b, share, extra):
    share[pl.ds(0, HALF), :] = half[...]
    share[pl.ds(XH, WIDE * BY), :] = x_edge[pl.ds(0, WIDE * BY), :]
    share[pl.ds(YH, WIDE * BX), :] = y_edge[pl.ds(0, WIDE * BX), :]
    share[pl.ds(CH, 8), :] = corner_a[...]
    share[pl.ds(CH + 3, 3), :] = corner_b[pl.ds(0, 3), :]
    extra[pl.ds(0, SIDE), :] = x_edge[pl.ds(WIDE * BY, SIDE), :]
    extra[pl.ds(SIDE, SIDE), :] = y_edge[pl.ds(WIDE * BX, SIDE), :]
    extra[pl.ds(2 * SIDE, 8), :] = corner_a[...]
    extra[pl.ds(2 * SIDE, 2), :] = corner_a[pl.ds(3, 2), :]
    extra[pl.ds(2 * SIDE + 2, 2), :] = corner_b[pl.ds(3, 2), :]


def order_kernel(*refs):
    parts, extra, out = refs[:8], refs[8], refs[9]
    tm = lax.axis_index("tm")
    ring, half = (tm // 2) % 4, tm // 8
    for far in range(2):
        for s in range(4):
            step = (half + far) % 2 * 4 + (ring + 4 - s) % 4
            out[pl.ds(pl.multiple_of(step * SHARE, 8), SHARE), :] = parts[far * 4 + s][...]
    out[pl.ds(ALL, EXTRA), :] = extra[...]


def coarse_kernel(mine, other, factor, factor4, ge_ref, ends, sibling, e0, e1, exl, exh, eyl, eyh, eprev, rhs, g_ref,
                  out0, out1, x_low, x_high, y_low, y_high, r, e, err3, now2, before2, sum2, sum2_before, fixed2):
    sx, sy, tm = lax.axis_index("sx"), lax.axis_index("sy"), lax.axis_index("tm")
    core = tm % 2
    has_xl, has_xh = inside(sx > 0), inside(sx < 3)
    has_yl, has_yh = inside(sy > 0), inside(sy < 3)
    has_prev = inside(tm > 0)
    nothing = jnp.zeros((8, BZ), f32)

    def fill(c, low, high):
        for m in range(COARSE):
            base = m * SHARE
            for x in range(EX):
                r[m, x, pl.ds(BY, 8), :] = nothing
            for j in range(WIDE):
                r[m, j, pl.ds(0, BY), :] = low[pl.ds(base + XH + j * BY, BY), :]
                r[m, BX + WIDE + j, pl.ds(0, BY), :] = high[pl.ds(base + XH + j * BY, BY), :]
            for x in range(BX):
                source = (low, high)[x // (BX // 2)]
                r[m, x + WIDE, pl.ds(0, BY), :] = source[pl.ds(base + x % (BX // 2) * BY, BY), :]
                r[m, x + WIDE, pl.ds(BY, WIDE), :] = high[pl.ds(base + YH + x * WIDE, WIDE), :]
                r[m, x + WIDE, pl.ds(EY - WIDE, WIDE), :] = low[pl.ds(base + YH + x * WIDE, WIDE), :]
            for i, (dx, dy) in enumerate(((1, 1), (1, 2), (2, 1))):
                below, above = WIDE - dx, BX + WIDE - 1 + dx
                r[m, below, pl.ds(EY - dy, 1), :] = low[pl.ds(base + CH + i, 1), :]
                r[m, below, pl.ds(BY - 1 + dy, 1), :] = low[pl.ds(base + CH + 3 + i, 1), :]
                r[m, above, pl.ds(BY - 1 + dy, 1), :] = high[pl.ds(base + CH + i, 1), :]
                r[m, above, pl.ds(EY - dy, 1), :] = high[pl.ds(base + CH + 3 + i, 1), :]
        xs, ys, cs = ALL, ALL + SIDE, ALL + 2 * SIDE
        for x in range(BX + 4):
            now2[x, pl.ds(BY, 8), :] = nothing
        for x in range(BX + 2):
            before2[x, pl.ds(BY, 8), :] = nothing
        mine_at = c * 2
        for j in range(2):
            now2[j, pl.ds(0, BY), :] = low[pl.ds(xs + (mine_at + j) * BY, BY), :] * has_xl
            now2[BX + 2 + j, pl.ds(0, BY), :] = high[pl.ds(xs + (mine_at + j) * BY, BY), :] * has_xh
        for x in range(BX):
            now2[x + 2, pl.ds(0, BY), :] = ends[1, x]
            now2[x + 2, pl.ds(BY, 2), :] = high[pl.ds(ys + mine_at * BX + 2 * x, 2), :] * has_yh
            now2[x + 2, pl.ds(EY - 2, 2), :] = low[pl.ds(ys + mine_at * BX + 2 * x, 2), :] * has_yl
        now2[1, pl.ds(EY - 1, 1), :] = low[pl.ds(cs + c, 1), :] * (has_xl * has_yl)
        now2[1, pl.ds(BY, 1), :] = low[pl.ds(cs + 2 + c, 1), :] * (has_xl * has_yh)
        now2[BX + 2, pl.ds(BY, 1), :] = high[pl.ds(cs + c, 1), :] * (has_xh * has_yh)
        now2[BX + 2, pl.ds(EY - 1, 1), :] = high[pl.ds(cs + 2 + c, 1), :] * (has_xh * has_yl)
        at_low, at_high, y_at, step = (4, 4, 4 * BX, 1) if c == 0 else (1, 0, 0, 2)
        before2[0, pl.ds(0, BY), :] = low[pl.ds(xs + at_low * BY, BY), :] * has_xl
        before2[BX + 1, pl.ds(0, BY), :] = high[pl.ds(xs + at_high * BY, BY), :] * has_xh
        for x in range(BX):
            before2[x + 1, pl.ds(0, BY), :] = sibling[2 - c, x]
            before2[x + 1, pl.ds(BY, 1), :] = high[pl.ds(ys + y_at + step * x, 1), :] * has_yh
            before2[x + 1, pl.ds(EY - 1, 1), :] = low[pl.ds(ys + y_at + step * x + step - 1, 1), :] * has_yl

    pl.when(core == 0)(lambda: fill(0, mine, other))
    pl.when(core == 1)(lambda: fill(1, other, mine))

    def sweep_one(x, carry):
        w = factor[x]
        running = jnp.zeros((EY, BZ), f32)
        for m in range(COARSE):
            running = w * (r[m, x] + running)
            e[m, x] = running
        return carry

    for x in range(EX):
        sweep_one(x, 0)

    def sweep_two(x, carry):
        w = factor[x + 1]
        g = [ge_ref[i, x] for i in range(6)]
        running = jnp.zeros((EY, BZ), f32)
        err3[0, x] = running
        for m in range(COARSE):
            value = e[m, x + 1]
            near = beside(value, e[m, x], e[m, x + 2], pltpu.roll(value, 1, 0), pltpu.roll(value, EY - 1, 0), g)
            running = keep * value + w * (r[m, x + 1] + 8.0 * near) + w * running
            err3[m + 1, x] = running
        return carry

    lax.fori_loop(0, BX + 4, sweep_two, 0, unroll=10)

    row = row_index()
    now, before, earliest = tm // 2 + 1, (tm + 1) // 2, tm // 2

    def turned(value):
        return pltpu.roll(value, 1, 0), pltpu.roll(value, EY - 1, 0)

    for x in range(BX + 4):
        sum2[x] = now2[x] + err3[now, x]
    for x in range(BX + 2):
        sum2_before[x] = before2[x] + err3[before, x + 1]
    for x in range(BX + 2):
        value = sum2[x + 1]
        near = beside(value, sum2[x], sum2[x + 2], *turned(value), [ge_ref[i, x + 1] for i in range(6)])
        fixed2[x] = keep * value + now2[x + 1] + factor4[x] * (4.0 * near + sum2_before[x])
    for x in range(BX):
        value = sum2_before[x + 1]
        near = beside(value, sum2_before[x], sum2_before[x + 2], *turned(value), [ge_ref[i, x + 2] for i in range(6)])
        two_before = ends[2, x] + err3[earliest, x + 2, pl.ds(0, BY), :]
        fixed_before = (keep * value + before2[x + 1] + factor4[x + 1] * (4.0 * near))[0:BY]
        fixed_before = fixed_before + factor4[x + 1, pl.ds(0, BY), :] * two_before
        g, coupling = row_coefficients(g_ref, x)
        weight = relax / (1.0 + 2.0 * coupling)
        running = (eprev[x] + fixed_before) * has_prev
        here = fixed2[x + 1]
        f_below, f_above = fixed2[x, pl.ds(0, BY), :], fixed2[x + 2, pl.ds(0, BY), :]
        for n, (err, out) in enumerate(((e0, out0), (e1, out1))):
            value = err[x] + here[0:BY]
            below = (err[x - 1] if x > 0 else exl[n]) + f_below
            above = (err[x + 1] if x < BX - 1 else exh[n]) + f_above
            low = eyl[n, pl.ds(x, 1), :] + here[EY - 1 : EY]
            high = eyh[n, pl.ds(x, 1), :] + here[BY : BY + 1]
            near = 2.0 * beside(value, below, above, *y_sides(value, low, high, row), g)
            running = keep * value + weight * (rhs[n, x] + near + running)
            out[x] = running
            put_edges((x_low, x_high, y_low, y_high), n, x, running)


def solution_kernel(fix0, fix1, fxl, fxh, fyl, fyh, fprev, first, exl, exh, yl, yh, eprev, h, g_ref,
                    out, x_low, x_high, y_low, y_high, last):
    has_prev = inside(lax.axis_index("tm") > 0)
    row = row_index()
    for x in range(BX):
        g, coupling = row_coefficients(g_ref, x)
        factor = relax / (1.0 + coupling)
        running = (eprev[x] + fprev[x]) * has_prev
        for n in range(STEPS):
            fix, c = (fix0, fix1)[n // 2], n // 2
            value = first[n, x] + fix[x]
            below = (first[n, x - 1] + fix[x - 1]) if x > 0 else (exl[n] + fxl[c])
            above = (first[n, x + 1] + fix[x + 1]) if x < BX - 1 else (exh[n] + fxh[c])
            at = pl.ds(n * BX + x, 1)
            low = yl[at, :] + fyl[c, pl.ds(x, 1), :]
            high = yh[at, :] + fyh[c, pl.ds(x, 1), :]
            sides = y_sides(value, low, high, row)
            running = keep * value + factor * (h[n, x] + beside(value, below, above, *sides, g) + running)
            out[n, x] = running
            put_edges((x_low, x_high, y_low, y_high), n, x, running)
        last[x] = running


def copy_kernel(source, target):
    target[...] = source[...]


def residual_kernel(sol, h, g_ref, hxl, hxh, hyl, hyh, prev, out):
    has_prev = inside(lax.axis_index("tm") > 0)
    row = row_index()
    for x in range(BX):
        g, coupling = row_coefficients(g_ref, x)
        diagonal = 1.0 + coupling
        earlier = prev[x] * has_prev
        for n in range(STEPS):
            value = sol[n, x]
            below = sol[n, x - 1] if x > 0 else hxl[n]
            above = sol[n, x + 1] if x < BX - 1 else hxh[n]
            sides = y_sides(value, hyl[n, pl.ds(x, 1), :], hyh[n, pl.ds(x, 1), :], row)
            out[n, x] = h[n, x] + earlier - diagonal * value + beside(value, below, above, *sides, g)
            earlier = value


def gather_steps(own):
    def along(value, s):
        return across_tm(value, lambda i: (i & 9) | ((i + 2 * s) & 6))

    far = across_tm(own, lambda i: i ^ 8)
    near = [own] + [along(own, s) for s in (1, 2, 3)]
    return near + [far] + [along(far, s) for s in (1, 2, 3)]


def per_device(h, k, u):
    fine, two = (STEPS, *FIELD), (2, *FIELD)
    ypack = (YROWS, BZ)
    (last,) = call(last_step_kernel, [FIELD], u)
    edges = call(first_edges_kernel, [(STEPS + KW, *EDGE)] * 2 + [(STEPS + 1, *EDGE)] * 2, u, k)
    (h,) = call(copy_kernel, [fine], h)
    halo, prev = exchange(edges, last)
    g, first, *edges, last, kx = call(
        first_kernel,
        [(7, *FIELD), fine, (STEPS, *EDGE), (STEPS, *EDGE), ypack, ypack, FIELD, (KX, BY, BZ)],
        u, h, k, *halo, prev,
    )
    first_halo, first_prev = exchange(edges, last)
    factor, factor4, g_coarse = call(
        coarse_terms_kernel,
        [(EX, EY, BZ), (BX + 2, EY, BZ), (6, BX + 4, EY, BZ)],
        kx, *first_halo[2:],
        scratch=[(KX, EY, BZ)],
    )
    rhs1, e0, e1, *edges = call(
        defect_fine_kernel, [two, FIELD, FIELD] + edge_shapes(2), first, h, g, *first_halo, first_prev
    )
    err1_halo, err1_prev = exchange(edges, e1)
    rhs2, err2, *edges = call(
        defect_mid_kernel, [FIELD, FIELD] + edge_shapes(1), e0, e1, rhs1, g, *err1_halo, err1_prev
    )
    err2_halo, chip_before = exchange(edges, err2, 2)
    (ends,) = call(defect_last_kernel, [(3, *FIELD)], err2, rhs2, g, *err2_halo, chip_before)
    sibling = across_tm(ends, lambda i: i ^ 1)
    half, x_edge, y_edge, corner_a, corner_b = call(
        coarse_edges_kernel,
        [(HALF, BZ), (WIDE * BY + SIDE, BZ), (WIDE * BX + SIDE, BZ), (8, BZ), (8, BZ)],
        ends, sibling,
        scratch=[FIELD],
    )
    share, extra = call(
        share_kernel,
        [(SHARE, BZ), (EXTRA, BZ)],
        half, crossed(x_edge, 1, 0), crossed(y_edge, 0, 1), crossed(corner_a, 1, 1), crossed(corner_b, 1, -1),
    )
    (mine,) = call(order_kernel, [(ALL + EXTRA, BZ)], *gather_steps(share), extra)
    other = across_tm(mine, lambda i: i ^ 1)
    fixed1a, fixed1b, *edges = call(
        coarse_kernel,
        [FIELD, FIELD] + edge_shapes(2),
        mine, other, factor, factor4, g_coarse, ends, sibling,
        e0, e1, *err1_halo, err1_prev, rhs1, g,
        scratch=[
            (COARSE, EX, EY, BZ), (COARSE, EX, EY, BZ), (COARSE + 1, BX + 4, EY, BZ),
            (BX + 4, EY, BZ), (BX + 2, EY, BZ), (BX + 4, EY, BZ), (BX + 2, EY, BZ), (BX + 2, EY, BZ),
        ],
    )
    fixed1_halo, fixed1_prev = exchange(edges, fixed1b)
    last_iterate, *edges, last = call(
        solution_kernel,
        [fine] + edge_shapes(STEPS) + [FIELD],
        fixed1a, fixed1b, *fixed1_halo, fixed1_prev, first, *first_halo, first_prev, h, g,
    )
    out_halo, out_prev = exchange(edges, last)
    (out,) = call(copy_kernel, [fine], last_iterate)
    (residual,) = call(residual_kernel, [fine], last_iterate, h, g, *out_halo, out_prev)
    return out, residual


def solution(mesh):
    placed = (P("tm", "sx", "sy", None), P("sx", "sy", None), P("tm", "sx", "sy", None))
    return jax.shard_map(
        per_device,
        mesh=mesh,
        in_specs=placed,
        out_specs=(P("tm", "sx", "sy", None), P("tm", "sx", "sy", None)),
        check_vma=False,
    )
```
